256 devices in a mesh: dp: 4 (over x), exp: 8 (over z), seq: 8 (over y, core).
Axes of the slice: x: 4, y: 4, z: 8, core: 2. Of those that a mesh axis runs over, the one named last changes fastest.
Arguments:
- query_rows: bfloat16 [32768, 5120], P(('dp', 'exp', 'seq')), may hold values from -22 to 22
- key_rows: bfloat16 [32768, 5120], P(('dp', 'exp', 'seq')), may hold values from -6 to 6
- value_rows: bfloat16 [32768, 5120], P(('dp', 'exp', 'seq')), may hold values from -6 to 6
- stream: bfloat16 [32768, 5120], P(('dp', 'exp', 'seq')), may hold values from -32 to 32
- shared_basis: bfloat16 [5120, 1024], P('seq'), may hold values from -0.078125 to 0.078125
- expert_gate_up: bfloat16 [128, 1024, 256], P(('exp', 'seq')), may hold values from -0.1875 to 0.1875
- expert_down: bfloat16 [128, 128, 5120], P(('exp', 'seq')), may hold values from -0.5 to 0.5
- attn_gate: bfloat16 [32, 5120], P(('dp', 'exp')), may hold values from 0.5 to 1.5
- ffn_scale: bfloat16 [32, 5120], P(('dp', 'exp')), may hold values from 0.5 to 1.5
- ffn_gate: bfloat16 [32, 5120], P(('dp', 'exp')), may hold values from 0.5 to 1.5
- expert_ids: int32 [32768, 2], P(('dp', 'exp', 'seq')), may hold values from 0 to 127, all different within a row; in each aligned block of 128 rows (0 to 127, 128 to 255, ...) at most 4 rows name the same one
- route_weights: float32 [32768, 2], P(('dp', 'exp', 'seq')), may hold values from 0.2 to 1
Outputs:
- output: bfloat16 [32768, 5120], P(('dp', 'exp', 'seq'))
The draws below stay inside these ranges and needn't reach their ends.
Inputs may be any that keep to these rules, and one draw needn't show every extreme that they name: `expert_ids`: the two experts of a token differ. Among the 128 tokens of one device no expert is named more than 4 times, and in some blocks one is named exactly 4 times; a token's slot at an expert is the number of earlier (token, k) entries of its device, in row-major order, that name the same expert.
All inputs are finite; a program needn't handle non-finite values.
Results may differ from the reference program's by a relative error of at most 0.0051.
Values may be sent and summed in bfloat16 or wider, within the bound.
A program may use at most 128 MiB of HBM per device.

```python
import math
import jax
import jax.numpy as jnp
import numpy as np
from jax import lax

HEADS = 40
HEAD_DIM = 128
D = 5120
RANK = 1024
EXPERT_HIDDEN = 128
TOK_DEV = 128
EXPERTS = 128
CAP = 4
CLIP_LEN = 1024
CLIPS = 32
TOKENS = 32768
N_DP = 4
N_EXP = 8
N_SEQ = 8


def draw_query_rows(key, part):
    key = jax.random.fold_in(key, 1)
    values_drawn = jnp.clip(1.5 * jax.random.normal(key, (TOKENS, D), jnp.float32), -6.0, 6.0)
    return values_drawn.astype(jnp.bfloat16)


def draw_key_rows(key, part):
    key = jax.random.fold_in(key, 2)
    values_drawn = jnp.clip(1.5 * jax.random.normal(key, (TOKENS, D), jnp.float32), -6.0, 6.0)
    return values_drawn.astype(jnp.bfloat16)


def draw_stream(key, part):
    key = jax.random.fold_in(key, 3)
    row_scale = jnp.exp(jax.random.uniform(jax.random.fold_in(key, 21), (TOKENS, 1), jnp.float32, jnp.log(0.3), jnp.log(3.0)))
    col_rise = 3.0 ** (jnp.arange(D, dtype=jnp.float32) / D)
    col_scale = 0.5 * col_rise[None, :] * jnp.exp(jax.random.uniform(jax.random.fold_in(key, 22), (1, D), jnp.float32, jnp.log(0.6), jnp.log(1.7)))
    noise_term = jnp.clip(jax.random.normal(key, (TOKENS, D), jnp.float32), -4.0, 4.0)
    values_drawn = noise_term * row_scale * col_scale
    return jnp.clip(values_drawn, -32.0, 32.0).astype(jnp.bfloat16)


def shard_levels(own_key, shape, pieces, low, high):
    level = 1.0
    for dim, shards_of in pieces:
        steps = jax.random.uniform(jax.random.fold_in(jax.random.fold_in(own_key, 6), dim), (shards_of,), jnp.float32, low / len(pieces), high / len(pieces))
        level = level * jnp.repeat(jnp.exp(steps), shape[dim] // shards_of).reshape((-1,) + (1,) * (len(shape) - 1 - dim))
    return level


def routed_block(key, own, number, rows, number_of, top, bound, lean):
    sequence = jax.random.permutation(key, number_of)
    crowded, usual = portions_of(number_of, rows * top, bound, lean, True), portions_of(number_of, rows * top, bound, lean, False)
    places = jnp.arange(number_of)

    def named(tallies, rotation):
        used = int((tallies > 0).sum())
        fixed = max(1, used // 4)
        shifted = fixed + (places - fixed + rotation * (used - fixed)) % max(1, number_of - fixed)
        return jnp.zeros((number_of,), jnp.int32).at[sequence[jnp.where(places < fixed, places, shifted)]].set(jnp.asarray(tallies, jnp.int32))

    tallies = jnp.where(number % 4 == 0, named(crowded, number // 4), named(usual, number - number // 4 - 1))
    mixed = jax.random.permutation(jax.random.fold_in(own, 3), number_of)
    giver, sink = mixed[0:number_of // 2 * 2:2], mixed[1:number_of // 2 * 2:2]
    margin = jnp.minimum(tallies[giver] - 1, bound - tallies[sink]) // 2
    margin = jnp.where((giver == sequence[0]) | (sink == sequence[0]) | (tallies[sink] == 0), 0, jnp.maximum(margin, 0))
    shifted = jax.random.randint(jax.random.fold_in(own, 4), (number_of // 2,), 0, 1 << 20) % (margin + 1)
    tallies = tallies.at[giver].add(-shifted).at[sink].add(shifted)
    labels = jnp.searchsorted(jnp.cumsum(tallies), jnp.arange(rows * top), side="right").astype(jnp.int32)
    table = labels.reshape(top, rows).T
    table = table[jax.random.permutation(jax.random.fold_in(own, 1), rows)]
    rotation = jax.random.randint(jax.random.fold_in(own, 2), (rows, 1), 0, top)
    return jnp.take_along_axis(table, (jnp.arange(top)[None, :] + rotation) % top, axis=1)


def portions_of(amount, total, most, skew, full):
    loads = [(1 << 20) // math.isqrt(rank ** skew) + 1 for rank in range(1, amount + 1)]
    largest = most if full else min(most, max(-(-total // amount), total * loads[0] // sum(loads)))
    least = 1 if total - largest >= amount - 1 else 0
    holding, rest = [largest] + [least] * (amount - 1), total - largest - least * (amount - 1)
    while rest > 0:
        candidates = [i for i in range(1, amount) if holding[i] < largest] or [i for i in range(1, amount) if holding[i] < most]
        whole, remaining = sum([loads[i] for i in candidates]), rest
        for i in candidates:
            extra = min(most - holding[i], max(1, remaining * loads[i] // whole), rest)
            holding[i] = holding[i] + extra
            rest = rest - extra
    return np.array(holding)


def centred(stream_key, shape, deviation, bound, pieces=(), held_as=jnp.bfloat16):
    values = deviation * jax.random.normal(stream_key, shape, jnp.float32)
    if pieces:
        values = values * shard_levels(stream_key, shape, pieces, -0.22, 0.18)
    return jnp.clip(values, -bound, bound).astype(held_as)


def setup_inputs(seed: int = 0) -> dict:
    keys = jax.random.split(jax.random.key(seed), 13)
    query_rows = draw_query_rows(jax.random.fold_in(keys[12], 71), 0)
    key_rows = draw_key_rows(jax.random.fold_in(keys[12], 71), 0)
    value_rows = centred(keys[2], (TOKENS, D), 1.0, 6.0, ((0, 256),))
    stream = draw_stream(jax.random.fold_in(keys[12], 71), 0)
    shared_basis = centred(keys[4], (D, RANK), D ** -0.5, 0.078125, ((0, 8),))
    expert_gate_up = centred(keys[5], (EXPERTS, RANK, 2 * EXPERT_HIDDEN), RANK ** -0.5, 0.1875, ((0, 64),))
    expert_down = centred(keys[6], (EXPERTS, EXPERT_HIDDEN, D), EXPERT_HIDDEN ** -0.5, 0.5, ((0, 64),))
    attn_gate = jnp.clip(0.5 + 1.0 * jax.random.uniform(keys[7], (CLIPS, D), jnp.float32) ** shard_levels(keys[7], (CLIPS, D), ((0, 32),), -0.2, 0.2), 0.5, 1.5).astype(jnp.bfloat16)
    ffn_scale = jnp.clip(0.5 + 1.0 * jax.random.uniform(keys[8], (CLIPS, D), jnp.float32) ** shard_levels(keys[8], (CLIPS, D), ((0, 32),), -0.2, 0.2), 0.5, 1.5).astype(jnp.bfloat16)
    ffn_gate = jnp.clip(0.5 + 1.0 * jax.random.uniform(keys[9], (CLIPS, D), jnp.float32) ** shard_levels(keys[9], (CLIPS, D), ((0, 32),), -0.2, 0.2), 0.5, 1.5).astype(jnp.bfloat16)
    expert_ids_keys = jax.random.split(jax.random.fold_in(keys[10], 1), TOKENS // TOK_DEV)
    expert_ids_turns = jax.random.permutation(jax.random.fold_in(keys[10], 3), TOKENS // TOK_DEV)
    expert_ids = jax.vmap(lambda own, number: routed_block(jax.random.fold_in(keys[10], 2), own, number, TOK_DEV, EXPERTS, 2, CAP, 2))(expert_ids_keys, expert_ids_turns).reshape((TOKENS, 2))
    route_weights = jnp.clip(0.2 + 0.8 * jax.random.uniform(keys[11], (TOKENS, 2), jnp.float32) ** shard_levels(keys[11], (TOKENS, 2), ((0, 256),), -0.2, 0.2), 0.2, 1.0)
    return {"query_rows": query_rows, "key_rows": key_rows, "value_rows": value_rows, "stream": stream, "shared_basis": shared_basis, "expert_gate_up": expert_gate_up, "expert_down": expert_down, "attn_gate": attn_gate, "ffn_scale": ffn_scale, "ffn_gate": ffn_gate, "expert_ids": expert_ids, "route_weights": route_weights}


epsilon = 1e-06

def attend_clip(clip_arrays):
    query_clip, key_clip, value_clip = clip_arrays
    query_four = query_clip.reshape(CLIP_LEN, HEADS, HEAD_DIM).astype(jnp.float32)
    key_four = key_clip.reshape(CLIP_LEN, HEADS, HEAD_DIM).astype(jnp.float32)
    value_four = value_clip.reshape(CLIP_LEN, HEADS, HEAD_DIM).astype(jnp.float32)
    scores = jnp.einsum('qhd,khd->hqk', query_four, key_four) * (1.0 / math.sqrt(HEAD_DIM))
    row_max = lax.optimization_barrier(jnp.max(scores, axis=-1, keepdims=True))
    raised = jnp.exp(scores - row_max)
    attn_probs = (raised / lax.optimization_barrier(jnp.sum(raised, axis=-1, keepdims=True))).astype(jnp.bfloat16)
    mixed_values = jnp.einsum('hqk,khd->qhd', attn_probs.astype(jnp.float32), value_four)
    return mixed_values.reshape(CLIP_LEN, D).astype(jnp.bfloat16)

def reference(query_rows, key_rows, value_rows, stream, shared_basis, expert_gate_up, expert_down, attn_gate, ffn_scale, ffn_gate, expert_ids, route_weights):
    device_count = N_DP * N_EXP * N_SEQ
    clip_shape = (CLIPS, CLIP_LEN, D)
    attended = lax.map(attend_clip, (query_rows.reshape(clip_shape), key_rows.reshape(clip_shape), value_rows.reshape(clip_shape)))
    residual = stream.reshape(clip_shape).astype(jnp.float32) + attn_gate.astype(jnp.float32)[:, None, :] * attended.astype(jnp.float32)
    modulated = (residual * ffn_scale.astype(jnp.float32)[:, None, :]).astype(jnp.bfloat16).reshape(TOKENS, D)
    projected = jnp.dot(modulated, shared_basis, preferred_element_type=jnp.float32)
    mean_square = lax.optimization_barrier(jnp.mean(residual * residual, axis=-1)).reshape(TOKENS)
    low_rank = (projected / jnp.sqrt(mean_square + epsilon)[:, None]).astype(jnp.bfloat16)
    block_ids = expert_ids.reshape(device_count, 2 * TOK_DEV)
    one_hot = (block_ids[:, :, None] == jnp.arange(EXPERTS, dtype=jnp.int32)[None, None, :]).astype(jnp.int32)
    earlier = jnp.cumsum(one_hot, axis=1) - one_hot
    slot_rank = lax.optimization_barrier(jnp.sum(earlier * one_hot, axis=2))
    device_rows = jnp.arange(device_count, dtype=jnp.int32)[:, None]
    slot_ids = (block_ids * (device_count * CAP) + device_rows * CAP + slot_rank).reshape(-1).astype(jnp.int32)
    table = jnp.full((EXPERTS * device_count * CAP,), 2 * TOKENS, jnp.int32)
    table = table.at[slot_ids].set(jnp.arange(2 * TOKENS, dtype=jnp.int32)).reshape(EXPERTS, device_count * CAP)
    flat_weights = route_weights.reshape(2 * TOKENS)

    def one_expert(accum, inputs):
        entries, gate_up_weights, down_weights = inputs
        is_live = entries < 2 * TOKENS
        safe_entry = jnp.where(is_live, entries, 0).astype(jnp.int32)
        token_rows = low_rank[safe_entry // 2]
        gate_up = jnp.dot(token_rows, gate_up_weights, preferred_element_type=jnp.float32)
        hidden = (jax.nn.silu(gate_up[:, :EXPERT_HIDDEN]) * gate_up[:, EXPERT_HIDDEN:]).astype(jnp.bfloat16)
        result = jnp.dot(hidden, down_weights, preferred_element_type=jnp.float32).astype(jnp.bfloat16)
        weight = jnp.where(is_live, flat_weights[safe_entry], jnp.zeros_like(flat_weights[safe_entry]))
        accum = accum.at[safe_entry // 2].add(weight[:, None] * result.astype(jnp.float32))
        return (accum, None)
    mixed, unused = lax.scan(one_expert, jnp.zeros((TOKENS, D), jnp.float32), (table, expert_gate_up, expert_down))
    output = residual + ffn_gate.astype(jnp.float32)[:, None, :] * mixed.reshape(clip_shape)
    return output.reshape(TOKENS, D).astype(jnp.bfloat16)
```

```python
import functools
import math

import jax
import jax.numpy as jnp
from jax import lax
from jax.experimental import pallas as pl
from jax.experimental.pallas import tpu as pltpu
from jax.sharding import PartitionSpec as P

HEAD_DIM = 128
MESH = pl.DeviceIdType.MESH


epsilon = 1e-06


def attention_kernel(
    query_ref,
    key_ref,
    value_ref,
    stream_ref,
    gate_ref,
    scale_ref,
    attended_ref,
    modulated_ref,
    square_ref,
    heads_in,
    heads_out,
    attended_all,
    in_send,
    in_recv,
    out_send,
    out_recv,
):
    n = lax.axis_size("seq")
    me = lax.axis_index("seq")
    tok_rows, model_width = attended_all.shape
    heads_here, _, length, _ = heads_in.shape
    head_cols = heads_here * HEAD_DIM
    query_block = 2 * tok_rows
    exponent_scale = 1.0 / (math.sqrt(HEAD_DIM) * math.log(2.0))
    sources = (query_ref, key_ref, value_ref)

    barrier = pltpu.get_barrier_semaphore()

    def greet(step, carry):
        peer = lax.rem(me + step, n)
        pl.semaphore_signal(barrier, inc=1, device_id={"seq": peer}, device_id_type=MESH)
        return carry

    lax.fori_loop(1, n, greet, 0)

    my_rows = pl.ds(pl.multiple_of(me * tok_rows, tok_rows), tok_rows)

    def own_head(head, carry):
        columns = pl.ds(pl.multiple_of(me * head_cols + head * HEAD_DIM, HEAD_DIM), HEAD_DIM)
        for which, source in enumerate(sources):
            pltpu.make_async_copy(
                source.at[:, columns], heads_in.at[head, which, my_rows, :], in_recv.at[head]
            ).start()
        return carry

    lax.fori_loop(0, heads_here, own_head, 0)
    pl.semaphore_wait(barrier, n - 1)

    def send_head(head, carry):
        def send_to(step, inner):
            peer = lax.rem(me + step, n)
            columns = pl.ds(
                pl.multiple_of(peer * head_cols + head * HEAD_DIM, HEAD_DIM), HEAD_DIM
            )
            for which, source in enumerate(sources):
                pltpu.make_async_remote_copy(
                    src_ref=source.at[:, columns],
                    dst_ref=heads_in.at[head, which, my_rows, :],
                    send_sem=in_send.at[head],
                    recv_sem=in_recv.at[head],
                    device_id={"seq": peer},
                    device_id_type=MESH,
                ).start()
            return inner

        return lax.fori_loop(1, n, send_to, carry)

    lax.fori_loop(0, heads_here, send_head, 0)

    lane = lax.broadcasted_iota(jnp.int32, (length, HEAD_DIM), 1)
    ones_column = jnp.where(lane == 0, 1.0, 0.0).astype(jnp.bfloat16)

    def attend_head(head, carry):
        arrived = heads_in.at[head]
        pltpu.make_async_copy(arrived, arrived, in_recv.at[head]).wait()
        my_columns = pl.ds(pl.multiple_of(me * head_cols + head * HEAD_DIM, HEAD_DIM), HEAD_DIM)

        def attend_block(block, inner):
            rows = pl.ds(pl.multiple_of(block * query_block, query_block), query_block)
            scores = lax.dot_general(
                heads_in[head, 0, rows, :],
                heads_in[head, 1],
                (((1,), (1,)), ((), ())),
                preferred_element_type=jnp.float32,
            )
            row_max = jnp.max(scores, axis=-1, keepdims=True)
            raised = jnp.exp2((scores - row_max) * exponent_scale).astype(jnp.bfloat16)
            value_ones = jnp.concatenate([heads_in[head, 2], ones_column], axis=1)
            mixed = jnp.dot(raised, value_ones, preferred_element_type=jnp.float32)
            mixed = mixed[:, :HEAD_DIM] / mixed[:, HEAD_DIM : HEAD_DIM + 1]
            heads_out[head, rows, :] = mixed.astype(jnp.bfloat16)

            for half in range(2):
                peer = 2 * block + half
                sent_rows = pl.ds(pl.multiple_of(peer * tok_rows, tok_rows), tok_rows)

                @pl.when(peer == me)
                def _keep():
                    pltpu.make_async_copy(
                        heads_out.at[head, sent_rows, :], attended_all.at[:, my_columns], out_recv
                    ).start()

                @pl.when(peer != me)
                def _send():
                    pltpu.make_async_remote_copy(
                        src_ref=heads_out.at[head, sent_rows, :],
                        dst_ref=attended_all.at[:, my_columns],
                        send_sem=out_send,
                        recv_sem=out_recv,
                        device_id={"seq": peer},
                        device_id_type=MESH,
                    ).start()

            return inner

        return lax.fori_loop(0, length // query_block, attend_block, carry)

    lax.fori_loop(0, heads_here, attend_head, 0)

    pltpu.make_async_copy(attended_all, attended_all, out_recv).wait()
    attended_ref[...] = attended_all[...]
    square = jnp.zeros((tok_rows, 1), jnp.float32)
    for start in range(0, model_width, 1024):
        part = slice(start, start + 1024)
        residual = stream_ref[:, part].astype(jnp.float32) + gate_ref[:, part].astype(
            jnp.float32
        ) * attended_all[:, part].astype(jnp.float32)
        modulated_ref[:, part] = (residual * scale_ref[:, part].astype(jnp.float32)).astype(
            jnp.bfloat16
        )
        square = square + jnp.sum(residual * residual, axis=1, keepdims=True)
    square_ref[...] = jnp.broadcast_to(square, square_ref.shape)

    def drain_in(head, carry):
        sent = heads_in.at[head, :, pl.ds(0, (n - 1) * tok_rows), :]
        pltpu.make_async_copy(sent, sent, in_send.at[head]).wait()
        return carry

    lax.fori_loop(0, heads_here, drain_in, 0)
    sent_out = heads_out.at[:, pl.ds(0, (n - 1) * tok_rows), :]
    pltpu.make_async_copy(sent_out, sent_out, out_send).wait()


def attention(query_rows, key_rows, value_rows, stream, attn_gate, ffn_scale):
    tok_rows, model_width = stream.shape
    n = lax.axis_size("seq")
    length = n * tok_rows
    heads_here = model_width // (n * HEAD_DIM)
    vmem = pl.BlockSpec(memory_space=pltpu.VMEM)
    anywhere = pl.BlockSpec(memory_space=pl.ANY)
    return pl.pallas_call(
        attention_kernel,
        out_shape=(
            jax.ShapeDtypeStruct((tok_rows, model_width), jnp.bfloat16),
            jax.ShapeDtypeStruct((tok_rows, model_width), jnp.bfloat16),
            jax.ShapeDtypeStruct((tok_rows, 128), jnp.float32),
        ),
        in_specs=[anywhere] * 3 + [vmem] * 3,
        out_specs=(vmem, vmem, vmem),
        scratch_shapes=[
            pltpu.VMEM((heads_here, 3, length, HEAD_DIM), jnp.bfloat16),
            pltpu.VMEM((heads_here, length, HEAD_DIM), jnp.bfloat16),
            pltpu.VMEM((tok_rows, model_width), jnp.bfloat16),
            pltpu.SemaphoreType.DMA((heads_here,)),
            pltpu.SemaphoreType.DMA((heads_here,)),
            pltpu.SemaphoreType.DMA,
            pltpu.SemaphoreType.DMA,
        ],
        compiler_params=pltpu.CompilerParams(
            collective_id=0, has_side_effects=True, vmem_limit_bytes=48 * 1024 * 1024
        ),
        cost_estimate=pl.CostEstimate(
            flops=4 * length * length * heads_here * HEAD_DIM,
            bytes_accessed=14 * tok_rows * model_width,
            transcendentals=heads_here * length * length,
        ),
        name="attention",
    )(query_rows, key_rows, value_rows, stream, attn_gate, ffn_scale)


def hidden_kernel(rows_ref, gate_up_ref, info_ref, hidden_ref):
    owner = lax.axis_index("exp") * lax.axis_size("seq") + lax.axis_index("seq")
    sources = info_ref.shape[0]
    tok_rows = info_ref.shape[2]
    rows_total = rows_ref.shape[0]
    slots = rows_total // sources
    half_cols = gate_up_ref.shape[2] // 2
    row = lax.broadcasted_iota(jnp.int32, (sources, slots, tok_rows), 1)
    slot_here = (row + owner * slots).astype(jnp.float32)
    weight = jnp.zeros((sources, slots, tok_rows), jnp.float32)
    for k in range(2):
        named = info_ref[:, k : k + 1, :]
        routed = info_ref[:, 2 + k : 3 + k, :]
        weight = weight + jnp.where(slot_here == named, routed, 0.0)
    weight = jnp.sum(weight, axis=2, keepdims=True).reshape(rows_total, 1)
    rows = rows_ref[...]
    first = jnp.dot(rows, gate_up_ref[0], preferred_element_type=jnp.float32)
    second = jnp.dot(rows, gate_up_ref[1], preferred_element_type=jnp.float32)
    place = lax.broadcasted_iota(jnp.int32, first.shape, 0) % slots
    gate_up = jnp.where(place < slots // 2, first, second)
    gate, up = gate_up[:, :half_cols], gate_up[:, half_cols:]
    hidden = gate / (1.0 + jnp.exp(-gate)) * up
    hidden_ref[...] = (hidden * weight).astype(jnp.bfloat16)


def run_hidden(slot_rows, gate_up_weights, info):
    rows_total = slot_rows.shape[0]
    hidden_cols = gate_up_weights.shape[2] // 2
    vmem = pl.BlockSpec(memory_space=pltpu.VMEM)
    return pl.pallas_call(
        hidden_kernel,
        out_shape=jax.ShapeDtypeStruct((rows_total, hidden_cols), jnp.bfloat16),
        in_specs=[vmem] * 3,
        out_specs=vmem,
        compiler_params=pltpu.CompilerParams(vmem_limit_bytes=32 * 1024 * 1024),
        name="hidden",
    )(slot_rows, gate_up_weights, info)


def down_kernel(groups, hidden_ref, down_ref, info_ref, mixed_ref, slot_out):
    sources, slots_total, cols = slot_out.shape
    exp_count = lax.axis_size("exp")
    dp_count = lax.axis_size("dp")
    owners = exp_count * groups
    slots = slots_total // owners
    run = groups * slots

    def one_owner(owner, carry):
        z, s = owner // groups, owner % groups
        rows = jnp.concatenate(
            [
                hidden_ref[
                    pl.ds(pl.multiple_of(((x * groups + s) * exp_count + z) * run, run), run), :
                ]
                for x in range(dp_count)
            ],
            axis=0,
        )
        first, second = [
            lax.dot_general(
                rows,
                down_ref[2 * owner + i],
                (((1,), (1,)), ((), ())),
                preferred_element_type=jnp.float32,
            )
            for i in range(2)
        ]
        place = lax.broadcasted_iota(jnp.int32, first.shape, 0) % slots
        chosen = jnp.where(place < slots // 2, first, second)
        at = pl.ds(pl.multiple_of(owner * slots, slots), slots)
        slot_out[:, at, :] = chosen.reshape(sources, slots, cols)
        return carry

    lax.fori_loop(0, owners, one_owner, 0)
    tok_rows = info_ref.shape[2]

    def one_source(source, carry):
        slot_iota = lax.broadcasted_iota(jnp.int32, (slots_total, tok_rows), 0).astype(jnp.float32)
        named = info_ref[source]
        pick = (slot_iota == named[0:1, :]) | (slot_iota == named[1:2, :])
        pick = jnp.where(pick, 1.0, 0.0).astype(jnp.bfloat16)
        mixed = lax.dot_general(
            slot_out[source].astype(jnp.bfloat16),
            pick,
            (((0,), (0,)), ((), ())),
            preferred_element_type=jnp.float32,
        )
        mixed_ref[source] = mixed.astype(jnp.bfloat16)
        return carry

    lax.fori_loop(0, sources, one_source, 0)


def run_down(hidden_all, down_columns, info):
    sources, _, tok_rows = info.shape
    groups = lax.axis_size("seq")
    experts, cols, _ = down_columns.shape
    vmem = pl.BlockSpec(memory_space=pltpu.VMEM)
    return pl.pallas_call(
        functools.partial(down_kernel, groups),
        out_shape=jax.ShapeDtypeStruct((sources, cols, tok_rows), jnp.bfloat16),
        in_specs=[vmem] * 3,
        out_specs=vmem,
        scratch_shapes=[pltpu.VMEM((sources, 4 * experts, cols), jnp.float32)],
        compiler_params=pltpu.CompilerParams(vmem_limit_bytes=56 * 1024 * 1024),
        name="down",
    )(hidden_all, down_columns, info)


def on_device(
    query_rows,
    key_rows,
    value_rows,
    stream,
    shared_basis,
    expert_gate_up,
    expert_down,
    attn_gate,
    ffn_scale,
    ffn_gate,
    expert_ids,
    route_weights,
):
    groups = lax.axis_size("seq")
    exp_count = lax.axis_size("exp")
    dp_count = lax.axis_size("dp")
    tok_rows, model_width = stream.shape
    owners = exp_count * groups
    experts_here, hidden_cols, _ = expert_down.shape
    expert_total = owners * experts_here
    capacity = 4 * tok_rows // expert_total
    rank_cols = shared_basis.shape[1]
    my_x = lax.axis_index("dp")

    flat_ids = expert_ids.reshape(2 * tok_rows)
    one_hot = (flat_ids[:, None] == jnp.arange(expert_total, dtype=jnp.int32)[None, :]).astype(
        jnp.int32
    )
    earlier = jnp.cumsum(one_hot, axis=0) - one_hot
    slot_rank = jnp.sum(earlier * one_hot, axis=1)
    slot_ids = flat_ids * capacity + slot_rank
    slot_pairs = slot_ids.reshape(tok_rows, 2)
    info = jnp.concatenate([slot_pairs.T.astype(jnp.float32), route_weights.T], axis=0)
    info_owner = lax.all_gather(info, ("exp", "seq"), axis=0, tiled=False)
    info_column = lax.all_gather(info, ("dp", "seq"), axis=0, tiled=False)

    block_cols = model_width // dp_count
    cols = block_cols // groups
    down_block = lax.dynamic_slice_in_dim(expert_down, my_x * block_cols, block_cols, axis=2)
    down_block = down_block.reshape(experts_here, hidden_cols, groups, cols).transpose(2, 0, 3, 1)
    down_block = lax.all_to_all(down_block, "seq", split_axis=0, concat_axis=0, tiled=True)
    down_columns = lax.all_gather(down_block, "exp", axis=0, tiled=True)
    down_columns = down_columns.reshape(expert_total, cols, hidden_cols)

    basis_cols = rank_cols // dp_count
    basis_block = lax.dynamic_slice_in_dim(shared_basis, my_x * basis_cols, basis_cols, axis=1)
    basis = lax.all_gather(basis_block, ("dp", "seq"), axis=0, tiled=True)
    basis = basis.reshape(dp_count, model_width, basis_cols)

    attended, modulated, square_sum = attention(
        query_rows, key_rows, value_rows, stream, attn_gate, ffn_scale
    )
    projected = jnp.einsum(
        "tk,xkn->txn", modulated, basis, preferred_element_type=jnp.float32
    ).reshape(tok_rows, rank_cols)
    low_rank = (projected / jnp.sqrt(square_sum[:, :1] / model_width + epsilon)).astype(
        jnp.bfloat16
    )
    slot_iota = jnp.arange(expert_total * capacity, dtype=jnp.int32)
    pick_matrix = jnp.sum(
        (slot_iota[:, None, None] == slot_pairs[None, :, :]).astype(jnp.int32), axis=2
    ).astype(jnp.bfloat16)
    outgoing = jnp.dot(pick_matrix, low_rank, preferred_element_type=jnp.float32).astype(
        jnp.bfloat16
    )
    slots = experts_here * capacity
    arrived = lax.all_to_all(
        outgoing.reshape(owners, slots, rank_cols),
        ("exp", "seq"),
        split_axis=0,
        concat_axis=0,
        tiled=True,
    )
    hidden = run_hidden(arrived.reshape(owners * slots, rank_cols), expert_gate_up, info_owner)
    hidden = lax.all_to_all(
        hidden.reshape(exp_count, groups * slots, hidden_cols),
        "exp",
        split_axis=0,
        concat_axis=0,
        tiled=True,
    )
    hidden_all = lax.all_gather(
        hidden.reshape(owners * slots, hidden_cols), ("dp", "seq"), axis=0, tiled=True
    )
    mixed = run_down(hidden_all, down_columns, info_column)
    mixed = lax.all_to_all(mixed, ("dp", "seq"), split_axis=0, concat_axis=0, tiled=True)
    mixed = mixed.reshape(model_width, tok_rows).T.astype(jnp.float32)
    residual = stream.astype(jnp.float32) + attn_gate.astype(jnp.float32) * attended.astype(
        jnp.float32
    )
    output = residual + ffn_gate.astype(jnp.float32) * mixed
    return output.astype(jnp.bfloat16)


def solution(mesh):
    in_specs = (
        P(("dp", "exp", "seq"), None),
        P(("dp", "exp", "seq"), None),
        P(("dp", "exp", "seq"), None),
        P(("dp", "exp", "seq"), None),
        P("seq", None),
        P(("exp", "seq"), None, None),
        P(("exp", "seq"), None, None),
        P(("dp", "exp"), None),
        P(("dp", "exp"), None),
        P(("dp", "exp"), None),
        P(("dp", "exp", "seq"), None),
        P(("dp", "exp", "seq"), None),
    )
    out_specs = P(("dp", "exp", "seq"), None)
    return jax.shard_map(
        on_device, mesh=mesh, in_specs=in_specs, out_specs=out_specs, check_vma=False
    )
```

```python
import functools
import math

import jax
import jax.numpy as jnp
from jax import lax
from jax.experimental import pallas as pl
from jax.experimental.pallas import tpu as pltpu
from jax.sharding import PartitionSpec as P

HEAD_DIM = 128
LANES = 128
MESH = pl.DeviceIdType.MESH
epsilon = 1e-06
CAP = 4


def block_kernel(
    query_ref,
    key_ref,
    value_ref,
    stream_ref,
    down_ref,
    gate_up_ref,
    basis_ref,
    attn_gate_ref,
    ffn_scale_ref,
    ffn_gate_ref,
    info_ref,
    output_ref,
    kv_in,
    qs_in,
    stream_own,
    att_out,
    attended,
    modulated,
    partial,
    own_part,
    core_send,
    core_recv,
    part_send,
    part_recv,
    out_rows,
    near_rows,
    slot_rows,
    gate_up,
    hidden,
    hidden_all,
    weights,
    slot_out,
    mix_out,
    mix_in,
    info_y,
    info_z,
    info_x,
    kv_sem,
    qs_sem,
    own_sem,
    info_sem,
    near_w_sem,
    ring_sem,
    pair_w_sem,
    gate_up_sem,
    core_sem,
    part_sem,
    att_sem,
    near_sem,
    slot_sem,
    hid_sem,
    mix_sem,
    sent,
):
    x_count, z_count, s_count = (lax.axis_size(name) for name in ("dp", "exp", "seq"))
    y_count = s_count // 2
    x, z, s = (lax.axis_index(name) for name in ("dp", "exp", "seq"))
    y, c = s // 2, s % 2
    other_c = 1 - c
    pair = 2 * y + other_c
    tok_rows, model_width = attended.shape
    head_cols = kv_in.shape[2]
    heads_here = head_cols // HEAD_DIM
    cols = weights.shape[4]
    rank = near_rows.shape[2]
    slots = 4 * CAP
    quarter = model_width // x_count

    def remote(src, dst, send_sem, recv_sem, device):
        return pltpu.make_async_remote_copy(
            src_ref=src,
            dst_ref=dst,
            send_sem=send_sem,
            recv_sem=recv_sem,
            device_id=device,
            device_id_type=MESH,
        )

    def wait_bytes(ref, sem):
        pltpu.make_async_copy(ref, ref, sem).wait()

    def first_column(y_to):
        return pl.multiple_of(x * quarter + (y_to // 2) * head_cols + (y_to % 2) * 256, LANES)

    def near_order(step):
        return lax.rem(1 + 2 * step - 3 * (step // 2), 4)

    barrier = pltpu.get_barrier_semaphore()

    def greet(device):
        pl.semaphore_signal(barrier, inc=1, device_id=device, device_id_type=MESH)

    def greet_seq(step, carry):
        greet({"seq": lax.rem(s + step, s_count)})
        return carry

    def greet_z(step, carry):
        greet({"exp": lax.rem(z + step, z_count)})
        return carry

    def greet_x(step, carry):
        greet({"dp": lax.rem(x + step, x_count)})

        def greet_xy(y_step, inner):
            greet(
                {
                    "dp": lax.rem(x + step, x_count),
                    "seq": 2 * lax.rem(y + y_step, y_count) + c,
                }
            )
            return inner

        return lax.fori_loop(1, y_count, greet_xy, carry)

    lax.fori_loop(1, s_count, greet_seq, 0)
    lax.fori_loop(1, z_count, greet_z, 0)
    lax.fori_loop(1, x_count, greet_x, 0)

    my_rows = pl.ds(pl.multiple_of(s * tok_rows, tok_rows), tok_rows)
    my_cols = pl.ds(pl.multiple_of(s * head_cols, head_cols), head_cols)
    kv_refs = (key_ref, value_ref)
    qs_refs = (query_ref, stream_ref)
    for which in range(2):
        pltpu.make_async_copy(
            kv_refs[which].at[:, my_cols], kv_in.at[which, my_rows, :], kv_sem
        ).start()
        pltpu.make_async_copy(
            qs_refs[which].at[:, my_cols], qs_in.at[s, which], qs_sem.at[s]
        ).start()
        pltpu.make_async_copy(
            down_ref.at[which, :, pl.ds(first_column(y), cols)],
            weights.at[c, z, y, pl.ds(which * LANES, LANES), :],
            near_w_sem,
        ).start()
    pltpu.make_async_copy(gate_up_ref, gate_up.at[c], gate_up_sem.at[0]).start()
    pltpu.make_async_copy(stream_ref, stream_own, own_sem).start()
    pltpu.make_async_copy(info_ref, info_y.at[y], info_sem.at[0]).start()

    pl.semaphore_wait(barrier, s_count - 1 + z_count - 1 + (x_count - 1) * y_count)

    def near_first(step, carry):
        y_to = lax.rem(y + near_order(step), y_count)
        device = {"seq": 2 * y_to + c}
        remote(info_ref, info_y.at[y], sent.at[0], info_sem.at[0], device).start()
        for which in range(2):
            remote(
                down_ref.at[which, :, pl.ds(first_column(y_to), cols)],
                weights.at[c, z, y, pl.ds(which * LANES, LANES), :],
                sent.at[1],
                near_w_sem,
                device,
            ).start()
        return carry

    lax.fori_loop(0, y_count - 1, near_first, 0)

    def send_parts(refs, slot_of, sem, send_sem):
        def one_chip(step, carry):
            y_to = lax.rem(y + near_order(step), y_count)

            def one_core(core, inner):
                s_to = 2 * y_to + core

                @pl.when(s_to != s)
                def _send():
                    columns = pl.ds(pl.multiple_of(s_to * head_cols, head_cols), head_cols)
                    for which in range(2):
                        remote(
                            refs[which].at[:, columns], slot_of(which), send_sem, sem, {"seq": s_to}
                        ).start()

                return inner

            return lax.fori_loop(0, 2, one_core, carry)

        lax.fori_loop(0, y_count, one_chip, 0)

    send_parts(kv_refs, lambda which: kv_in.at[which, my_rows, :], kv_sem, sent.at[2])
    send_parts(qs_refs, lambda which: qs_in.at[s, which], qs_sem.at[s], sent.at[3])
    remote(gate_up_ref, gate_up.at[c], sent.at[4], gate_up_sem.at[1], {"seq": pair}).start()

    wait_bytes(info_y, info_sem.at[0])
    pltpu.make_async_copy(info_y, info_z.at[z], info_sem.at[1]).start()
    pltpu.make_async_copy(info_y, info_x.at[x], info_sem.at[2]).start()

    def info_to_z(step, carry):
        remote(
            info_y,
            info_z.at[z],
            sent.at[5],
            info_sem.at[1],
            {"exp": lax.rem(z + step, z_count)},
        ).start()
        return carry

    def info_to_x(step, carry):
        remote(
            info_y,
            info_x.at[x],
            sent.at[6],
            info_sem.at[2],
            {"dp": lax.rem(x + step, x_count)},
        ).start()
        return carry

    lax.fori_loop(1, z_count, info_to_z, 0)
    lax.fori_loop(1, x_count, info_to_x, 0)

    def pass_on(block, up, down):
        held = weights.at[c, block]
        if up is not None:

            @pl.when(up)
            def _up():
                remote(
                    held,
                    held,
                    sent.at[7],
                    ring_sem.at[block],
                    {"exp": lax.rem(z + 1, z_count)},
                ).start()

        if down is not None:

            @pl.when(down)
            def _down():
                remote(
                    held,
                    held,
                    sent.at[7],
                    ring_sem.at[block],
                    {"exp": lax.rem(z + z_count - 1, z_count)},
                ).start()

        remote(held, held, sent.at[8], pair_w_sem, {"seq": pair}).start()

    always = z >= 0
    half = z_count // 2

    def ring_step(step):
        below = lax.rem(z + z_count - step, z_count)
        above = lax.rem(z + step, z_count)
        wait_bytes(weights.at[c, below], ring_sem.at[below])
        if step == half:
            pass_on(below, None, None)
            return
        pass_on(below, always if step < half - 1 else c == 0, None)
        wait_bytes(weights.at[c, above], ring_sem.at[above])
        pass_on(above, None, always if step < half - 1 else c == 1)

    wait_bytes(weights.at[c, z], near_w_sem)
    pass_on(z, always, always)
    ring_step(1)

    wait_bytes(kv_in, kv_sem)
    ring_step(2)

    length = s_count * tok_rows
    lane = lax.broadcasted_iota(jnp.int32, (length, HEAD_DIM), 1)
    ones_column = jnp.where(lane == 0, 1.0, 0.0).astype(jnp.bfloat16)
    exponent_scale = 1.0 / (math.sqrt(HEAD_DIM) * math.log(2.0))
    gate_row = attn_gate_ref[:, my_cols].astype(jnp.float32)
    scale_row = ffn_scale_ref[:, my_cols].astype(jnp.float32)
    two = 2 * tok_rows
    tail_lane = lax.broadcasted_iota(jnp.int32, (two, LANES), 1)

    def with_tail(values, square, tail):
        high = square.astype(jnp.bfloat16).astype(jnp.float32)
        extra = jnp.where(tail == 0, high, jnp.where(tail == 1, square - high, 0.0))
        return jnp.concatenate([values, extra], axis=1)

    def add_core_part(step):
        wait_bytes(core_recv.at[step], core_sem.at[step])
        total = own_part[step] + core_recv[step].astype(jnp.float32)
        square = total[:, rank : rank + 1] + total[:, rank + 1 : rank + 2]
        return total[:, :rank], square

    def send_part(step):
        values, square = add_core_part(step)
        part_send[step] = with_tail(values, square, tail_lane[:tok_rows]).astype(jnp.bfloat16)
        distance = near_order(step)
        y_to = lax.rem(y + y_count - distance, y_count)
        remote(
            part_send.at[step],
            part_recv.at[step],
            sent.at[10],
            part_sem,
            {"seq": 2 * y_to + c},
        ).start()

    def one_chip(step, carry):
        y_from = lax.rem(y + y_count - near_order(step), y_count)
        for core in range(2):
            wait_bytes(qs_in.at[2 * y_from + core], qs_sem.at[2 * y_from + core])
        both = pl.ds(2 * y_from, 2)
        square = jnp.zeros((two, 1), jnp.float32)
        for head in range(heads_here):
            part = slice(head * HEAD_DIM, (head + 1) * HEAD_DIM)
            scores = lax.dot_general(
                qs_in[both, 0, :, part].reshape(two, HEAD_DIM),
                kv_in[0, :, part],
                (((1,), (1,)), ((), ())),
                preferred_element_type=jnp.float32,
            )
            row_max = jnp.max(scores, axis=-1, keepdims=True)
            raised = jnp.exp2((scores - row_max) * exponent_scale).astype(jnp.bfloat16)
            value_ones = jnp.concatenate([kv_in[1, :, part], ones_column], axis=1)
            mixed = jnp.dot(raised, value_ones, preferred_element_type=jnp.float32)
            mixed = (mixed[:, :HEAD_DIM] / mixed[:, HEAD_DIM : HEAD_DIM + 1]).astype(jnp.bfloat16)
            att_out[both, :, part] = mixed.reshape(2, tok_rows, HEAD_DIM)
            residual = qs_in[both, 1, :, part].reshape(two, HEAD_DIM).astype(
                jnp.float32
            ) + gate_row[:, part] * mixed.astype(jnp.float32)
            modulated[:, part] = (residual * scale_row[:, part]).astype(jnp.bfloat16)
            square = square + jnp.sum(residual * residual, axis=1, keepdims=True)
        product = jnp.dot(modulated[...], basis_ref[...], preferred_element_type=jnp.float32)
        partial[...] = with_tail(product, square, tail_lane).reshape(partial.shape)
        own_part[step] = partial[c]
        core_send[step] = partial[other_c].astype(jnp.bfloat16)
        remote(
            core_send.at[step], core_recv.at[step], sent.at[9], core_sem.at[step], {"seq": pair}
        ).start()

        @pl.when(step > 0)
        def _previous():
            send_part(step - 1)

        return carry

    lax.fori_loop(0, 2, one_chip, 0)
    ring_step(3)
    lax.fori_loop(2, y_count, one_chip, 0)

    def send_attended(s_to, carry):
        @pl.when(s_to == s)
        def _keep():
            pltpu.make_async_copy(att_out.at[s_to], attended.at[:, my_cols], att_sem).start()

        @pl.when(s_to != s)
        def _send():
            remote(
                att_out.at[s_to], attended.at[:, my_cols], sent.at[11], att_sem, {"seq": s_to}
            ).start()

        return carry

    values, square = add_core_part(y_count - 1)
    wait_bytes(part_recv, part_sem)
    for step in range(y_count - 1):
        arrived = part_recv[step].astype(jnp.float32)
        values = values + arrived[:, :rank]
        square = square + arrived[:, rank : rank + 1] + arrived[:, rank + 1 : rank + 2]
    low_rank = (values / jnp.sqrt(square / model_width + epsilon)).astype(jnp.bfloat16)

    def pick_rows(y_to):
        row = lax.broadcasted_iota(jnp.int32, (z_count * slots, tok_rows), 0)
        slot_here = (((row // slots) * y_count + y_to) * slots + row % slots).astype(jnp.float32)
        pick = (slot_here == info_ref[0:1, :]) | (slot_here == info_ref[1:2, :])
        pick = jnp.where(pick, 1.0, 0.0).astype(jnp.bfloat16)
        return jnp.dot(pick, low_rank, preferred_element_type=jnp.float32).astype(jnp.bfloat16)

    for step in range(y_count - 1):
        y_to = lax.rem(y + near_order(step), y_count)
        out_rows[step] = pick_rows(y_to)
        remote(
            out_rows.at[step], near_rows.at[y], sent.at[12], near_sem.at[y], {"seq": 2 * y_to + c}
        ).start()
    near_rows[y] = pick_rows(y)

    lax.fori_loop(0, s_count, send_attended, 0)

    def forward_rows(step, carry):
        y_from = lax.rem(y + y_count - near_order(lax.rem(step + y_count - 1, y_count)), y_count)

        @pl.when(step > 0)
        def _arrive():
            wait_bytes(near_rows.at[y_from], near_sem.at[y_from])

        def to_z(z_step, inner):
            z_to = lax.rem(z + z_step, z_count)
            rows = pl.ds(pl.multiple_of(z_to * slots, slots), slots)
            remote(
                near_rows.at[y_from, rows, :],
                slot_rows.at[z, y_from],
                sent.at[13],
                slot_sem,
                {"exp": z_to},
            ).start()
            return inner

        own = pl.ds(pl.multiple_of(z * slots, slots), slots)
        pltpu.make_async_copy(near_rows.at[y_from, own, :], slot_rows.at[z, y_from], slot_sem).start()
        return lax.fori_loop(1, z_count, to_z, carry)

    lax.fori_loop(0, y_count, forward_rows, 0)

    wait_bytes(info_z, info_sem.at[1])
    wait_bytes(gate_up.at[c], gate_up_sem.at[0])
    wait_bytes(gate_up.at[other_c], gate_up_sem.at[1])
    sources = z_count * y_count
    rows_total = sources * slots
    named = info_z[...].reshape(sources, info_z.shape[2], tok_rows)
    place = lax.broadcasted_iota(jnp.int32, (sources, slots, tok_rows), 1)
    slot_here = (place + (z * y_count + y) * slots).astype(jnp.float32)
    weight = jnp.where(slot_here == named[:, 0:1, :], named[:, 2:3, :], 0.0) + jnp.where(
        slot_here == named[:, 1:2, :], named[:, 3:4, :], 0.0
    )
    weight = jnp.sum(weight, axis=2, keepdims=True).reshape(rows_total, 1)

    wait_bytes(slot_rows, slot_sem)
    rows = slot_rows[...].reshape(rows_total, rank)
    expert = lax.broadcasted_iota(jnp.int32, (rows_total, 1), 0) % slots // CAP
    both_halves = jnp.zeros((rows_total, gate_up.shape[3]), jnp.float32)
    for which in range(4):
        product = jnp.dot(
            rows, gate_up[which // 2, which % 2], preferred_element_type=jnp.float32
        )
        both_halves = jnp.where(expert == which, product, both_halves)
    gate, up = both_halves[:, :LANES], both_halves[:, LANES:]
    hidden[...] = (gate / (1.0 + jnp.exp(-gate)) * up * weight).astype(jnp.bfloat16)

    run = y_count * slots
    own_run = pl.ds(pl.multiple_of(z * run, run), run)

    def hidden_to_z(step, carry):
        z_to = lax.rem(z + step, z_count)
        remote(
            hidden.at[pl.ds(pl.multiple_of(z_to * run, run), run), :],
            hidden_all.at[y, x, own_run, :],
            sent.at[14],
            hid_sem.at[0],
            {"exp": z_to},
        ).start()
        return carry

    pltpu.make_async_copy(
        hidden.at[own_run, :], hidden_all.at[y, x, own_run, :], hid_sem.at[0]
    ).start()
    lax.fori_loop(1, z_count, hidden_to_z, 0)
    wait_bytes(hidden_all.at[y, x], hid_sem.at[0])

    def hidden_to_x(step, carry):
        held = hidden_all.at[y, x]
        remote(
            held, held, sent.at[15], hid_sem.at[1], {"dp": lax.rem(x + step, x_count)}
        ).start()
        return carry

    lax.fori_loop(1, x_count, hidden_to_x, 0)
    wait_bytes(hidden_all.at[y, pl.ds(0, x_count - 1)], hid_sem.at[1])

    def hidden_to_y(step, carry):
        held = hidden_all.at[y]
        y_to = lax.rem(y + near_order(step), y_count)
        remote(held, held, sent.at[16], hid_sem.at[2 + y], {"seq": 2 * y_to + c}).start()
        return carry

    lax.fori_loop(0, y_count - 1, hidden_to_y, 0)

    ring_step(half)
    wait_bytes(weights.at[other_c], pair_w_sem)
    wait_bytes(info_x, info_sem.at[2])

    group = x_count * y_count
    chip_rows = group * slots
    chip_expert = lax.broadcasted_iota(jnp.int32, (chip_rows, LANES), 0) % slots // CAP

    def down_chip(step, carry):
        y_from = lax.rem(y + y_count - near_order(lax.rem(step + y_count - 1, y_count)), y_count)

        @pl.when(step > 0)
        def _arrive():
            wait_bytes(hidden_all.at[y_from], hid_sem.at[2 + y_from])

        def down_one(z_from, inner):
            at = pl.ds(pl.multiple_of(z_from * run, run), run)
            held = jnp.concatenate(
                [hidden_all[y_from, x_from, at, :] for x_from in range(x_count)], axis=0
            )
            held = held.astype(jnp.float32)
            masked = [
                jnp.where(chip_expert == which, held, 0.0).astype(jnp.bfloat16)
                for which in range(4)
            ]
            product = jnp.dot(
                jnp.concatenate(masked[:2], axis=1),
                weights[0, z_from, y_from],
                preferred_element_type=jnp.float32,
            ) + jnp.dot(
                jnp.concatenate(masked[2:], axis=1),
                weights[1, z_from, y_from],
                preferred_element_type=jnp.float32,
            )
            to = pl.ds(pl.multiple_of((z_from * y_count + y_from) * slots, slots), slots)
            slot_out[:, to, :] = product.astype(jnp.bfloat16).reshape(group, slots, cols)
            return inner

        return lax.fori_loop(0, z_count, down_one, carry)

    lax.fori_loop(0, y_count, down_chip, 0)

    mine = x * y_count + y

    def mix_one(step, carry):
        x_to = lax.rem(x + (step + 1) // y_count, x_count)
        y_to = lax.rem(y + step + 1, y_count)
        to = x_to * y_count + y_to
        slot_iota = lax.broadcasted_iota(jnp.int32, (slot_out.shape[1], tok_rows), 0).astype(
            jnp.float32
        )
        named_here = info_x[x_to, y_to]
        pick = (slot_iota == named_here[0:1, :]) | (slot_iota == named_here[1:2, :])
        pick = jnp.where(pick, 1.0, 0.0).astype(jnp.bfloat16)
        mixed = lax.dot_general(
            pick, slot_out[to], (((0,), (0,)), ((), ())), preferred_element_type=jnp.float32
        )
        mix_out[to] = mixed.astype(jnp.bfloat16)

        @pl.when(to == mine)
        def _keep():
            pltpu.make_async_copy(mix_out.at[to], mix_in.at[mine], mix_sem).start()

        @pl.when(to != mine)
        def _send():
            remote(
                mix_out.at[to],
                mix_in.at[mine],
                sent.at[17],
                mix_sem,
                {"dp": x_to, "seq": 2 * y_to + c},
            ).start()

        return carry

    lax.fori_loop(0, group, mix_one, 0)

    wait_bytes(stream_own, own_sem)
    wait_bytes(attended, att_sem)
    wait_bytes(mix_in, mix_sem)
    for block in range(s_count):
        part = slice(block * head_cols, (block + 1) * head_cols)
        mixed = jnp.concatenate([mix_in[2 * block], mix_in[2 * block + 1, :, LANES:]], axis=1)
        residual = stream_own[:, part].astype(jnp.float32) + attn_gate_ref[:, part].astype(
            jnp.float32
        ) * attended[:, part].astype(jnp.float32)
        output_ref[:, part] = (
            residual + ffn_gate_ref[:, part].astype(jnp.float32) * mixed.astype(jnp.float32)
        ).astype(jnp.bfloat16)

    wait_bytes(info_y.at[pl.ds(0, y_count - 1)], sent.at[0])
    wait_bytes(weights.at[0, 0, pl.ds(0, y_count - 1)], sent.at[1])
    wait_bytes(kv_in.at[:, pl.ds(0, (s_count - 1) * tok_rows), :], sent.at[2])
    wait_bytes(qs_in.at[pl.ds(0, s_count - 1)], sent.at[3])
    wait_bytes(gate_up.at[0], sent.at[4])
    wait_bytes(info_z.at[pl.ds(0, z_count - 1)], sent.at[5])
    wait_bytes(info_x.at[pl.ds(0, x_count - 1)], sent.at[6])
    wait_bytes(weights.at[0, pl.ds(0, z_count - 1)], sent.at[7])
    wait_bytes(weights.at[0], sent.at[8])
    wait_bytes(core_send, sent.at[9])
    wait_bytes(part_send, sent.at[10])
    wait_bytes(att_out.at[pl.ds(0, s_count - 1)], sent.at[11])
    wait_bytes(out_rows, sent.at[12])
    wait_bytes(slot_rows.at[pl.ds(0, z_count - 1)], sent.at[13])
    wait_bytes(hidden.at[pl.ds(0, (z_count - 1) * run), :], sent.at[14])
    wait_bytes(hidden_all.at[0, pl.ds(0, x_count - 1)], sent.at[15])
    wait_bytes(hidden_all.at[pl.ds(0, y_count - 1)], sent.at[16])
    wait_bytes(mix_out.at[pl.ds(0, group - 1)], sent.at[17])


def on_device(
    query_rows,
    key_rows,
    value_rows,
    stream,
    shared_basis,
    expert_gate_up,
    expert_down,
    attn_gate,
    ffn_scale,
    ffn_gate,
    expert_ids,
    route_weights,
):
    x_count, z_count, s_count = (lax.axis_size(name) for name in ("dp", "exp", "seq"))
    y_count = s_count // 2
    tok_rows, model_width = stream.shape
    experts_here, hidden_cols, _ = expert_down.shape
    expert_total = z_count * s_count * experts_here
    rank = shared_basis.shape[1]
    head_cols = model_width // s_count
    cols = 384
    slots = 4 * CAP
    length = s_count * tok_rows
    group = x_count * y_count

    flat_ids = expert_ids.T.reshape(2 * tok_rows)
    one_hot = (flat_ids[:, None] == jnp.arange(expert_total, dtype=jnp.int32)[None, :]).astype(
        jnp.bfloat16
    )
    entry = jnp.arange(2 * tok_rows, dtype=jnp.int32)
    order = 2 * (entry % tok_rows) + entry // tok_rows
    before = (order[None, :] < order[:, None]).astype(jnp.bfloat16)
    same = jnp.dot(before, one_hot, preferred_element_type=jnp.float32)
    slot_rank = jnp.sum(same * one_hot.astype(jnp.float32), axis=1)
    slot_ids = flat_ids.astype(jnp.float32) * CAP + slot_rank
    info = jnp.concatenate(
        [
            slot_ids.reshape(2, tok_rows),
            route_weights.T,
            jnp.zeros((4, tok_rows), jnp.float32),
        ],
        axis=0,
    )

    vmem = pl.BlockSpec(memory_space=pltpu.VMEM)
    anywhere = pl.BlockSpec(memory_space=pl.ANY)
    bf16, f32 = jnp.bfloat16, jnp.float32
    wide = rank + LANES
    dma = pltpu.SemaphoreType.DMA
    return pl.pallas_call(
        block_kernel,
        out_shape=jax.ShapeDtypeStruct((tok_rows, model_width), bf16),
        in_specs=[anywhere] * 6 + [vmem] * 5,
        out_specs=vmem,
        scratch_shapes=[
            pltpu.VMEM((2, length, head_cols), bf16),
            pltpu.VMEM((s_count, 2, tok_rows, head_cols), bf16),
            pltpu.VMEM((tok_rows, model_width), bf16),
            pltpu.VMEM((s_count, tok_rows, head_cols), bf16),
            pltpu.VMEM((tok_rows, model_width), bf16),
            pltpu.VMEM((2 * tok_rows, head_cols), bf16),
            pltpu.VMEM((2, tok_rows, wide), f32),
            pltpu.VMEM((y_count, tok_rows, wide), f32),
            pltpu.VMEM((y_count, tok_rows, wide), bf16),
            pltpu.VMEM((y_count, tok_rows, wide), bf16),
            pltpu.VMEM((y_count - 1, tok_rows, wide), bf16),
            pltpu.VMEM((y_count - 1, tok_rows, wide), bf16),
            pltpu.VMEM((y_count - 1, z_count * slots, rank), bf16),
            pltpu.VMEM((y_count, z_count * slots, rank), bf16),
            pltpu.VMEM((z_count, y_count, slots, rank), bf16),
            pltpu.VMEM((2,) + expert_gate_up.shape, bf16),
            pltpu.VMEM((z_count * y_count * slots, hidden_cols), bf16),
            pltpu.VMEM((y_count, x_count, z_count * y_count * slots, hidden_cols), bf16),
            pltpu.VMEM((2, z_count, y_count, experts_here * hidden_cols, cols), bf16),
            pltpu.VMEM((group, z_count * y_count * slots, cols), bf16),
            pltpu.VMEM((group, tok_rows, cols), bf16),
            pltpu.VMEM((group, tok_rows, cols), bf16),
            pltpu.VMEM((y_count, 8, tok_rows), f32),
            pltpu.VMEM((z_count, y_count, 8, tok_rows), f32),
            pltpu.VMEM((x_count, y_count, 8, tok_rows), f32),
            dma,
            dma((s_count,)),
            dma,
            dma((3,)),
            dma,
            dma((z_count,)),
            dma,
            dma((2,)),
            dma((y_count,)),
            dma,
            dma,
            dma((y_count,)),
            dma,
            dma((2 + y_count,)),
            dma,
            dma((18,)),
        ],
        compiler_params=pltpu.CompilerParams(
            collective_id=0, has_side_effects=True, vmem_limit_bytes=62 * 1024 * 1024
        ),
        name="block",
    )(
        query_rows,
        key_rows,
        value_rows,
        stream,
        expert_down,
        expert_gate_up,
        shared_basis,
        attn_gate,
        ffn_scale,
        ffn_gate,
        info,
    )


def solution(mesh):
    in_specs = (
        P(("dp", "exp", "seq"), None),
        P(("dp", "exp", "seq"), None),
        P(("dp", "exp", "seq"), None),
        P(("dp", "exp", "seq"), None),
        P("seq", None),
        P(("exp", "seq"), None, None),
        P(("exp", "seq"), None, None),
        P(("dp", "exp"), None),
        P(("dp", "exp"), None),
        P(("dp", "exp"), None),
        P(("dp", "exp", "seq"), None),
        P(("dp", "exp", "seq"), None),
    )
    out_specs = P(("dp", "exp", "seq"), None)
    return jax.shard_map(
        on_device, mesh=mesh, in_specs=in_specs, out_specs=out_specs, check_vma=False
    )
```

```python
import functools
import math

import jax
import jax.numpy as jnp
from jax import lax
from jax.experimental import pallas as pl
from jax.experimental.pallas import tpu as pltpu
from jax.sharding import PartitionSpec as P

HEAD_DIM = 128
LANES = 128
MESH = pl.DeviceIdType.MESH
epsilon = 1e-06
CAP = 4


def block_kernel(
    query_ref,
    key_ref,
    value_ref,
    stream_ref,
    down_ref,
    gate_up_ref,
    basis_ref,
    attn_gate_ref,
    ffn_scale_ref,
    ffn_gate_ref,
    ids_ref,
    route_ref,
    output_ref,
    kv_in,
    qs_in,
    stream_own,
    att_out,
    attended,
    modulated,
    partial,
    own_part,
    core_send,
    core_recv,
    part_send,
    part_recv,
    out_rows,
    near_rows,
    slot_rows,
    gate_up,
    hidden_all,
    weights,
    slot_out,
    mix_out,
    mix_in,
    info_own,
    info_y,
    info_x,
    kv_sem,
    qs_sem,
    batch_sem,
    own_sem,
    info_sem,
    near_w_sem,
    ring_sem,
    pair_w_sem,
    near_g_sem,
    ring_g_sem,
    pair_g_sem,
    core_sem,
    part_sem,
    att_sem,
    near_sem,
    slot_sem,
    hid_sem,
    hid_y_sem,
    hid_x_sem,
    mix_sem,
    sent,
):
    x_count, z_count, s_count = (lax.axis_size(name) for name in ("dp", "exp", "seq"))
    y_count = s_count // 2
    x, z, s = (lax.axis_index(name) for name in ("dp", "exp", "seq"))
    y, c = s // 2, s % 2
    other_c = 1 - c
    pair = 2 * y + other_c
    tok_rows, model_width = attended.shape
    head_cols = kv_in.shape[2]
    heads_here = head_cols // HEAD_DIM
    cols = weights.shape[4]
    rank = near_rows.shape[2]
    slots = 4 * CAP
    quarter = model_width // x_count

    def remote(src, dst, send_sem, recv_sem, device):
        return pltpu.make_async_remote_copy(
            src_ref=src,
            dst_ref=dst,
            send_sem=send_sem,
            recv_sem=recv_sem,
            device_id=device,
            device_id_type=MESH,
        )

    def wait_bytes(ref, sem):
        pltpu.make_async_copy(ref, ref, sem).wait()

    def first_column(y_to):
        return pl.multiple_of(x * quarter + (y_to // 2) * head_cols + (y_to % 2) * 256, LANES)

    def near_order(step):
        return step + step // 2 - 2 * (step // 3)

    barrier = pltpu.get_barrier_semaphore()

    def greet(device):
        pl.semaphore_signal(barrier, inc=1, device_id=device, device_id_type=MESH)

    def greet_seq(step, carry):
        greet({"seq": lax.rem(s + step, s_count)})
        return carry

    def greet_z(step, carry):
        greet({"exp": lax.rem(z + step, z_count)})
        return carry

    def greet_x(step, carry):
        greet({"dp": lax.rem(x + step, x_count)})

        def greet_xy(y_step, inner):
            greet(
                {
                    "dp": lax.rem(x + step, x_count),
                    "seq": 2 * lax.rem(y + y_step, y_count) + c,
                }
            )
            return inner

        return lax.fori_loop(1, y_count, greet_xy, carry)

    lax.fori_loop(1, s_count, greet_seq, 0)
    lax.fori_loop(1, z_count, greet_z, 0)
    lax.fori_loop(1, x_count, greet_x, 0)

    my_rows = pl.ds(pl.multiple_of(s * tok_rows, tok_rows), tok_rows)
    my_cols = pl.ds(pl.multiple_of(s * head_cols, head_cols), head_cols)
    kv_refs = (key_ref, value_ref)
    qs_refs = (query_ref, stream_ref)
    for which in range(2):
        pltpu.make_async_copy(
            kv_refs[which].at[:, my_cols], kv_in.at[which, my_rows, :], kv_sem
        ).start()
        pltpu.make_async_copy(
            qs_refs[which].at[:, my_cols], qs_in.at[s, which], qs_sem.at[s]
        ).start()
        pltpu.make_async_copy(
            down_ref.at[which, :, pl.ds(first_column(y), cols)],
            weights.at[c, z, y, pl.ds(which * LANES, LANES), :],
            near_w_sem,
        ).start()
    pltpu.make_async_copy(stream_ref, stream_own, own_sem).start()

    rank_part = rank // z_count
    twin = z - 2 * x

    @pl.when(z // 2 == x)
    def _own_gate_up():
        part = pl.ds(pl.multiple_of(z * rank_part, rank_part), rank_part)
        pltpu.make_async_copy(
            gate_up_ref.at[:, part, :], gate_up.at[c, z, twin], near_g_sem
        ).start()

    pl.semaphore_wait(barrier, s_count - 1 + z_count - 1 + (x_count - 1) * y_count)

    def near_first(step, carry):
        y_to = lax.rem(y + near_order(step), y_count)
        device = {"seq": 2 * y_to + c}
        for which in range(2):
            remote(
                down_ref.at[which, :, pl.ds(first_column(y_to), cols)],
                weights.at[c, z, y, pl.ds(which * LANES, LANES), :],
                sent.at[1],
                near_w_sem,
                device,
            ).start()
        return carry

    lax.fori_loop(1, y_count, near_first, 0)

    @pl.when(z // 2 == x)
    def _spread_gate_up():
        def to_z(step, carry):
            z_to = lax.rem(z + step, z_count)
            part = pl.ds(pl.multiple_of(z_to * rank_part, rank_part), rank_part)
            remote(
                gate_up_ref.at[:, part, :],
                gate_up.at[c, z_to, twin],
                sent.at[4],
                near_g_sem,
                {"exp": z_to},
            ).start()
            return carry

        lax.fori_loop(1, z_count, to_z, 0)


    def send_batch(refs, slot_of, sem, send_sem, distances):
        def one_copy(index, carry):
            s_to = 2 * lax.rem(y + distances[0] + 2 * (index % len(distances)), y_count) + (
                index // len(distances)
            )
            columns = pl.ds(pl.multiple_of(s_to * head_cols, head_cols), head_cols)
            for which in range(2):
                remote(
                    refs[which].at[:, columns], slot_of(which), send_sem, sem, {"seq": s_to}
                ).start()
            return carry

        if len(distances) == 2:
            columns = pl.ds(pl.multiple_of(pair * head_cols, head_cols), head_cols)
            for which in range(2):
                remote(
                    refs[which].at[:, columns], slot_of(which), send_sem, sem, {"seq": pair}
                ).start()
        lax.fori_loop(0, 2 * len(distances), one_copy, 0)

    batches = ((1, 3), (2,))

    def send_kv(batch):
        send_batch(
            kv_refs,
            lambda which: kv_in.at[which, my_rows, :],
            kv_sem,
            batch_sem.at[0, batch],
            batches[batch],
        )

    def send_qs(batch):
        send_batch(
            qs_refs,
            lambda which: qs_in.at[s, which],
            qs_sem.at[s],
            batch_sem.at[1, batch],
            batches[batch],
        )

    def batch_left(kind, batch):
        peers = 5 if batch == 0 else 2
        wait_bytes(qs_in.at[pl.ds(0, peers)], batch_sem.at[kind, batch])

    send_kv(0)

    entries = 2 * tok_rows
    experts = 4 * z_count * y_count
    ids_row = jnp.concatenate([ids_ref[0:1, :], ids_ref[1:2, :]], axis=1)
    named = lax.broadcasted_iota(jnp.int32, (experts, entries), 0) == ids_row
    entry = [lax.broadcasted_iota(jnp.int32, (entries, entries), axis) for axis in (0, 1)]
    entry = [2 * (one % tok_rows) + one // tok_rows for one in entry]
    before = jnp.where(entry[0] < entry[1], 1.0, 0.0).astype(jnp.bfloat16)
    counts = jnp.dot(
        jnp.where(named, 1.0, 0.0).astype(jnp.bfloat16), before, preferred_element_type=jnp.float32
    )
    slot_ids = (
        jnp.sum(jnp.where(named, counts, 0.0), axis=0, keepdims=True)
        + ids_row.astype(jnp.float32) * CAP
    )
    info_row = lax.broadcasted_iota(jnp.int32, info_own.shape, 0)
    info = jnp.where(info_row == 2, route_ref[0:1, :], 0.0)
    info = jnp.where(info_row == 3, route_ref[1:2, :], info)
    info = jnp.where(info_row == 0, slot_ids[:, :tok_rows], info)
    info_own[...] = jnp.where(info_row == 1, slot_ids[:, tok_rows:], info)
    pltpu.make_async_copy(info_own, info_y.at[y], info_sem.at[0]).start()

    def info_to_y(step, carry):
        y_to = lax.rem(y + step, y_count)
        remote(
            info_own, info_y.at[y], sent.at[0], info_sem.at[0], {"seq": 2 * y_to + c}
        ).start()
        return carry

    lax.fori_loop(1, y_count, info_to_y, 0)

    always = z >= 0
    half = z_count // 2

    def pass_on(buffer, sems, left_sem, pair_left, pair_sem, block, up, down):
        held = buffer.at[c, block]

        def pass_to(z_to):
            remote(held, held, left_sem, sems.at[block], {"exp": lax.rem(z_to, z_count)}).start()

        if up is not None:

            @pl.when(up)
            def _up():
                pass_to(z + 1)

        if down is not None:

            @pl.when(down)
            def _down():
                pass_to(z + z_count - 1)

        remote(held, held, pair_left, pair_sem, {"seq": pair}).start()

    def ring_step(ring, step):
        buffer, sems = ring[0], ring[1]
        below = lax.rem(z + z_count - step, z_count)
        above = lax.rem(z + step, z_count)
        wait_bytes(buffer.at[c, below], sems.at[below])
        if step == half:
            pass_on(*ring, below, None, None)
            return
        pass_on(*ring, below, always if step < half - 1 else c == 0, None)
        wait_bytes(buffer.at[c, above], sems.at[above])
        pass_on(*ring, above, None, always if step < half - 1 else c == 1)

    gate_ring = (gate_up, ring_g_sem, sent.at[13], sent.at[14], pair_g_sem)
    down_ring = (weights, ring_sem, sent.at[7], sent.at[8], pair_w_sem)

    wait_bytes(gate_up.at[c, z], near_g_sem)
    pass_on(*gate_ring, z, always, always)
    send_kv(1)
    ring_step(gate_ring, 1)
    wait_bytes(weights.at[c, z], near_w_sem)
    pass_on(*down_ring, z, always, always)
    batch_left(0, 0)
    send_qs(0)
    ring_step(gate_ring, 2)
    ring_step(gate_ring, 3)

    wait_bytes(info_y, info_sem.at[0])
    pltpu.make_async_copy(info_y, info_x.at[x], info_sem.at[1]).start()

    def info_to_x(step, carry):
        remote(
            info_y,
            info_x.at[x],
            sent.at[6],
            info_sem.at[1],
            {"dp": lax.rem(x + step, x_count)},
        ).start()
        return carry

    lax.fori_loop(1, x_count, info_to_x, 0)
    wait_bytes(kv_in, kv_sem)

    length = s_count * tok_rows
    lane = lax.broadcasted_iota(jnp.int32, (length, HEAD_DIM), 1)
    ones_column = jnp.where(lane == 0, 1.0, 0.0).astype(jnp.bfloat16)
    exponent_scale = 1.0 / (math.sqrt(HEAD_DIM) * math.log(2.0))
    gate_row = attn_gate_ref[:, my_cols].astype(jnp.float32)
    scale_row = ffn_scale_ref[:, my_cols].astype(jnp.float32)
    two = 2 * tok_rows
    tail_lane = lax.broadcasted_iota(jnp.int32, (two, LANES), 1)

    def with_tail(values, square, tail):
        high = square.astype(jnp.bfloat16).astype(jnp.float32)
        extra = jnp.where(tail == 0, high, jnp.where(tail == 1, square - high, 0.0))
        return jnp.concatenate([values, extra], axis=1)

    def add_core_part(step):
        wait_bytes(core_recv.at[step], core_sem.at[step])
        total = own_part[step] + core_recv[step].astype(jnp.float32)
        square = total[:, rank : rank + 1] + total[:, rank + 1 : rank + 2]
        return total[:, :rank], square

    def send_part(step):
        values, square = add_core_part(step)
        part_send[step - 1] = with_tail(values, square, tail_lane[:tok_rows]).astype(jnp.bfloat16)
        distance = near_order(step)
        y_to = lax.rem(y + y_count - distance, y_count)
        remote(
            part_send.at[step - 1],
            part_recv.at[step - 1],
            sent.at[10],
            part_sem,
            {"seq": 2 * y_to + c},
        ).start()

    def one_chip(step, carry):
        y_from = lax.rem(y + y_count - near_order(step), y_count)

        @pl.when(step > 1)
        def _previous():
            send_part(step - 1)

        for core in range(2):
            wait_bytes(qs_in.at[2 * y_from + core], qs_sem.at[2 * y_from + core])
        both = pl.ds(2 * y_from, 2)
        square = jnp.zeros((two, 1), jnp.float32)
        for head in range(heads_here):
            part = slice(head * HEAD_DIM, (head + 1) * HEAD_DIM)
            scores = lax.dot_general(
                qs_in[both, 0, :, part].reshape(two, HEAD_DIM),
                kv_in[0, :, part],
                (((1,), (1,)), ((), ())),
                preferred_element_type=jnp.float32,
            )
            row_max = jnp.max(scores, axis=-1, keepdims=True)
            raised = jnp.exp2((scores - row_max) * exponent_scale).astype(jnp.bfloat16)
            value_ones = jnp.concatenate([kv_in[1, :, part], ones_column], axis=1)
            mixed = jnp.dot(raised, value_ones, preferred_element_type=jnp.float32)
            mixed = (mixed[:, :HEAD_DIM] / mixed[:, HEAD_DIM : HEAD_DIM + 1]).astype(jnp.bfloat16)
            att_out[both, :, part] = mixed.reshape(2, tok_rows, HEAD_DIM)
            residual = qs_in[both, 1, :, part].reshape(two, HEAD_DIM).astype(
                jnp.float32
            ) + gate_row[:, part] * mixed.astype(jnp.float32)
            modulated[:, part] = (residual * scale_row[:, part]).astype(jnp.bfloat16)
            square = square + jnp.sum(residual * residual, axis=1, keepdims=True)
        product = jnp.dot(modulated[...], basis_ref[...], preferred_element_type=jnp.float32)
        partial[...] = with_tail(product, square, tail_lane).reshape(partial.shape)
        own_part[step] = partial[c]
        core_send[step] = partial[other_c].astype(jnp.bfloat16)
        remote(
            core_send.at[step], core_recv.at[step], sent.at[9], core_sem.at[step], {"seq": pair}
        ).start()
        return carry

    def after_chip(step, carry):
        one_chip(step, carry)

        @pl.when(step == 0)
        def _last_batch():
            ring_step(gate_ring, half)
            batch_left(0, 1)
            send_qs(1)

        @pl.when(step == 1)
        def _ring_one():
            ring_step(down_ring, 1)

        @pl.when(step == 2)
        def _ring_two():
            ring_step(down_ring, 2)

        return carry

    lax.fori_loop(0, y_count, after_chip, 0)
    send_part(y_count - 1)

    def send_attended(s_to, carry):
        @pl.when(s_to == s)
        def _keep():
            pltpu.make_async_copy(att_out.at[s_to], attended.at[:, my_cols], att_sem).start()

        @pl.when(s_to != s)
        def _send():
            remote(
                att_out.at[s_to], attended.at[:, my_cols], sent.at[11], att_sem, {"seq": s_to}
            ).start()

        return carry

    values, square = add_core_part(0)
    wait_bytes(part_recv, part_sem)
    for step in range(y_count - 1):
        arrived = part_recv[step].astype(jnp.float32)
        values = values + arrived[:, :rank]
        square = square + arrived[:, rank : rank + 1] + arrived[:, rank + 1 : rank + 2]
    low_rank = (values / jnp.sqrt(square / model_width + epsilon)).astype(jnp.bfloat16)

    def pick_rows(y_to):
        row = lax.broadcasted_iota(jnp.int32, (z_count * slots, tok_rows), 0)
        slot_here = (((row // slots) * y_count + y_to) * slots + row % slots).astype(jnp.float32)
        pick = (slot_here == info_own[0:1, :]) | (slot_here == info_own[1:2, :])
        pick = jnp.where(pick, 1.0, 0.0).astype(jnp.bfloat16)
        return jnp.dot(pick, low_rank, preferred_element_type=jnp.float32).astype(jnp.bfloat16)

    near_rows[y] = pick_rows(y)
    chip_slots = 2 * slots

    def forward_rows(y_from):
        def to_x(x_step, inner):
            x_to = lax.rem(x + near_order(x_step), x_count)
            rows = pl.ds(pl.multiple_of(x_to * chip_slots, chip_slots), chip_slots)
            remote(
                near_rows.at[y_from, rows, :],
                slot_rows.at[x, y_from],
                sent.at[5],
                slot_sem,
                {"dp": x_to},
            ).start()
            return inner

        lax.fori_loop(1, x_count, to_x, 0)
        own = pl.ds(pl.multiple_of(x * chip_slots, chip_slots), chip_slots)
        pltpu.make_async_copy(near_rows.at[y_from, own, :], slot_rows.at[x, y_from], slot_sem).start()

    forward_rows(y)
    for step in range(1, y_count):
        y_to = lax.rem(y + near_order(step), y_count)
        out_rows[step - 1] = pick_rows(y_to)
        remote(
            out_rows.at[step - 1],
            near_rows.at[y],
            sent.at[12],
            near_sem.at[y],
            {"seq": 2 * y_to + c},
        ).start()


    def forward_near(step, carry):
        y_from = lax.rem(y + y_count - near_order(step), y_count)
        wait_bytes(near_rows.at[y_from], near_sem.at[y_from])
        forward_rows(y_from)
        return carry

    lax.fori_loop(1, y_count, forward_near, 0)
    ring_step(down_ring, 3)

    wait_bytes(info_x, info_sem.at[1])
    group = x_count * y_count
    chip_rows = group * slots
    named_all = info_x[...].reshape(group, info_x.shape[2], tok_rows)
    place = lax.broadcasted_iota(jnp.int32, (group, slots, tok_rows), 1)
    weight = []
    for which in range(2):
        slot_here = (place + ((2 * x + which) * y_count + y) * slots).astype(jnp.float32)
        routed = jnp.where(
            slot_here == named_all[:, 0:1, :], named_all[:, 2:3, :], 0.0
        ) + jnp.where(slot_here == named_all[:, 1:2, :], named_all[:, 3:4, :], 0.0)
        weight.append(jnp.sum(routed, axis=2, keepdims=True).reshape(chip_rows, 1))

    wait_bytes(gate_up.at[other_c], pair_g_sem)
    wait_bytes(slot_rows, slot_sem)
    expert = lax.broadcasted_iota(jnp.int32, (chip_rows, 1), 0) % slots // CAP

    for twin_here in range(2):
        rows = slot_rows[:, :, pl.ds(twin_here * slots, slots), :].reshape(chip_rows, rank)
        both_halves = jnp.zeros((chip_rows, gate_up.shape[5]), jnp.float32)
        for which in range(4):
            product = jnp.dot(
                rows,
                gate_up[which // 2, :, twin_here, which % 2].reshape(rank, gate_up.shape[5]),
                preferred_element_type=jnp.float32,
            )
            both_halves = jnp.where(expert == which, product, both_halves)
        gate, up = both_halves[:, :LANES], both_halves[:, LANES:]
        hidden = gate / (1.0 + jnp.exp(-gate)) * up * weight[twin_here]
        hidden_all[x, y, twin_here] = hidden.astype(jnp.bfloat16)
        held = hidden_all.at[x, y, twin_here]

        def hidden_near(step, carry):
            if twin_here == 0:
                device = {"dp": lax.rem(x + near_order(step), x_count)}
            else:
                device = {"seq": 2 * lax.rem(y + near_order(step), y_count) + c}
            remote(held, held, sent.at[15], hid_sem.at[twin_here], device).start()
            return carry

        lax.fori_loop(1, x_count, hidden_near, 0)

    wait_bytes(hidden_all.at[pl.ds(0, x_count - 1), y, 0], hid_sem.at[0])

    def hidden_to_y(step, carry):
        held = hidden_all.at[:, y, 0]
        y_to = lax.rem(y + near_order(step), y_count)
        remote(held, held, sent.at[16], hid_y_sem.at[y], {"seq": 2 * y_to + c}).start()
        return carry

    lax.fori_loop(1, y_count, hidden_to_y, 0)
    wait_bytes(hidden_all.at[x, pl.ds(0, y_count - 1), 1], hid_sem.at[1])

    def hidden_to_x(step, carry):
        held = hidden_all.at[x, :, 1]
        x_to = lax.rem(x + near_order(step), x_count)
        remote(held, held, sent.at[18], hid_x_sem.at[x], {"dp": x_to}).start()
        return carry

    lax.fori_loop(1, x_count, hidden_to_x, 0)
    lax.fori_loop(0, s_count, send_attended, 0)
    ring_step(down_ring, half)
    wait_bytes(weights.at[other_c], pair_w_sem)

    chip_expert = lax.broadcasted_iota(jnp.int32, (chip_rows, LANES), 0) % slots // CAP

    def down_block(x_from, y_from, twin_here):
        held = hidden_all[x_from, y_from, twin_here].astype(jnp.float32)
        z_from = 2 * x_from + twin_here
        masked = [
            jnp.where(chip_expert == which, held, 0.0).astype(jnp.bfloat16) for which in range(4)
        ]
        product = jnp.dot(
            jnp.concatenate(masked[:2], axis=1),
            weights[0, z_from, y_from],
            preferred_element_type=jnp.float32,
        ) + jnp.dot(
            jnp.concatenate(masked[2:], axis=1),
            weights[1, z_from, y_from],
            preferred_element_type=jnp.float32,
        )
        to = pl.ds(pl.multiple_of((z_from * y_count + y_from) * slots, slots), slots)
        slot_out[:, to, :] = product.astype(jnp.bfloat16).reshape(group, slots, cols)

    def down_step(step, carry):
        y_from = lax.rem(y + y_count - near_order(step), y_count)
        x_from = lax.rem(x + x_count - near_order(step), x_count)

        @pl.when(step > 0)
        def _arrive_y():
            wait_bytes(hidden_all.at[:, y_from, 0], hid_y_sem.at[y_from])

        def down_first(other, inner):
            down_block(other, y_from, 0)
            return inner

        lax.fori_loop(0, x_count, down_first, 0)

        @pl.when(step > 0)
        def _arrive_x():
            wait_bytes(hidden_all.at[x_from, :, 1], hid_x_sem.at[x_from])

        def down_second(other, inner):
            down_block(x_from, other, 1)
            return inner

        lax.fori_loop(0, y_count, down_second, 0)
        return carry

    lax.fori_loop(0, y_count, down_step, 0)

    mine = x * y_count + y

    def mix_one(step, carry):
        x_to = lax.rem(x + (step + 1) // y_count, x_count)
        y_to = lax.rem(y + step + 1, y_count)
        to = x_to * y_count + y_to
        slot_iota = lax.broadcasted_iota(jnp.int32, (slot_out.shape[1], tok_rows), 0).astype(
            jnp.float32
        )
        named_here = info_x[x_to, y_to]
        pick = (slot_iota == named_here[0:1, :]) | (slot_iota == named_here[1:2, :])
        pick = jnp.where(pick, 1.0, 0.0).astype(jnp.bfloat16)
        mixed = lax.dot_general(
            pick, slot_out[to], (((0,), (0,)), ((), ())), preferred_element_type=jnp.float32
        )
        mix_out[to] = mixed.astype(jnp.bfloat16)

        @pl.when(to == mine)
        def _keep():
            pltpu.make_async_copy(mix_out.at[to], mix_in.at[mine], mix_sem).start()

        @pl.when(to != mine)
        def _send():
            remote(
                mix_out.at[to],
                mix_in.at[mine],
                sent.at[17],
                mix_sem,
                {"dp": x_to, "seq": 2 * y_to + c},
            ).start()

        return carry

    lax.fori_loop(0, group, mix_one, 0)

    wait_bytes(stream_own, own_sem)
    wait_bytes(attended, att_sem)
    wait_bytes(mix_in, mix_sem)
    for block in range(s_count):
        part = slice(block * head_cols, (block + 1) * head_cols)
        mixed = jnp.concatenate([mix_in[2 * block], mix_in[2 * block + 1, :, LANES:]], axis=1)
        residual = stream_own[:, part].astype(jnp.float32) + attn_gate_ref[:, part].astype(
            jnp.float32
        ) * attended[:, part].astype(jnp.float32)
        output_ref[:, part] = (
            residual + ffn_gate_ref[:, part].astype(jnp.float32) * mixed.astype(jnp.float32)
        ).astype(jnp.bfloat16)

    wait_bytes(info_y.at[pl.ds(0, y_count - 1)], sent.at[0])
    wait_bytes(weights.at[0, 0, pl.ds(0, y_count - 1)], sent.at[1])
    batch_left(1, 0)
    batch_left(1, 1)

    @pl.when(z // 2 == x)
    def _spread_done():
        wait_bytes(gate_up.at[0, pl.ds(0, z_count - 1), 0], sent.at[4])

    wait_bytes(slot_rows.at[pl.ds(0, x_count - 1)], sent.at[5])
    wait_bytes(info_x.at[pl.ds(0, x_count - 1)], sent.at[6])
    wait_bytes(weights.at[0, pl.ds(0, z_count - 1)], sent.at[7])
    wait_bytes(weights.at[0], sent.at[8])
    wait_bytes(core_send, sent.at[9])
    wait_bytes(part_send, sent.at[10])
    wait_bytes(att_out.at[pl.ds(0, s_count - 1)], sent.at[11])
    wait_bytes(out_rows, sent.at[12])
    wait_bytes(gate_up.at[0, pl.ds(0, z_count - 1)], sent.at[13])
    wait_bytes(gate_up.at[0], sent.at[14])
    wait_bytes(hidden_all.at[pl.ds(0, 2), pl.ds(0, y_count - 1), 0], sent.at[15])
    wait_bytes(hidden_all.at[:, pl.ds(0, y_count - 1), 0], sent.at[16])
    wait_bytes(hidden_all.at[pl.ds(0, x_count - 1), :, 1], sent.at[18])
    wait_bytes(mix_out.at[pl.ds(0, group - 1)], sent.at[17])


def on_device(
    query_rows,
    key_rows,
    value_rows,
    stream,
    shared_basis,
    expert_gate_up,
    expert_down,
    attn_gate,
    ffn_scale,
    ffn_gate,
    expert_ids,
    route_weights,
):
    x_count, z_count, s_count = (lax.axis_size(name) for name in ("dp", "exp", "seq"))
    y_count = s_count // 2
    tok_rows, model_width = stream.shape
    experts_here, hidden_cols, _ = expert_down.shape
    expert_total = z_count * s_count * experts_here
    rank = shared_basis.shape[1]
    head_cols = model_width // s_count
    cols = 384
    slots = 4 * CAP
    length = s_count * tok_rows
    group = x_count * y_count

    vmem = pl.BlockSpec(memory_space=pltpu.VMEM)
    anywhere = pl.BlockSpec(memory_space=pl.ANY)
    bf16, f32 = jnp.bfloat16, jnp.float32
    wide = rank + LANES
    dma = pltpu.SemaphoreType.DMA
    return pl.pallas_call(
        block_kernel,
        out_shape=jax.ShapeDtypeStruct((tok_rows, model_width), bf16),
        in_specs=[anywhere] * 6 + [vmem] * 6,
        out_specs=vmem,
        scratch_shapes=[
            pltpu.VMEM((2, length, head_cols), bf16),
            pltpu.VMEM((s_count, 2, tok_rows, head_cols), bf16),
            pltpu.VMEM((tok_rows, model_width), bf16),
            pltpu.VMEM((s_count, tok_rows, head_cols), bf16),
            pltpu.VMEM((tok_rows, model_width), bf16),
            pltpu.VMEM((2 * tok_rows, head_cols), bf16),
            pltpu.VMEM((2, tok_rows, wide), f32),
            pltpu.VMEM((y_count, tok_rows, wide), f32),
            pltpu.VMEM((y_count, tok_rows, wide), bf16),
            pltpu.VMEM((y_count, tok_rows, wide), bf16),
            pltpu.VMEM((y_count - 1, tok_rows, wide), bf16),
            pltpu.VMEM((y_count - 1, tok_rows, wide), bf16),
            pltpu.VMEM((y_count - 1, z_count * slots, rank), bf16),
            pltpu.VMEM((y_count, z_count * slots, rank), bf16),
            pltpu.VMEM((x_count, y_count, 2 * slots, rank), bf16),
            pltpu.VMEM(
                (2, z_count, 2, experts_here, rank // z_count, 2 * hidden_cols), bf16
            ),
            pltpu.VMEM((x_count, y_count, 2, group * slots, hidden_cols), bf16),
            pltpu.VMEM((2, z_count, y_count, experts_here * hidden_cols, cols), bf16),
            pltpu.VMEM((group, z_count * y_count * slots, cols), bf16),
            pltpu.VMEM((group, tok_rows, cols), bf16),
            pltpu.VMEM((group, tok_rows, cols), bf16),
            pltpu.VMEM((8, tok_rows), f32),
            pltpu.VMEM((y_count, 8, tok_rows), f32),
            pltpu.VMEM((x_count, y_count, 8, tok_rows), f32),
            dma,
            dma((s_count,)),
            dma((2, 2)),
            dma,
            dma((2,)),
            dma,
            dma((z_count,)),
            dma,
            dma,
            dma((z_count,)),
            dma,
            dma((y_count,)),
            dma,
            dma,
            dma((y_count,)),
            dma,
            dma((2,)),
            dma((y_count,)),
            dma((x_count,)),
            dma,
            dma((19,)),
        ],
        compiler_params=pltpu.CompilerParams(
            collective_id=0, has_side_effects=True, vmem_limit_bytes=62 * 1024 * 1024
        ),
        name="block",
    )(
        query_rows,
        key_rows,
        value_rows,
        stream,
        expert_down,
        expert_gate_up,
        shared_basis,
        attn_gate,
        ffn_scale,
        ffn_gate,
        expert_ids.T,
        route_weights.T,
    )


def solution(mesh):
    in_specs = (
        P(("dp", "exp", "seq"), None),
        P(("dp", "exp", "seq"), None),
        P(("dp", "exp", "seq"), None),
        P(("dp", "exp", "seq"), None),
        P("seq", None),
        P(("exp", "seq"), None, None),
        P(("exp", "seq"), None, None),
        P(("dp", "exp"), None),
        P(("dp", "exp"), None),
        P(("dp", "exp"), None),
        P(("dp", "exp", "seq"), None),
        P(("dp", "exp", "seq"), None),
    )
    out_specs = P(("dp", "exp", "seq"), None)
    return jax.shard_map(
        on_device, mesh=mesh, in_specs=in_specs, out_specs=out_specs, check_vma=False
    )
```

```python
import functools
import math

import jax
import jax.numpy as jnp
from jax import lax
from jax.experimental import pallas as pl
from jax.experimental.pallas import tpu as pltpu
from jax.sharding import PartitionSpec as P

HEAD_DIM = 128
LANES = 128
MESH = pl.DeviceIdType.MESH
epsilon = 1e-06
CAP = 4


def block_kernel(
    query_ref,
    key_ref,
    value_ref,
    stream_ref,
    down_ref,
    gate_up_ref,
    basis_ref,
    attn_gate_ref,
    ffn_scale_ref,
    ffn_gate_ref,
    ids_ref,
    route_ref,
    output_ref,
    kv_in,
    qs_in,
    stream_own,
    att_out,
    attended,
    modulated,
    partial,
    own_part,
    core_send,
    core_recv,
    part_send,
    part_recv,
    out_rows,
    near_rows,
    slot_rows,
    gate_up,
    hidden_all,
    weights,
    slot_out,
    mix_out,
    mix_in,
    info_own,
    info_y,
    info_x,
    slot_weight,
    picks,
    kv_sem,
    qs_sem,
    batch_sem,
    own_sem,
    info_sem,
    near_w_sem,
    ring_sem,
    pair_w_sem,
    near_g_sem,
    ring_g_sem,
    pair_g_sem,
    core_sem,
    part_sem,
    att_sem,
    near_sem,
    slot_sem,
    hid_sem,
    hid_y_sem,
    hid_x_sem,
    mix_sem,
    sent,
):
    x_count, z_count, s_count = (lax.axis_size(name) for name in ("dp", "exp", "seq"))
    y_count = s_count // 2
    x, z, s = (lax.axis_index(name) for name in ("dp", "exp", "seq"))
    y, c = s // 2, s % 2
    other_c = 1 - c
    pair = 2 * y + other_c
    tok_rows, model_width = attended.shape
    head_cols = kv_in.shape[2]
    heads_here = head_cols // HEAD_DIM
    cols = weights.shape[4]
    rank = near_rows.shape[2]
    slots = 4 * CAP
    quarter = model_width // x_count

    def remote(src, dst, send_sem, recv_sem, device):
        return pltpu.make_async_remote_copy(
            src_ref=src,
            dst_ref=dst,
            send_sem=send_sem,
            recv_sem=recv_sem,
            device_id=device,
            device_id_type=MESH,
        )

    def wait_bytes(ref, sem):
        pltpu.make_async_copy(ref, ref, sem).wait()

    def first_column(y_to):
        return pl.multiple_of(x * quarter + (y_to // 2) * head_cols + (y_to % 2) * 256, LANES)

    def near_order(step):
        return step + step // 2 - 2 * (step // 3)

    barrier = pltpu.get_barrier_semaphore()

    def greet(device):
        pl.semaphore_signal(barrier, inc=1, device_id=device, device_id_type=MESH)

    def greet_seq(step, carry):
        greet({"seq": lax.rem(s + step, s_count)})
        return carry

    def greet_z(step, carry):
        greet({"exp": lax.rem(z + step, z_count)})
        return carry

    def greet_x(step, carry):
        greet({"dp": lax.rem(x + step, x_count)})

        def greet_xy(y_step, inner):
            greet(
                {
                    "dp": lax.rem(x + step, x_count),
                    "seq": 2 * lax.rem(y + y_step, y_count) + c,
                }
            )
            return inner

        return lax.fori_loop(1, y_count, greet_xy, carry)

    lax.fori_loop(1, s_count, greet_seq, 0)
    lax.fori_loop(1, z_count, greet_z, 0)
    lax.fori_loop(1, x_count, greet_x, 0)

    my_rows = pl.ds(pl.multiple_of(s * tok_rows, tok_rows), tok_rows)
    my_cols = pl.ds(pl.multiple_of(s * head_cols, head_cols), head_cols)
    kv_refs = (key_ref, value_ref)
    qs_refs = (query_ref, stream_ref)
    for which in range(2):
        pltpu.make_async_copy(
            kv_refs[which].at[:, my_cols], kv_in.at[which, my_rows, :], kv_sem
        ).start()
        pltpu.make_async_copy(
            qs_refs[which].at[:, my_cols], qs_in.at[s, which], qs_sem.at[s]
        ).start()
        pltpu.make_async_copy(
            down_ref.at[which, :, pl.ds(first_column(y), cols)],
            weights.at[c, z, y, pl.ds(which * LANES, LANES), :],
            near_w_sem,
        ).start()
    pltpu.make_async_copy(stream_ref, stream_own, own_sem).start()

    rank_part = rank // z_count
    twin = z - 2 * x

    @pl.when(z // 2 == x)
    def _own_gate_up():
        part = pl.ds(pl.multiple_of(z * rank_part, rank_part), rank_part)
        pltpu.make_async_copy(
            gate_up_ref.at[:, part, :], gate_up.at[c, z, twin], near_g_sem
        ).start()

    entries = 2 * tok_rows
    experts = 4 * z_count * y_count
    ids_row = jnp.concatenate([ids_ref[0:1, :], ids_ref[1:2, :]], axis=1)
    named = lax.broadcasted_iota(jnp.int32, (experts, entries), 0) == ids_row
    entry = [lax.broadcasted_iota(jnp.int32, (entries, entries), axis) for axis in (0, 1)]
    entry = [2 * (one % tok_rows) + one // tok_rows for one in entry]
    before = jnp.where(entry[0] < entry[1], 1.0, 0.0).astype(jnp.bfloat16)
    counts = jnp.dot(
        jnp.where(named, 1.0, 0.0).astype(jnp.bfloat16), before, preferred_element_type=jnp.float32
    )
    slot_ids = (
        jnp.sum(jnp.where(named, counts, 0.0), axis=0, keepdims=True)
        + ids_row.astype(jnp.float32) * CAP
    )
    info_row = lax.broadcasted_iota(jnp.int32, info_own.shape, 0)
    info = jnp.where(info_row == 2, route_ref[0:1, :], 0.0)
    info = jnp.where(info_row == 3, route_ref[1:2, :], info)
    info = jnp.where(info_row == 0, slot_ids[:, :tok_rows], info)
    info_own[...] = jnp.where(info_row == 1, slot_ids[:, tok_rows:], info)
    pltpu.make_async_copy(info_own, info_y.at[y], info_sem.at[0]).start()

    pl.semaphore_wait(barrier, s_count - 1 + z_count - 1 + (x_count - 1) * y_count)

    def info_to_y(step, carry):
        y_to = lax.rem(y + step, y_count)
        remote(
            info_own, info_y.at[y], sent.at[0], info_sem.at[0], {"seq": 2 * y_to + c}
        ).start()
        return carry

    lax.fori_loop(1, y_count, info_to_y, 0)

    def near_first(step, carry):
        y_to = lax.rem(y + near_order(step), y_count)
        device = {"seq": 2 * y_to + c}
        for which in range(2):
            remote(
                down_ref.at[which, :, pl.ds(first_column(y_to), cols)],
                weights.at[c, z, y, pl.ds(which * LANES, LANES), :],
                sent.at[1],
                near_w_sem,
                device,
            ).start()
        return carry

    lax.fori_loop(1, y_count, near_first, 0)

    @pl.when(z // 2 == x)
    def _spread_gate_up():
        def to_z(step, carry):
            z_to = lax.rem(z + step, z_count)
            part = pl.ds(pl.multiple_of(z_to * rank_part, rank_part), rank_part)
            remote(
                gate_up_ref.at[:, part, :],
                gate_up.at[c, z_to, twin],
                sent.at[4],
                near_g_sem,
                {"exp": z_to},
            ).start()
            return carry

        lax.fori_loop(1, z_count, to_z, 0)


    def send_batch(refs, slot_of, sem, send_sem, distances):
        def one_copy(index, carry):
            s_to = 2 * lax.rem(y + distances[0] + 2 * (index % len(distances)), y_count) + (
                index // len(distances)
            )
            columns = pl.ds(pl.multiple_of(s_to * head_cols, head_cols), head_cols)
            for which in range(2):
                remote(
                    refs[which].at[:, columns], slot_of(which), send_sem, sem, {"seq": s_to}
                ).start()
            return carry

        if len(distances) == 2:
            columns = pl.ds(pl.multiple_of(pair * head_cols, head_cols), head_cols)
            for which in range(2):
                remote(
                    refs[which].at[:, columns], slot_of(which), send_sem, sem, {"seq": pair}
                ).start()
        lax.fori_loop(0, 2 * len(distances), one_copy, 0)

    batches = ((1, 3), (2,))

    def send_kv(batch):
        send_batch(
            kv_refs,
            lambda which: kv_in.at[which, my_rows, :],
            kv_sem,
            batch_sem.at[0, batch],
            batches[batch],
        )

    def send_qs(batch):
        send_batch(
            qs_refs,
            lambda which: qs_in.at[s, which],
            qs_sem.at[s],
            batch_sem.at[1, batch],
            batches[batch],
        )

    def batch_left(kind, batch):
        peers = 5 if batch == 0 else 2
        wait_bytes(qs_in.at[pl.ds(0, peers)], batch_sem.at[kind, batch])

    send_kv(0)

    always = z >= 0
    half = z_count // 2

    def pass_on(buffer, sems, left_sem, pair_left, pair_sem, block, up, down):
        held = buffer.at[c, block]

        def pass_to(z_to):
            remote(held, held, left_sem, sems.at[block], {"exp": lax.rem(z_to, z_count)}).start()

        if up is not None:

            @pl.when(up)
            def _up():
                pass_to(z + 1)

        if down is not None:

            @pl.when(down)
            def _down():
                pass_to(z + z_count - 1)

        remote(held, held, pair_left, pair_sem, {"seq": pair}).start()

    def ring_step(ring, step):
        buffer, sems = ring[0], ring[1]
        below = lax.rem(z + z_count - step, z_count)
        above = lax.rem(z + step, z_count)
        wait_bytes(buffer.at[c, below], sems.at[below])
        if step == half:
            pass_on(*ring, below, None, None)
            return
        pass_on(*ring, below, always if step < half - 1 else c == 0, None)
        wait_bytes(buffer.at[c, above], sems.at[above])
        pass_on(*ring, above, None, always if step < half - 1 else c == 1)

    gate_ring = (gate_up, ring_g_sem, sent.at[13], sent.at[14], pair_g_sem)
    down_ring = (weights, ring_sem, sent.at[7], sent.at[8], pair_w_sem)

    wait_bytes(gate_up.at[c, z], near_g_sem)
    wait_bytes(info_y, info_sem.at[0])
    pltpu.make_async_copy(info_y, info_x.at[x], info_sem.at[1]).start()

    def info_to_x(step, carry):
        remote(
            info_y,
            info_x.at[x],
            sent.at[6],
            info_sem.at[1],
            {"dp": lax.rem(x + step, x_count)},
        ).start()
        return carry

    lax.fori_loop(1, x_count, info_to_x, 0)
    pass_on(*gate_ring, z, always, always)
    send_kv(1)
    ring_step(gate_ring, 1)
    wait_bytes(weights.at[c, z], near_w_sem)
    pass_on(*down_ring, z, always, always)
    batch_left(0, 0)
    send_qs(0)
    ring_step(gate_ring, 2)
    ring_step(gate_ring, 3)

    wait_bytes(info_x, info_sem.at[1])
    group = x_count * y_count
    chip_rows = group * slots
    named_all = info_x[...].reshape(group, info_x.shape[2], tok_rows)
    place = lax.broadcasted_iota(jnp.int32, (group, slots, tok_rows), 1)
    for which in range(2):
        slot_here = (place + ((2 * x + which) * y_count + y) * slots).astype(jnp.float32)
        routed = jnp.where(
            slot_here == named_all[:, 0:1, :], named_all[:, 2:3, :], 0.0
        ) + jnp.where(slot_here == named_all[:, 1:2, :], named_all[:, 3:4, :], 0.0)
        slot_weight[which] = jnp.sum(routed, axis=2, keepdims=True).reshape(chip_rows, 1)

    def make_pick(source, carry):
        slot_iota = lax.broadcasted_iota(jnp.int32, (picks.shape[2], tok_rows), 0).astype(
            jnp.float32
        )
        named_here = info_x[source // y_count, source % y_count]
        pick = (slot_iota == named_here[0:1, :]) | (slot_iota == named_here[1:2, :])
        picks[source] = jnp.where(pick, 1.0, 0.0).T.astype(jnp.bfloat16)
        return carry

    lax.fori_loop(0, group, make_pick, 0)
    wait_bytes(kv_in, kv_sem)

    length = s_count * tok_rows
    lane = lax.broadcasted_iota(jnp.int32, (length, HEAD_DIM), 1)
    ones_column = jnp.where(lane == 0, 1.0, 0.0).astype(jnp.bfloat16)
    exponent_scale = 1.0 / (math.sqrt(HEAD_DIM) * math.log(2.0))
    gate_row = attn_gate_ref[:, my_cols].astype(jnp.float32)
    scale_row = ffn_scale_ref[:, my_cols].astype(jnp.float32)
    two = 2 * tok_rows
    tail_lane = lax.broadcasted_iota(jnp.int32, (two, LANES), 1)

    def with_tail(values, square, tail):
        high = square.astype(jnp.bfloat16).astype(jnp.float32)
        extra = jnp.where(tail == 0, high, jnp.where(tail == 1, square - high, 0.0))
        return jnp.concatenate([values, extra], axis=1)

    def add_core_part(step):
        wait_bytes(core_recv.at[step], core_sem.at[step])
        total = own_part[step] + core_recv[step].astype(jnp.float32)
        square = total[:, rank : rank + 1] + total[:, rank + 1 : rank + 2]
        return total[:, :rank], square

    def send_part(step):
        values, square = add_core_part(step)
        part_send[step - 1] = with_tail(values, square, tail_lane[:tok_rows]).astype(jnp.bfloat16)
        distance = near_order(step)
        y_to = lax.rem(y + y_count - distance, y_count)
        remote(
            part_send.at[step - 1],
            part_recv.at[step - 1],
            sent.at[10],
            part_sem,
            {"seq": 2 * y_to + c},
        ).start()

    def one_chip(step, carry):
        y_from = lax.rem(y + y_count - near_order(step), y_count)

        @pl.when(step > 1)
        def _previous():
            send_part(step - 1)

        for core in range(2):
            wait_bytes(qs_in.at[2 * y_from + core], qs_sem.at[2 * y_from + core])
        both = pl.ds(2 * y_from, 2)
        square = jnp.zeros((two, 1), jnp.float32)
        for head in range(heads_here):
            part = slice(head * HEAD_DIM, (head + 1) * HEAD_DIM)
            scores = lax.dot_general(
                qs_in[both, 0, :, part].reshape(two, HEAD_DIM),
                kv_in[0, :, part],
                (((1,), (1,)), ((), ())),
                preferred_element_type=jnp.float32,
            )
            row_max = jnp.max(scores, axis=-1, keepdims=True)
            raised = jnp.exp2((scores - row_max) * exponent_scale).astype(jnp.bfloat16)
            value_ones = jnp.concatenate([kv_in[1, :, part], ones_column], axis=1)
            mixed = jnp.dot(raised, value_ones, preferred_element_type=jnp.float32)
            mixed = (mixed[:, :HEAD_DIM] / mixed[:, HEAD_DIM : HEAD_DIM + 1]).astype(jnp.bfloat16)
            att_out[both, :, part] = mixed.reshape(2, tok_rows, HEAD_DIM)
            residual = qs_in[both, 1, :, part].reshape(two, HEAD_DIM).astype(
                jnp.float32
            ) + gate_row[:, part] * mixed.astype(jnp.float32)
            modulated[:, part] = (residual * scale_row[:, part]).astype(jnp.bfloat16)
            square = square + jnp.sum(residual * residual, axis=1, keepdims=True)
        product = jnp.dot(modulated[...], basis_ref[...], preferred_element_type=jnp.float32)
        partial[...] = with_tail(product, square, tail_lane).reshape(partial.shape)
        own_part[step] = partial[c]
        core_send[step] = partial[other_c].astype(jnp.bfloat16)
        remote(
            core_send.at[step], core_recv.at[step], sent.at[9], core_sem.at[step], {"seq": pair}
        ).start()
        return carry

    def after_chip(step, carry):
        one_chip(step, carry)

        @pl.when(step == 0)
        def _last_batch():
            ring_step(gate_ring, half)
            batch_left(0, 1)
            send_qs(1)

        @pl.when(step == 2)
        def _ring_one():
            ring_step(down_ring, 1)

        return carry

    lax.fori_loop(0, y_count, after_chip, 0)
    send_part(y_count - 1)

    def send_attended(s_to, carry):
        @pl.when(s_to == s)
        def _keep():
            pltpu.make_async_copy(att_out.at[s_to], attended.at[:, my_cols], att_sem).start()

        @pl.when(s_to != s)
        def _send():
            remote(
                att_out.at[s_to], attended.at[:, my_cols], sent.at[11], att_sem, {"seq": s_to}
            ).start()

        return carry

    values, square = add_core_part(0)
    wait_bytes(part_recv, part_sem)
    for step in range(y_count - 1):
        arrived = part_recv[step].astype(jnp.float32)
        values = values + arrived[:, :rank]
        square = square + arrived[:, rank : rank + 1] + arrived[:, rank + 1 : rank + 2]
    low_rank = (values / jnp.sqrt(square / model_width + epsilon)).astype(jnp.bfloat16)

    def pick_rows(y_to):
        row = lax.broadcasted_iota(jnp.int32, (z_count * slots, tok_rows), 0)
        slot_here = (((row // slots) * y_count + y_to) * slots + row % slots).astype(jnp.float32)
        pick = (slot_here == info_own[0:1, :]) | (slot_here == info_own[1:2, :])
        pick = jnp.where(pick, 1.0, 0.0).astype(jnp.bfloat16)
        return jnp.dot(pick, low_rank, preferred_element_type=jnp.float32).astype(jnp.bfloat16)

    chip_slots = 2 * slots

    def forward_rows(y_from):
        def to_x(x_step, inner):
            x_to = lax.rem(x + near_order(x_step), x_count)
            rows = pl.ds(pl.multiple_of(x_to * chip_slots, chip_slots), chip_slots)
            remote(
                near_rows.at[y_from, rows, :],
                slot_rows.at[x, y_from],
                sent.at[5],
                slot_sem,
                {"dp": x_to},
            ).start()
            return inner

        lax.fori_loop(1, x_count, to_x, 0)
        own = pl.ds(pl.multiple_of(x * chip_slots, chip_slots), chip_slots)
        pltpu.make_async_copy(near_rows.at[y_from, own, :], slot_rows.at[x, y_from], slot_sem).start()

    for step in range(1, y_count):
        y_to = lax.rem(y + near_order(step), y_count)
        out_rows[step - 1] = pick_rows(y_to)
        remote(
            out_rows.at[step - 1],
            near_rows.at[y],
            sent.at[12],
            near_sem.at[y],
            {"seq": 2 * y_to + c},
        ).start()


    near_rows[y] = pick_rows(y)
    forward_rows(y)
    ring_step(down_ring, 2)

    def forward_near(step, carry):
        y_from = lax.rem(y + y_count - near_order(step), y_count)
        wait_bytes(near_rows.at[y_from], near_sem.at[y_from])
        forward_rows(y_from)
        return carry

    lax.fori_loop(1, y_count, forward_near, 0)

    wait_bytes(gate_up.at[other_c], pair_g_sem)
    wait_bytes(slot_rows, slot_sem)
    expert = lax.broadcasted_iota(jnp.int32, (chip_rows, 1), 0) % slots // CAP

    for twin_here in range(2):
        rows = slot_rows[:, :, pl.ds(twin_here * slots, slots), :].reshape(chip_rows, rank)
        both_halves = jnp.zeros((chip_rows, gate_up.shape[5]), jnp.float32)
        for which in range(4):
            product = jnp.dot(
                rows,
                gate_up[which // 2, :, twin_here, which % 2].reshape(rank, gate_up.shape[5]),
                preferred_element_type=jnp.float32,
            )
            both_halves = jnp.where(expert == which, product, both_halves)
        gate, up = both_halves[:, :LANES], both_halves[:, LANES:]
        hidden = gate / (1.0 + jnp.exp(-gate)) * up * slot_weight[twin_here]
        hidden_all[x, y, twin_here] = hidden.astype(jnp.bfloat16)
        held = hidden_all.at[x, y, twin_here]

        def hidden_near(step, carry):
            if twin_here == 0:
                device = {"dp": lax.rem(x + near_order(step), x_count)}
            else:
                device = {"seq": 2 * lax.rem(y + near_order(step), y_count) + c}
            remote(held, held, sent.at[15], hid_sem.at[twin_here], device).start()
            return carry

        lax.fori_loop(1, x_count, hidden_near, 0)

    ring_step(down_ring, 3)
    wait_bytes(hidden_all.at[pl.ds(0, x_count - 1), y, 0], hid_sem.at[0])

    def hidden_to_y(step, carry):
        held = hidden_all.at[:, y, 0]
        y_to = lax.rem(y + near_order(step), y_count)
        remote(held, held, sent.at[16], hid_y_sem.at[y], {"seq": 2 * y_to + c}).start()
        return carry

    lax.fori_loop(1, y_count, hidden_to_y, 0)
    wait_bytes(hidden_all.at[x, pl.ds(0, y_count - 1), 1], hid_sem.at[1])

    def hidden_to_x(step, carry):
        held = hidden_all.at[x, :, 1]
        x_to = lax.rem(x + near_order(step), x_count)
        remote(held, held, sent.at[18], hid_x_sem.at[x], {"dp": x_to}).start()
        return carry

    lax.fori_loop(1, x_count, hidden_to_x, 0)
    lax.fori_loop(0, s_count, send_attended, 0)
    ring_step(down_ring, half)
    wait_bytes(weights.at[other_c], pair_w_sem)

    chip_expert = lax.broadcasted_iota(jnp.int32, (chip_rows, LANES), 0) % slots // CAP

    masks = [
        jnp.where(chip_expert == which, 1.0, 0.0).astype(jnp.bfloat16) for which in range(4)
    ]

    def down_block(x_from, y_from, twin_here):
        held = hidden_all[x_from, y_from, twin_here]
        z_from = 2 * x_from + twin_here
        masked = [held * mask for mask in masks]
        product = jnp.dot(
            jnp.concatenate(masked[:2], axis=1),
            weights[0, z_from, y_from],
            preferred_element_type=jnp.float32,
        ) + jnp.dot(
            jnp.concatenate(masked[2:], axis=1),
            weights[1, z_from, y_from],
            preferred_element_type=jnp.float32,
        )
        to = pl.ds(pl.multiple_of((z_from * y_count + y_from) * slots, slots), slots)
        slot_out[:, to, :] = product.astype(jnp.bfloat16).reshape(group, slots, cols)

    def down_step(step, carry):
        y_from = lax.rem(y + y_count - near_order(step), y_count)
        x_from = lax.rem(x + x_count - near_order(step), x_count)

        @pl.when(step > 0)
        def _arrive_y():
            wait_bytes(hidden_all.at[:, y_from, 0], hid_y_sem.at[y_from])

        def down_first(other, inner):
            down_block(other, y_from, 0)
            return inner

        lax.fori_loop(0, x_count, down_first, 0)

        @pl.when(step > 0)
        def _arrive_x():
            wait_bytes(hidden_all.at[x_from, :, 1], hid_x_sem.at[x_from])

        def down_second(other, inner):
            down_block(x_from, other, 1)
            return inner

        lax.fori_loop(0, y_count, down_second, 0)
        return carry

    lax.fori_loop(0, y_count, down_step, 0)

    mine = x * y_count + y

    def mix_one(step, carry):
        x_to = lax.rem(x + (step + 1) // y_count, x_count)
        y_to = lax.rem(y + step + 1, y_count)
        to = x_to * y_count + y_to
        mixed = jnp.dot(picks[to], slot_out[to], preferred_element_type=jnp.float32)
        mix_out[to] = mixed.astype(jnp.bfloat16)

        @pl.when(to == mine)
        def _keep():
            pltpu.make_async_copy(mix_out.at[to], mix_in.at[mine], mix_sem.at[mine]).start()

        @pl.when(to != mine)
        def _send():
            remote(
                mix_out.at[to],
                mix_in.at[mine],
                sent.at[17],
                mix_sem.at[mine],
                {"dp": x_to, "seq": 2 * y_to + c},
            ).start()

        return carry

    lax.fori_loop(0, group, mix_one, 0)

    wait_bytes(stream_own, own_sem)
    wait_bytes(attended, att_sem)
    for block in range(s_count):
        part = slice(block * head_cols, (block + 1) * head_cols)
        for part_of in (2 * block, 2 * block + 1):
            wait_bytes(mix_in.at[part_of], mix_sem.at[part_of])
        mixed = jnp.concatenate([mix_in[2 * block], mix_in[2 * block + 1, :, LANES:]], axis=1)
        residual = stream_own[:, part].astype(jnp.float32) + attn_gate_ref[:, part].astype(
            jnp.float32
        ) * attended[:, part].astype(jnp.float32)
        output_ref[:, part] = (
            residual + ffn_gate_ref[:, part].astype(jnp.float32) * mixed.astype(jnp.float32)
        ).astype(jnp.bfloat16)

    wait_bytes(info_y.at[pl.ds(0, y_count - 1)], sent.at[0])
    wait_bytes(weights.at[0, 0, pl.ds(0, y_count - 1)], sent.at[1])
    batch_left(1, 0)
    batch_left(1, 1)

    @pl.when(z // 2 == x)
    def _spread_done():
        wait_bytes(gate_up.at[0, pl.ds(0, z_count - 1), 0], sent.at[4])

    wait_bytes(slot_rows.at[pl.ds(0, x_count - 1)], sent.at[5])
    wait_bytes(info_x.at[pl.ds(0, x_count - 1)], sent.at[6])
    wait_bytes(weights.at[0, pl.ds(0, z_count - 1)], sent.at[7])
    wait_bytes(weights.at[0], sent.at[8])
    wait_bytes(core_send, sent.at[9])
    wait_bytes(part_send, sent.at[10])
    wait_bytes(att_out.at[pl.ds(0, s_count - 1)], sent.at[11])
    wait_bytes(out_rows, sent.at[12])
    wait_bytes(gate_up.at[0, pl.ds(0, z_count - 1)], sent.at[13])
    wait_bytes(gate_up.at[0], sent.at[14])
    wait_bytes(hidden_all.at[pl.ds(0, 2), pl.ds(0, y_count - 1), 0], sent.at[15])
    wait_bytes(hidden_all.at[:, pl.ds(0, y_count - 1), 0], sent.at[16])
    wait_bytes(hidden_all.at[pl.ds(0, x_count - 1), :, 1], sent.at[18])
    wait_bytes(mix_out.at[pl.ds(0, group - 1)], sent.at[17])


def on_device(
    query_rows,
    key_rows,
    value_rows,
    stream,
    shared_basis,
    expert_gate_up,
    expert_down,
    attn_gate,
    ffn_scale,
    ffn_gate,
    expert_ids,
    route_weights,
):
    x_count, z_count, s_count = (lax.axis_size(name) for name in ("dp", "exp", "seq"))
    y_count = s_count // 2
    tok_rows, model_width = stream.shape
    experts_here, hidden_cols, _ = expert_down.shape
    expert_total = z_count * s_count * experts_here
    rank = shared_basis.shape[1]
    head_cols = model_width // s_count
    cols = 384
    slots = 4 * CAP
    length = s_count * tok_rows
    group = x_count * y_count

    vmem = pl.BlockSpec(memory_space=pltpu.VMEM)
    anywhere = pl.BlockSpec(memory_space=pl.ANY)
    bf16, f32 = jnp.bfloat16, jnp.float32
    wide = rank + LANES
    dma = pltpu.SemaphoreType.DMA
    return pl.pallas_call(
        block_kernel,
        out_shape=jax.ShapeDtypeStruct((tok_rows, model_width), bf16),
        in_specs=[anywhere] * 6 + [vmem] * 6,
        out_specs=vmem,
        scratch_shapes=[
            pltpu.VMEM((2, length, head_cols), bf16),
            pltpu.VMEM((s_count, 2, tok_rows, head_cols), bf16),
            pltpu.VMEM((tok_rows, model_width), bf16),
            pltpu.VMEM((s_count, tok_rows, head_cols), bf16),
            pltpu.VMEM((tok_rows, model_width), bf16),
            pltpu.VMEM((2 * tok_rows, head_cols), bf16),
            pltpu.VMEM((2, tok_rows, wide), f32),
            pltpu.VMEM((y_count, tok_rows, wide), f32),
            pltpu.VMEM((y_count, tok_rows, wide), bf16),
            pltpu.VMEM((y_count, tok_rows, wide), bf16),
            pltpu.VMEM((y_count - 1, tok_rows, wide), bf16),
            pltpu.VMEM((y_count - 1, tok_rows, wide), bf16),
            pltpu.VMEM((y_count - 1, z_count * slots, rank), bf16),
            pltpu.VMEM((y_count, z_count * slots, rank), bf16),
            pltpu.VMEM((x_count, y_count, 2 * slots, rank), bf16),
            pltpu.VMEM(
                (2, z_count, 2, experts_here, rank // z_count, 2 * hidden_cols), bf16
            ),
            pltpu.VMEM((x_count, y_count, 2, group * slots, hidden_cols), bf16),
            pltpu.VMEM((2, z_count, y_count, experts_here * hidden_cols, cols), bf16),
            pltpu.VMEM((group, z_count * y_count * slots, cols), bf16),
            pltpu.VMEM((group, tok_rows, cols), bf16),
            pltpu.VMEM((group, tok_rows, cols), bf16),
            pltpu.VMEM((8, tok_rows), f32),
            pltpu.VMEM((y_count, 8, tok_rows), f32),
            pltpu.VMEM((x_count, y_count, 8, tok_rows), f32),
            pltpu.VMEM((2, group * slots, 1), f32),
            pltpu.VMEM((group, tok_rows, group * 2 * slots), bf16),
            dma,
            dma((s_count,)),
            dma((2, 2)),
            dma,
            dma((2,)),
            dma,
            dma((z_count,)),
            dma,
            dma,
            dma((z_count,)),
            dma,
            dma((y_count,)),
            dma,
            dma,
            dma((y_count,)),
            dma,
            dma((2,)),
            dma((y_count,)),
            dma((x_count,)),
            dma((group,)),
            dma((19,)),
        ],
        compiler_params=pltpu.CompilerParams(
            collective_id=0, has_side_effects=True, vmem_limit_bytes=62 * 1024 * 1024
        ),
        name="block",
    )(
        query_rows,
        key_rows,
        value_rows,
        stream,
        expert_down,
        expert_gate_up,
        shared_basis,
        attn_gate,
        ffn_scale,
        ffn_gate,
        expert_ids.T,
        route_weights.T,
    )


def solution(mesh):
    in_specs = (
        P(("dp", "exp", "seq"), None),
        P(("dp", "exp", "seq"), None),
        P(("dp", "exp", "seq"), None),
        P(("dp", "exp", "seq"), None),
        P("seq", None),
        P(("exp", "seq"), None, None),
        P(("exp", "seq"), None, None),
        P(("dp", "exp"), None),
        P(("dp", "exp"), None),
        P(("dp", "exp"), None),
        P(("dp", "exp", "seq"), None),
        P(("dp", "exp", "seq"), None),
    )
    out_specs = P(("dp", "exp", "seq"), None)
    return jax.shard_map(
        on_device, mesh=mesh, in_specs=in_specs, out_specs=out_specs, check_vma=False
    )
```

```python
import functools
import math

import jax
import jax.numpy as jnp
from jax import lax
from jax.experimental import pallas as pl
from jax.experimental.pallas import tpu as pltpu
from jax.sharding import PartitionSpec as P

HEAD_DIM = 128
LANES = 128
MESH = pl.DeviceIdType.MESH
epsilon = 1e-06
CAP = 4


def block_kernel(
    query_ref,
    key_ref,
    value_ref,
    stream_ref,
    down_ref,
    gate_up_ref,
    basis_ref,
    attn_gate_ref,
    ffn_scale_ref,
    ffn_gate_ref,
    ids_ref,
    route_ref,
    output_ref,
    kv_in,
    qs_in,
    stream_own,
    att_out,
    attended,
    modulated,
    partial,
    own_part,
    core_send,
    core_recv,
    part_send,
    part_recv,
    out_rows,
    near_rows,
    slot_rows,
    gate_up,
    hidden_all,
    weights,
    slot_out,
    mix_out,
    mix_in,
    info_own,
    info_y,
    info_x,
    slot_weight,
    picks,
    kv_sem,
    qs_sem,
    batch_sem,
    own_sem,
    info_sem,
    near_w_sem,
    ring_sem,
    pair_w_sem,
    near_g_sem,
    ring_g_sem,
    pair_g_sem,
    core_sem,
    part_sem,
    att_sem,
    near_sem,
    slot_sem,
    hid_sem,
    hid_y_sem,
    hid_x_sem,
    mix_sem,
    sent,
):
    x_count, z_count, s_count = (lax.axis_size(name) for name in ("dp", "exp", "seq"))
    y_count = s_count // 2
    x, z, s = (lax.axis_index(name) for name in ("dp", "exp", "seq"))
    y, c = s // 2, s % 2
    other_c = 1 - c
    pair = 2 * y + other_c
    tok_rows, model_width = attended.shape
    head_cols = kv_in.shape[2]
    heads_here = head_cols // HEAD_DIM
    cols = weights.shape[4]
    rank = near_rows.shape[2]
    slots = 4 * CAP
    quarter = model_width // x_count

    def remote(src, dst, send_sem, recv_sem, device):
        return pltpu.make_async_remote_copy(
            src_ref=src,
            dst_ref=dst,
            send_sem=send_sem,
            recv_sem=recv_sem,
            device_id=device,
            device_id_type=MESH,
        )

    def wait_bytes(ref, sem):
        pltpu.make_async_copy(ref, ref, sem).wait()

    def first_column(y_to):
        return pl.multiple_of(x * quarter + (y_to // 2) * head_cols + (y_to % 2) * 256, LANES)

    def near_order(step):
        return step + step // 2 - 2 * (step // 3)

    barrier = pltpu.get_barrier_semaphore()

    def greet(device):
        pl.semaphore_signal(barrier, inc=1, device_id=device, device_id_type=MESH)

    def greet_seq(step, carry):
        greet({"seq": lax.rem(s + step, s_count)})
        return carry

    def greet_z(step, carry):
        greet({"exp": lax.rem(z + step, z_count)})
        return carry

    def greet_x(step, carry):
        greet({"dp": lax.rem(x + step, x_count)})

        def greet_xy(y_step, inner):
            greet(
                {
                    "dp": lax.rem(x + step, x_count),
                    "seq": 2 * lax.rem(y + y_step, y_count) + c,
                }
            )
            return inner

        return lax.fori_loop(1, y_count, greet_xy, carry)

    lax.fori_loop(1, s_count, greet_seq, 0)
    lax.fori_loop(1, z_count, greet_z, 0)
    lax.fori_loop(1, x_count, greet_x, 0)

    my_rows = pl.ds(pl.multiple_of(s * tok_rows, tok_rows), tok_rows)
    my_cols = pl.ds(pl.multiple_of(s * head_cols, head_cols), head_cols)
    kv_refs = (key_ref, value_ref)
    qs_refs = (query_ref, stream_ref)
    for which in range(2):
        pltpu.make_async_copy(
            kv_refs[which].at[:, my_cols], kv_in.at[which, my_rows, :], kv_sem
        ).start()
        pltpu.make_async_copy(
            qs_refs[which].at[:, my_cols], qs_in.at[s, which], qs_sem.at[s]
        ).start()
        pltpu.make_async_copy(
            down_ref.at[which, :, pl.ds(first_column(y), cols)],
            weights.at[c, z, y, pl.ds(which * LANES, LANES), :],
            near_w_sem,
        ).start()
    pltpu.make_async_copy(stream_ref, stream_own, own_sem).start()

    rank_part = rank // z_count
    twin = z - 2 * x

    @pl.when(z // 2 == x)
    def _own_gate_up():
        part = pl.ds(pl.multiple_of(z * rank_part, rank_part), rank_part)
        pltpu.make_async_copy(
            gate_up_ref.at[:, part, :], gate_up.at[c, z, twin], near_g_sem
        ).start()

    entries = 2 * tok_rows
    experts = 4 * z_count * y_count
    ids_row = jnp.concatenate([ids_ref[0:1, :], ids_ref[1:2, :]], axis=1)
    named = lax.broadcasted_iota(jnp.int32, (experts, entries), 0) == ids_row
    entry = [lax.broadcasted_iota(jnp.int32, (entries, entries), axis) for axis in (0, 1)]
    entry = [2 * (one % tok_rows) + one // tok_rows for one in entry]
    before = jnp.where(entry[0] < entry[1], 1.0, 0.0).astype(jnp.bfloat16)
    counts = jnp.dot(
        jnp.where(named, 1.0, 0.0).astype(jnp.bfloat16), before, preferred_element_type=jnp.float32
    )
    slot_ids = (
        jnp.sum(jnp.where(named, counts, 0.0), axis=0, keepdims=True)
        + ids_row.astype(jnp.float32) * CAP
    )
    info_row = lax.broadcasted_iota(jnp.int32, info_own.shape, 0)
    info = jnp.where(info_row == 2, route_ref[0:1, :], 0.0)
    info = jnp.where(info_row == 3, route_ref[1:2, :], info)
    info = jnp.where(info_row == 0, slot_ids[:, :tok_rows], info)
    info_own[...] = jnp.where(info_row == 1, slot_ids[:, tok_rows:], info)
    pltpu.make_async_copy(info_own, info_y.at[y], info_sem.at[0]).start()

    pl.semaphore_wait(barrier, s_count - 1 + z_count - 1 + (x_count - 1) * y_count)

    def info_to_y(step, carry):
        y_to = lax.rem(y + step, y_count)
        remote(
            info_own, info_y.at[y], sent.at[0], info_sem.at[0], {"seq": 2 * y_to + c}
        ).start()
        return carry

    lax.fori_loop(1, y_count, info_to_y, 0)

    def near_first(step, carry):
        y_to = lax.rem(y + near_order(step), y_count)
        device = {"seq": 2 * y_to + c}
        for which in range(2):
            remote(
                down_ref.at[which, :, pl.ds(first_column(y_to), cols)],
                weights.at[c, z, y, pl.ds(which * LANES, LANES), :],
                sent.at[1],
                near_w_sem,
                device,
            ).start()
        return carry

    lax.fori_loop(1, y_count, near_first, 0)

    @pl.when(z // 2 == x)
    def _spread_gate_up():
        def to_z(step, carry):
            z_to = lax.rem(z + step, z_count)
            part = pl.ds(pl.multiple_of(z_to * rank_part, rank_part), rank_part)
            remote(
                gate_up_ref.at[:, part, :],
                gate_up.at[c, z_to, twin],
                sent.at[4],
                near_g_sem,
                {"exp": z_to},
            ).start()
            return carry

        lax.fori_loop(1, z_count, to_z, 0)


    def send_batch(refs, slot_of, sem, send_sem, distances):
        def one_copy(index, carry):
            s_to = 2 * lax.rem(y + distances[0] + 2 * (index % len(distances)), y_count) + (
                index // len(distances)
            )
            columns = pl.ds(pl.multiple_of(s_to * head_cols, head_cols), head_cols)
            for which in range(2):
                remote(
                    refs[which].at[:, columns], slot_of(which), send_sem, sem, {"seq": s_to}
                ).start()
            return carry

        if len(distances) == 2:
            columns = pl.ds(pl.multiple_of(pair * head_cols, head_cols), head_cols)
            for which in range(2):
                remote(
                    refs[which].at[:, columns], slot_of(which), send_sem, sem, {"seq": pair}
                ).start()
        lax.fori_loop(0, 2 * len(distances), one_copy, 0)

    batches = ((1, 3), (2,))

    def send_kv(batch):
        send_batch(
            kv_refs,
            lambda which: kv_in.at[which, my_rows, :],
            kv_sem,
            batch_sem.at[0, batch],
            batches[batch],
        )

    def send_qs(batch):
        send_batch(
            qs_refs,
            lambda which: qs_in.at[s, which],
            qs_sem.at[s],
            batch_sem.at[1, batch],
            batches[batch],
        )

    def batch_left(kind, batch):
        peers = 5 if batch == 0 else 2
        wait_bytes(qs_in.at[pl.ds(0, peers)], batch_sem.at[kind, batch])

    send_kv(0)

    always = z >= 0
    half = z_count // 2

    def pass_on(buffer, sems, left_sem, pair_left, pair_sem, block, up, down):
        held = buffer.at[c, block]

        def pass_to(z_to):
            remote(held, held, left_sem, sems.at[block], {"exp": lax.rem(z_to, z_count)}).start()

        if up is not None:

            @pl.when(up)
            def _up():
                pass_to(z + 1)

        if down is not None:

            @pl.when(down)
            def _down():
                pass_to(z + z_count - 1)

        remote(held, held, pair_left, pair_sem, {"seq": pair}).start()

    def ring_step(ring, step):
        buffer, sems = ring[0], ring[1]
        below = lax.rem(z + z_count - step, z_count)
        above = lax.rem(z + step, z_count)
        wait_bytes(buffer.at[c, below], sems.at[below])
        if step == half:
            pass_on(*ring, below, None, None)
            return
        pass_on(*ring, below, always if step < half - 1 else c == 0, None)
        wait_bytes(buffer.at[c, above], sems.at[above])
        pass_on(*ring, above, None, always if step < half - 1 else c == 1)

    gate_ring = (gate_up, ring_g_sem, sent.at[13], sent.at[14], pair_g_sem)
    down_ring = (weights, ring_sem, sent.at[7], sent.at[8], pair_w_sem)

    wait_bytes(gate_up.at[c, z], near_g_sem)
    wait_bytes(info_y, info_sem.at[0])
    pltpu.make_async_copy(info_y, info_x.at[x], info_sem.at[1]).start()

    def info_to_x(step, carry):
        remote(
            info_y,
            info_x.at[x],
            sent.at[6],
            info_sem.at[1],
            {"dp": lax.rem(x + step, x_count)},
        ).start()
        return carry

    lax.fori_loop(1, x_count, info_to_x, 0)
    pass_on(*gate_ring, z, always, always)
    send_kv(1)
    ring_step(gate_ring, 1)
    wait_bytes(weights.at[c, z], near_w_sem)
    pass_on(*down_ring, z, always, always)
    batch_left(0, 0)
    send_qs(0)
    ring_step(gate_ring, 2)
    ring_step(gate_ring, 3)
    batch_left(0, 1)
    send_qs(1)

    wait_bytes(info_x, info_sem.at[1])
    group = x_count * y_count
    chip_rows = group * slots
    named_all = info_x[...].reshape(group, info_x.shape[2], tok_rows)
    place = lax.broadcasted_iota(jnp.int32, (group, slots, tok_rows), 1)
    for which in range(2):
        slot_here = (place + ((2 * x + which) * y_count + y) * slots).astype(jnp.float32)
        routed = jnp.where(
            slot_here == named_all[:, 0:1, :], named_all[:, 2:3, :], 0.0
        ) + jnp.where(slot_here == named_all[:, 1:2, :], named_all[:, 3:4, :], 0.0)
        slot_weight[which] = jnp.sum(routed, axis=2, keepdims=True).reshape(chip_rows, 1)

    def make_pick(source, carry):
        slot_iota = lax.broadcasted_iota(jnp.int32, (picks.shape[2], tok_rows), 0).astype(
            jnp.float32
        )
        named_here = info_x[source // y_count, source % y_count]
        pick = (slot_iota == named_here[0:1, :]) | (slot_iota == named_here[1:2, :])
        picks[source] = jnp.where(pick, 1.0, 0.0).T.astype(jnp.bfloat16)
        return carry

    lax.fori_loop(0, group, make_pick, 0)
    wait_bytes(kv_in, kv_sem)

    length = s_count * tok_rows
    lane = lax.broadcasted_iota(jnp.int32, (length, HEAD_DIM), 1)
    ones_column = jnp.where(lane == 0, 1.0, 0.0).astype(jnp.bfloat16)
    exponent_scale = 1.0 / (math.sqrt(HEAD_DIM) * math.log(2.0))
    gate_row = attn_gate_ref[:, my_cols].astype(jnp.float32)
    scale_row = ffn_scale_ref[:, my_cols].astype(jnp.float32)
    two = 2 * tok_rows
    tail_lane = lax.broadcasted_iota(jnp.int32, (two, LANES), 1)

    def with_tail(values, square, tail):
        high = square.astype(jnp.bfloat16).astype(jnp.float32)
        extra = jnp.where(tail == 0, high, jnp.where(tail == 1, square - high, 0.0))
        return jnp.concatenate([values, extra], axis=1)

    def add_core_part(step):
        wait_bytes(core_recv.at[step], core_sem.at[step])
        total = own_part[step] + core_recv[step].astype(jnp.float32)
        square = total[:, rank : rank + 1] + total[:, rank + 1 : rank + 2]
        return total[:, :rank], square

    def send_part(step):
        values, square = add_core_part(step)
        part_send[step - 1] = with_tail(values, square, tail_lane[:tok_rows]).astype(jnp.bfloat16)
        distance = near_order(step)
        y_to = lax.rem(y + y_count - distance, y_count)
        remote(
            part_send.at[step - 1],
            part_recv.at[step - 1],
            sent.at[10],
            part_sem,
            {"seq": 2 * y_to + c},
        ).start()

    def one_chip(step, carry):
        y_from = lax.rem(y + y_count - near_order(step), y_count)

        @pl.when(step > 1)
        def _previous():
            send_part(step - 1)

        for core in range(2):
            wait_bytes(qs_in.at[2 * y_from + core], qs_sem.at[2 * y_from + core])
        both = pl.ds(2 * y_from, 2)
        square = jnp.zeros((two, 1), jnp.float32)
        for head in range(heads_here):
            part = slice(head * HEAD_DIM, (head + 1) * HEAD_DIM)
            scores = lax.dot_general(
                qs_in[both, 0, :, part].reshape(two, HEAD_DIM),
                kv_in[0, :, part],
                (((1,), (1,)), ((), ())),
                preferred_element_type=jnp.float32,
            )
            row_max = jnp.max(scores, axis=-1, keepdims=True)
            raised = jnp.exp2((scores - row_max) * exponent_scale).astype(jnp.bfloat16)
            value_ones = jnp.concatenate([kv_in[1, :, part], ones_column], axis=1)
            mixed = jnp.dot(raised, value_ones, preferred_element_type=jnp.float32)
            mixed = (mixed[:, :HEAD_DIM] / mixed[:, HEAD_DIM : HEAD_DIM + 1]).astype(jnp.bfloat16)
            att_out[both, :, part] = mixed.reshape(2, tok_rows, HEAD_DIM)
            residual = qs_in[both, 1, :, part].reshape(two, HEAD_DIM).astype(
                jnp.float32
            ) + gate_row[:, part] * mixed.astype(jnp.float32)
            modulated[:, part] = (residual * scale_row[:, part]).astype(jnp.bfloat16)
            square = square + jnp.sum(residual * residual, axis=1, keepdims=True)
        product = jnp.dot(modulated[...], basis_ref[...], preferred_element_type=jnp.float32)
        partial[...] = with_tail(product, square, tail_lane).reshape(partial.shape)
        own_part[step] = partial[c]
        core_send[step] = partial[other_c].astype(jnp.bfloat16)
        remote(
            core_send.at[step], core_recv.at[step], sent.at[9], core_sem.at[step], {"seq": pair}
        ).start()
        return carry

    def after_chip(step, carry):
        one_chip(step, carry)

        @pl.when(step == 0)
        def _last_batch():
            ring_step(gate_ring, half)

        @pl.when(step == 2)
        def _ring_one():
            ring_step(down_ring, 1)

        return carry

    lax.fori_loop(0, y_count, after_chip, 0)
    send_part(y_count - 1)

    def send_attended(index, carry):
        s_to = lax.rem(s + index, s_count)

        @pl.when(s_to == s)
        def _keep():
            pltpu.make_async_copy(att_out.at[s_to], attended.at[:, my_cols], att_sem).start()

        @pl.when(s_to != s)
        def _send():
            remote(
                att_out.at[s_to], attended.at[:, my_cols], sent.at[11], att_sem, {"seq": s_to}
            ).start()

        return carry

    values, square = add_core_part(0)
    wait_bytes(part_recv, part_sem)
    for step in range(y_count - 1):
        arrived = part_recv[step].astype(jnp.float32)
        values = values + arrived[:, :rank]
        square = square + arrived[:, rank : rank + 1] + arrived[:, rank + 1 : rank + 2]
    low_rank = (values / jnp.sqrt(square / model_width + epsilon)).astype(jnp.bfloat16)

    def pick_rows(y_to):
        row = lax.broadcasted_iota(jnp.int32, (z_count * slots, tok_rows), 0)
        slot_here = (((row // slots) * y_count + y_to) * slots + row % slots).astype(jnp.float32)
        pick = (slot_here == info_own[0:1, :]) | (slot_here == info_own[1:2, :])
        pick = jnp.where(pick, 1.0, 0.0).astype(jnp.bfloat16)
        return jnp.dot(pick, low_rank, preferred_element_type=jnp.float32).astype(jnp.bfloat16)

    chip_slots = 2 * slots

    def forward_rows(y_from):
        def to_x(x_step, inner):
            x_to = lax.rem(x + near_order(x_step), x_count)
            rows = pl.ds(pl.multiple_of(x_to * chip_slots, chip_slots), chip_slots)
            remote(
                near_rows.at[y_from, rows, :],
                slot_rows.at[x, y_from],
                sent.at[5],
                slot_sem,
                {"dp": x_to},
            ).start()
            return inner

        lax.fori_loop(1, x_count, to_x, 0)
        own = pl.ds(pl.multiple_of(x * chip_slots, chip_slots), chip_slots)
        pltpu.make_async_copy(near_rows.at[y_from, own, :], slot_rows.at[x, y_from], slot_sem).start()

    for step in range(1, y_count):
        y_to = lax.rem(y + near_order(step), y_count)
        out_rows[step - 1] = pick_rows(y_to)
        remote(
            out_rows.at[step - 1],
            near_rows.at[y],
            sent.at[12],
            near_sem.at[y],
            {"seq": 2 * y_to + c},
        ).start()


    near_rows[y] = pick_rows(y)
    forward_rows(y)
    ring_step(down_ring, 2)

    def forward_near(step, carry):
        y_from = lax.rem(y + y_count - near_order(step), y_count)
        wait_bytes(near_rows.at[y_from], near_sem.at[y_from])
        forward_rows(y_from)
        return lax.fori_loop(2 * step, 2 * step + 2, send_attended, carry)

    lax.fori_loop(0, 2, send_attended, 0)
    lax.fori_loop(1, y_count, forward_near, 0)

    wait_bytes(gate_up.at[other_c], pair_g_sem)
    wait_bytes(slot_rows, slot_sem)
    expert = lax.broadcasted_iota(jnp.int32, (chip_rows, 1), 0) % slots // CAP

    for twin_here in range(2):
        rows = slot_rows[:, :, pl.ds(twin_here * slots, slots), :].reshape(chip_rows, rank)
        both_halves = jnp.zeros((chip_rows, gate_up.shape[5]), jnp.float32)
        for which in range(4):
            product = jnp.dot(
                rows,
                gate_up[which // 2, :, twin_here, which % 2].reshape(rank, gate_up.shape[5]),
                preferred_element_type=jnp.float32,
            )
            both_halves = jnp.where(expert == which, product, both_halves)
        gate, up = both_halves[:, :LANES], both_halves[:, LANES:]
        hidden = gate / (1.0 + jnp.exp(-gate)) * up * slot_weight[twin_here]
        hidden_all[x, y, twin_here] = hidden.astype(jnp.bfloat16)
        held = hidden_all.at[x, y, twin_here]

        def hidden_near(step, carry):
            if twin_here == 0:
                device = {"dp": lax.rem(x + near_order(step), x_count)}
            else:
                device = {"seq": 2 * lax.rem(y + near_order(step), y_count) + c}
            remote(held, held, sent.at[15], hid_sem.at[twin_here], device).start()
            return carry

        lax.fori_loop(1, x_count, hidden_near, 0)

    ring_step(down_ring, 3)
    wait_bytes(hidden_all.at[pl.ds(0, x_count - 1), y, 0], hid_sem.at[0])

    def hidden_to_y(step, carry):
        held = hidden_all.at[:, y, 0]
        y_to = lax.rem(y + near_order(step), y_count)
        remote(held, held, sent.at[16], hid_y_sem.at[y], {"seq": 2 * y_to + c}).start()
        return carry

    lax.fori_loop(1, y_count, hidden_to_y, 0)
    wait_bytes(hidden_all.at[x, pl.ds(0, y_count - 1), 1], hid_sem.at[1])

    def hidden_to_x(step, carry):
        held = hidden_all.at[x, :, 1]
        x_to = lax.rem(x + near_order(step), x_count)
        remote(held, held, sent.at[18], hid_x_sem.at[x], {"dp": x_to}).start()
        return carry

    lax.fori_loop(1, x_count, hidden_to_x, 0)
    ring_step(down_ring, half)
    wait_bytes(weights.at[other_c], pair_w_sem)

    chip_expert = lax.broadcasted_iota(jnp.int32, (chip_rows, LANES), 0) % slots // CAP

    masks = [
        jnp.where(chip_expert == which, 1.0, 0.0).astype(jnp.bfloat16) for which in range(4)
    ]

    def down_block(x_from, y_from, twin_here):
        held = hidden_all[x_from, y_from, twin_here]
        z_from = 2 * x_from + twin_here
        masked = [held * mask for mask in masks]
        product = jnp.dot(
            jnp.concatenate(masked[:2], axis=1),
            weights[0, z_from, y_from],
            preferred_element_type=jnp.float32,
        ) + jnp.dot(
            jnp.concatenate(masked[2:], axis=1),
            weights[1, z_from, y_from],
            preferred_element_type=jnp.float32,
        )
        to = pl.ds(pl.multiple_of((z_from * y_count + y_from) * slots, slots), slots)
        slot_out[:, to, :] = product.astype(jnp.bfloat16).reshape(group, slots, cols)

    def down_step(step, carry):
        y_from = lax.rem(y + y_count - near_order(step), y_count)
        x_from = lax.rem(x + x_count - near_order(step), x_count)

        @pl.when(step > 0)
        def _arrive_y():
            wait_bytes(hidden_all.at[:, y_from, 0], hid_y_sem.at[y_from])

        def down_first(other, inner):
            down_block(other, y_from, 0)
            return inner

        lax.fori_loop(0, x_count, down_first, 0)

        @pl.when(step > 0)
        def _arrive_x():
            wait_bytes(hidden_all.at[x_from, :, 1], hid_x_sem.at[x_from])

        def down_second(other, inner):
            down_block(x_from, other, 1)
            return inner

        lax.fori_loop(0, y_count, down_second, 0)
        return carry

    lax.fori_loop(0, y_count, down_step, 0)

    mine = x * y_count + y

    def mix_one(step, carry):
        x_to = lax.rem(x + (step + 1) // y_count, x_count)
        y_to = lax.rem(y + step + 1, y_count)
        to = x_to * y_count + y_to
        mixed = jnp.dot(picks[to], slot_out[to], preferred_element_type=jnp.float32)
        mix_out[to] = mixed.astype(jnp.bfloat16)

        def give(first, last):
            source = mix_out.at[to, :, first:last]
            target = mix_in.at[mine, :, first:last]

            @pl.when(to == mine)
            def _keep():
                pltpu.make_async_copy(source, target, mix_sem.at[mine]).start()

            @pl.when(to != mine)
            def _send():
                remote(
                    source,
                    target,
                    sent.at[17],
                    mix_sem.at[mine],
                    {"dp": x_to, "seq": 2 * y_to + c},
                ).start()

        @pl.when(y % 2 == c)
        def _whole():
            give(0, cols)

        @pl.when((y % 2 == 0) & (c == 1))
        def _low():
            give(0, cols - LANES)

        @pl.when((y % 2 == 1) & (c == 0))
        def _high():
            give(LANES, cols)

        return carry

    lax.fori_loop(0, group, mix_one, 0)

    wait_bytes(stream_own, own_sem)
    wait_bytes(attended, att_sem)

    def finish(core):
        for block in range(s_count):
            part = slice(block * head_cols, (block + 1) * head_cols)
            even, odd = 2 * block, 2 * block + 1
            if core == 0:
                wait_bytes(mix_in.at[even], mix_sem.at[even])
                wait_bytes(mix_in.at[odd, :, LANES:cols], mix_sem.at[odd])
                mixed = [mix_in[even], mix_in[odd, :, LANES:]]
            else:
                wait_bytes(mix_in.at[even, :, 0 : cols - LANES], mix_sem.at[even])
                wait_bytes(mix_in.at[odd], mix_sem.at[odd])
                mixed = [mix_in[even, :, : cols - LANES], mix_in[odd]]
            mixed = jnp.concatenate(mixed, axis=1)
            residual = stream_own[:, part].astype(jnp.float32) + attn_gate_ref[:, part].astype(
                jnp.float32
            ) * attended[:, part].astype(jnp.float32)
            output_ref[:, part] = (
                residual + ffn_gate_ref[:, part].astype(jnp.float32) * mixed.astype(jnp.float32)
            ).astype(jnp.bfloat16)

    for core in range(2):

        @pl.when(c == core)
        def _finish():
            finish(core)

    wait_bytes(info_y.at[pl.ds(0, y_count - 1)], sent.at[0])
    wait_bytes(weights.at[0, 0, pl.ds(0, y_count - 1)], sent.at[1])
    batch_left(1, 0)
    batch_left(1, 1)

    @pl.when(z // 2 == x)
    def _spread_done():
        wait_bytes(gate_up.at[0, pl.ds(0, z_count - 1), 0], sent.at[4])

    wait_bytes(slot_rows.at[pl.ds(0, x_count - 1)], sent.at[5])
    wait_bytes(info_x.at[pl.ds(0, x_count - 1)], sent.at[6])
    wait_bytes(weights.at[0, pl.ds(0, z_count - 1)], sent.at[7])
    wait_bytes(weights.at[0], sent.at[8])
    wait_bytes(core_send, sent.at[9])
    wait_bytes(part_send, sent.at[10])
    wait_bytes(att_out.at[pl.ds(0, s_count - 1)], sent.at[11])
    wait_bytes(out_rows, sent.at[12])
    wait_bytes(gate_up.at[0, pl.ds(0, z_count - 1)], sent.at[13])
    wait_bytes(gate_up.at[0], sent.at[14])
    wait_bytes(hidden_all.at[pl.ds(0, 2), pl.ds(0, y_count - 1), 0], sent.at[15])
    wait_bytes(hidden_all.at[:, pl.ds(0, y_count - 1), 0], sent.at[16])
    wait_bytes(hidden_all.at[pl.ds(0, x_count - 1), :, 1], sent.at[18])

    @pl.when(y % 2 == c)
    def _whole_done():
        wait_bytes(mix_out.at[pl.ds(0, group - 1)], sent.at[17])

    @pl.when(y % 2 != c)
    def _part_done():
        wait_bytes(mix_out.at[pl.ds(0, group - 1), :, 0 : cols - LANES], sent.at[17])


def on_device(
    query_rows,
    key_rows,
    value_rows,
    stream,
    shared_basis,
    expert_gate_up,
    expert_down,
    attn_gate,
    ffn_scale,
    ffn_gate,
    expert_ids,
    route_weights,
):
    x_count, z_count, s_count = (lax.axis_size(name) for name in ("dp", "exp", "seq"))
    y_count = s_count // 2
    tok_rows, model_width = stream.shape
    experts_here, hidden_cols, _ = expert_down.shape
    expert_total = z_count * s_count * experts_here
    rank = shared_basis.shape[1]
    head_cols = model_width // s_count
    cols = 384
    slots = 4 * CAP
    length = s_count * tok_rows
    group = x_count * y_count

    vmem = pl.BlockSpec(memory_space=pltpu.VMEM)
    anywhere = pl.BlockSpec(memory_space=pl.ANY)
    bf16, f32 = jnp.bfloat16, jnp.float32
    wide = rank + LANES
    dma = pltpu.SemaphoreType.DMA
    return pl.pallas_call(
        block_kernel,
        out_shape=jax.ShapeDtypeStruct((tok_rows, model_width), bf16),
        in_specs=[anywhere] * 6 + [vmem] * 6,
        out_specs=vmem,
        scratch_shapes=[
            pltpu.VMEM((2, length, head_cols), bf16),
            pltpu.VMEM((s_count, 2, tok_rows, head_cols), bf16),
            pltpu.VMEM((tok_rows, model_width), bf16),
            pltpu.VMEM((s_count, tok_rows, head_cols), bf16),
            pltpu.VMEM((tok_rows, model_width), bf16),
            pltpu.VMEM((2 * tok_rows, head_cols), bf16),
            pltpu.VMEM((2, tok_rows, wide), f32),
            pltpu.VMEM((y_count, tok_rows, wide), f32),
            pltpu.VMEM((y_count, tok_rows, wide), bf16),
            pltpu.VMEM((y_count, tok_rows, wide), bf16),
            pltpu.VMEM((y_count - 1, tok_rows, wide), bf16),
            pltpu.VMEM((y_count - 1, tok_rows, wide), bf16),
            pltpu.VMEM((y_count - 1, z_count * slots, rank), bf16),
            pltpu.VMEM((y_count, z_count * slots, rank), bf16),
            pltpu.VMEM((x_count, y_count, 2 * slots, rank), bf16),
            pltpu.VMEM(
                (2, z_count, 2, experts_here, rank // z_count, 2 * hidden_cols), bf16
            ),
            pltpu.VMEM((x_count, y_count, 2, group * slots, hidden_cols), bf16),
            pltpu.VMEM((2, z_count, y_count, experts_here * hidden_cols, cols), bf16),
            pltpu.VMEM((group, z_count * y_count * slots, cols), bf16),
            pltpu.VMEM((group, tok_rows, cols), bf16),
            pltpu.VMEM((group, tok_rows, cols), bf16),
            pltpu.VMEM((8, tok_rows), f32),
            pltpu.VMEM((y_count, 8, tok_rows), f32),
            pltpu.VMEM((x_count, y_count, 8, tok_rows), f32),
            pltpu.VMEM((2, group * slots, 1), f32),
            pltpu.VMEM((group, tok_rows, group * 2 * slots), bf16),
            dma,
            dma((s_count,)),
            dma((2, 2)),
            dma,
            dma((2,)),
            dma,
            dma((z_count,)),
            dma,
            dma,
            dma((z_count,)),
            dma,
            dma((y_count,)),
            dma,
            dma,
            dma((y_count,)),
            dma,
            dma((2,)),
            dma((y_count,)),
            dma((x_count,)),
            dma((group,)),
            dma((19,)),
        ],
        compiler_params=pltpu.CompilerParams(
            collective_id=0, has_side_effects=True, vmem_limit_bytes=62 * 1024 * 1024
        ),
        name="block",
    )(
        query_rows,
        key_rows,
        value_rows,
        stream,
        expert_down,
        expert_gate_up,
        shared_basis,
        attn_gate,
        ffn_scale,
        ffn_gate,
        expert_ids.T,
        route_weights.T,
    )


def solution(mesh):
    in_specs = (
        P(("dp", "exp", "seq"), None),
        P(("dp", "exp", "seq"), None),
        P(("dp", "exp", "seq"), None),
        P(("dp", "exp", "seq"), None),
        P("seq", None),
        P(("exp", "seq"), None, None),
        P(("exp", "seq"), None, None),
        P(("dp", "exp"), None),
        P(("dp", "exp"), None),
        P(("dp", "exp"), None),
        P(("dp", "exp", "seq"), None),
        P(("dp", "exp", "seq"), None),
    )
    out_specs = P(("dp", "exp", "seq"), None)
    return jax.shard_map(
        on_device, mesh=mesh, in_specs=in_specs, out_specs=out_specs, check_vma=False
    )
```

```python
import functools
import math

import jax
import jax.numpy as jnp
from jax import lax
from jax.experimental import pallas as pl
from jax.experimental.pallas import tpu as pltpu
from jax.sharding import PartitionSpec as P

HEAD_DIM = 128
LANES = 128
MESH = pl.DeviceIdType.MESH
epsilon = 1e-06
CAP = 4


def block_kernel(
    query_ref,
    key_ref,
    value_ref,
    stream_ref,
    down_ref,
    gate_up_ref,
    basis_ref,
    attn_gate_ref,
    ffn_scale_ref,
    ffn_gate_ref,
    ids_ref,
    route_ref,
    output_ref,
    kv_in,
    qs_in,
    stream_own,
    att_out,
    attended,
    modulated,
    partial,
    own_part,
    core_send,
    core_recv,
    part_send,
    part_recv,
    out_rows,
    near_rows,
    slot_rows,
    gate_up,
    hidden_all,
    weights,
    slot_out,
    mix_out,
    mix_in,
    info_own,
    info_y,
    info_x,
    slot_weight,
    picks,
    kv_sem,
    qs_sem,
    batch_sem,
    own_sem,
    info_sem,
    near_w_sem,
    ring_sem,
    pair_w_sem,
    near_g_sem,
    ring_g_sem,
    pair_g_sem,
    core_sem,
    part_sem,
    att_sem,
    near_sem,
    slot_sem,
    hid_sem,
    hid_y_sem,
    hid_x_sem,
    mix_sem,
    sent,
):
    x_count, z_count, s_count = (lax.axis_size(name) for name in ("dp", "exp", "seq"))
    y_count = s_count // 2
    x, z, s = (lax.axis_index(name) for name in ("dp", "exp", "seq"))
    y, c = s // 2, s % 2
    other_c = 1 - c
    pair = 2 * y + other_c
    tok_rows, model_width = attended.shape
    head_cols = kv_in.shape[2]
    heads_here = head_cols // HEAD_DIM
    cols = weights.shape[4]
    rank = near_rows.shape[2]
    slots = 4 * CAP
    quarter = model_width // x_count

    def remote(src, dst, send_sem, recv_sem, device):
        return pltpu.make_async_remote_copy(
            src_ref=src,
            dst_ref=dst,
            send_sem=send_sem,
            recv_sem=recv_sem,
            device_id=device,
            device_id_type=MESH,
        )

    def wait_bytes(ref, sem):
        pltpu.make_async_copy(ref, ref, sem).wait()

    def first_column(y_to):
        return pl.multiple_of(x * quarter + (y_to // 2) * head_cols + (y_to % 2) * 256, LANES)

    def near_order(step):
        return step + step // 2 - 2 * (step // 3)

    barrier = pltpu.get_barrier_semaphore()

    def greet(device):
        pl.semaphore_signal(barrier, inc=1, device_id=device, device_id_type=MESH)

    def greet_seq(step, carry):
        greet({"seq": lax.rem(s + step, s_count)})
        return carry

    def greet_z(step, carry):
        greet({"exp": lax.rem(z + step, z_count)})
        return carry

    def greet_x(step, carry):
        greet({"dp": lax.rem(x + step, x_count)})

        def greet_xy(y_step, inner):
            greet(
                {
                    "dp": lax.rem(x + step, x_count),
                    "seq": 2 * lax.rem(y + y_step, y_count) + c,
                }
            )
            return inner

        return lax.fori_loop(1, y_count, greet_xy, carry)

    lax.fori_loop(1, s_count, greet_seq, 0)
    lax.fori_loop(1, z_count, greet_z, 0)
    lax.fori_loop(1, x_count, greet_x, 0)

    my_rows = pl.ds(pl.multiple_of(s * tok_rows, tok_rows), tok_rows)
    my_cols = pl.ds(pl.multiple_of(s * head_cols, head_cols), head_cols)
    kv_refs = (key_ref, value_ref)
    qs_refs = (query_ref, stream_ref)
    for which in range(2):
        pltpu.make_async_copy(
            kv_refs[which].at[:, my_cols], kv_in.at[which, my_rows, :], kv_sem
        ).start()
        pltpu.make_async_copy(
            qs_refs[which].at[:, my_cols], qs_in.at[s, which], qs_sem.at[s]
        ).start()
        pltpu.make_async_copy(
            down_ref.at[which, :, pl.ds(first_column(y), cols)],
            weights.at[c, z, y, pl.ds(which * LANES, LANES), :],
            near_w_sem,
        ).start()
    pltpu.make_async_copy(stream_ref, stream_own, own_sem).start()

    rank_part = rank // z_count
    twin = z - 2 * x

    @pl.when(z // 2 == x)
    def _own_gate_up():
        part = pl.ds(pl.multiple_of(z * rank_part, rank_part), rank_part)
        pltpu.make_async_copy(
            gate_up_ref.at[:, part, :], gate_up.at[c, z, twin], near_g_sem
        ).start()

    entries = 2 * tok_rows
    experts = 4 * z_count * y_count
    ids_row = jnp.concatenate([ids_ref[0:1, :], ids_ref[1:2, :]], axis=1)
    named = lax.broadcasted_iota(jnp.int32, (experts, entries), 0) == ids_row
    entry = [lax.broadcasted_iota(jnp.int32, (entries, entries), axis) for axis in (0, 1)]
    entry = [2 * (one % tok_rows) + one // tok_rows for one in entry]
    before = jnp.where(entry[0] < entry[1], 1.0, 0.0).astype(jnp.bfloat16)
    counts = jnp.dot(
        jnp.where(named, 1.0, 0.0).astype(jnp.bfloat16), before, preferred_element_type=jnp.float32
    )
    slot_ids = (
        jnp.sum(jnp.where(named, counts, 0.0), axis=0, keepdims=True)
        + ids_row.astype(jnp.float32) * CAP
    )
    info_row = lax.broadcasted_iota(jnp.int32, info_own.shape, 0)
    info = jnp.where(info_row == 2, route_ref[0:1, :], 0.0)
    info = jnp.where(info_row == 3, route_ref[1:2, :], info)
    info = jnp.where(info_row == 0, slot_ids[:, :tok_rows], info)
    info_own[...] = jnp.where(info_row == 1, slot_ids[:, tok_rows:], info)
    pltpu.make_async_copy(info_own, info_y.at[y], info_sem.at[0]).start()

    pl.semaphore_wait(barrier, s_count - 1 + z_count - 1 + (x_count - 1) * y_count)

    def info_to_y(step, carry):
        y_to = lax.rem(y + step, y_count)
        remote(
            info_own, info_y.at[y], sent.at[0], info_sem.at[0], {"seq": 2 * y_to + c}
        ).start()
        return carry

    lax.fori_loop(1, y_count, info_to_y, 0)

    def near_first(step, carry):
        y_to = lax.rem(y + near_order(step), y_count)
        device = {"seq": 2 * y_to + c}
        for which in range(2):
            remote(
                down_ref.at[which, :, pl.ds(first_column(y_to), cols)],
                weights.at[c, z, y, pl.ds(which * LANES, LANES), :],
                sent.at[1],
                near_w_sem,
                device,
            ).start()
        return carry

    lax.fori_loop(1, y_count, near_first, 0)

    @pl.when(z // 2 == x)
    def _spread_gate_up():
        def to_z(step, carry):
            z_to = lax.rem(z + step, z_count)
            part = pl.ds(pl.multiple_of(z_to * rank_part, rank_part), rank_part)
            remote(
                gate_up_ref.at[:, part, :],
                gate_up.at[c, z_to, twin],
                sent.at[4],
                near_g_sem,
                {"exp": z_to},
            ).start()
            return carry

        lax.fori_loop(1, z_count, to_z, 0)


    def send_batch(refs, slot_of, sem, send_sem, distances):
        def one_copy(index, carry):
            s_to = 2 * lax.rem(y + distances[0] + 2 * (index % len(distances)), y_count) + (
                index // len(distances)
            )
            columns = pl.ds(pl.multiple_of(s_to * head_cols, head_cols), head_cols)
            for which in range(2):
                remote(
                    refs[which].at[:, columns], slot_of(which), send_sem, sem, {"seq": s_to}
                ).start()
            return carry

        if len(distances) == 2:
            columns = pl.ds(pl.multiple_of(pair * head_cols, head_cols), head_cols)
            for which in range(2):
                remote(
                    refs[which].at[:, columns], slot_of(which), send_sem, sem, {"seq": pair}
                ).start()
        lax.fori_loop(0, 2 * len(distances), one_copy, 0)

    batches = ((1, 3), (2,))

    def send_kv(batch):
        send_batch(
            kv_refs,
            lambda which: kv_in.at[which, my_rows, :],
            kv_sem,
            batch_sem.at[0, batch],
            batches[batch],
        )

    def send_qs(batch):
        send_batch(
            qs_refs,
            lambda which: qs_in.at[s, which],
            qs_sem.at[s],
            batch_sem.at[1, batch],
            batches[batch],
        )

    def batch_left(kind, batch):
        peers = 5 if batch == 0 else 2
        wait_bytes(qs_in.at[pl.ds(0, peers)], batch_sem.at[kind, batch])

    send_kv(0)

    always = z >= 0
    half = z_count // 2

    def pass_on(buffer, sems, left_sem, pair_left, pair_sem, block, up, down):
        held = buffer.at[c, block]

        def pass_to(z_to):
            remote(held, held, left_sem, sems.at[block], {"exp": lax.rem(z_to, z_count)}).start()

        if up is not None:

            @pl.when(up)
            def _up():
                pass_to(z + 1)

        if down is not None:

            @pl.when(down)
            def _down():
                pass_to(z + z_count - 1)

        remote(held, held, pair_left, pair_sem, {"seq": pair}).start()

    def ring_step(ring, step):
        buffer, sems = ring[0], ring[1]
        below = lax.rem(z + z_count - step, z_count)
        above = lax.rem(z + step, z_count)
        wait_bytes(buffer.at[c, below], sems.at[below])
        if step == half:
            pass_on(*ring, below, None, None)
            return
        pass_on(*ring, below, always if step < half - 1 else c == 0, None)
        wait_bytes(buffer.at[c, above], sems.at[above])
        pass_on(*ring, above, None, always if step < half - 1 else c == 1)

    gate_ring = (gate_up, ring_g_sem, sent.at[13], sent.at[14], pair_g_sem)
    down_ring = (weights, ring_sem, sent.at[7], sent.at[8], pair_w_sem)

    wait_bytes(gate_up.at[c, z], near_g_sem)
    wait_bytes(info_y, info_sem.at[0])
    pltpu.make_async_copy(info_y, info_x.at[x], info_sem.at[1]).start()

    def info_to_x(step, carry):
        remote(
            info_y,
            info_x.at[x],
            sent.at[6],
            info_sem.at[1],
            {"dp": lax.rem(x + step, x_count)},
        ).start()
        return carry

    lax.fori_loop(1, x_count, info_to_x, 0)
    pass_on(*gate_ring, z, always, always)
    send_kv(1)
    ring_step(gate_ring, 1)
    wait_bytes(weights.at[c, z], near_w_sem)
    pass_on(*down_ring, z, always, always)
    batch_left(0, 0)
    send_qs(0)
    ring_step(gate_ring, 2)
    ring_step(gate_ring, 3)
    batch_left(0, 1)
    send_qs(1)

    wait_bytes(info_x, info_sem.at[1])
    group = x_count * y_count
    chip_rows = group * slots
    def make_pick(source, carry):
        slot_iota = lax.broadcasted_iota(jnp.int32, (picks.shape[2], tok_rows), 0).astype(
            jnp.float32
        )
        named_here = info_x[source // y_count, source % y_count]
        pick = (slot_iota == named_here[0:1, :]) | (slot_iota == named_here[1:2, :])
        picks[source] = jnp.where(pick, 1.0, 0.0).astype(jnp.bfloat16).T
        return carry

    wait_bytes(kv_in, kv_sem)

    length = s_count * tok_rows
    lane = lax.broadcasted_iota(jnp.int32, (length, HEAD_DIM), 1)
    ones_column = jnp.where(lane == 0, 1.0, 0.0).astype(jnp.bfloat16)
    exponent_scale = 1.0 / (math.sqrt(HEAD_DIM) * math.log(2.0))
    gate_row = attn_gate_ref[:, my_cols].astype(jnp.float32)
    scale_row = ffn_scale_ref[:, my_cols].astype(jnp.float32)
    two = 2 * tok_rows
    tail_lane = lax.broadcasted_iota(jnp.int32, (two, LANES), 1)

    def with_tail(values, square, tail):
        high = square.astype(jnp.bfloat16).astype(jnp.float32)
        extra = jnp.where(tail == 0, high, jnp.where(tail == 1, square - high, 0.0))
        return jnp.concatenate([values, extra], axis=1)

    def add_core_part(step):
        wait_bytes(core_recv.at[step], core_sem.at[step])
        total = own_part[step] + core_recv[step].astype(jnp.float32)
        square = total[:, rank : rank + 1] + total[:, rank + 1 : rank + 2]
        return total[:, :rank], square

    def send_part(step):
        values, square = add_core_part(step)
        part_send[step - 1] = with_tail(values, square, tail_lane[:tok_rows]).astype(jnp.bfloat16)
        distance = near_order(step)
        y_to = lax.rem(y + y_count - distance, y_count)
        remote(
            part_send.at[step - 1],
            part_recv.at[step - 1],
            sent.at[10],
            part_sem,
            {"seq": 2 * y_to + c},
        ).start()

    def one_chip(step, carry):
        y_from = lax.rem(y + y_count - near_order(step), y_count)

        @pl.when(step > 1)
        def _previous():
            send_part(step - 1)

        for core in range(2):
            wait_bytes(qs_in.at[2 * y_from + core], qs_sem.at[2 * y_from + core])
        both = pl.ds(2 * y_from, 2)
        square = jnp.zeros((two, 1), jnp.float32)
        for head in range(heads_here):
            part = slice(head * HEAD_DIM, (head + 1) * HEAD_DIM)
            scores = lax.dot_general(
                qs_in[both, 0, :, part].reshape(two, HEAD_DIM),
                kv_in[0, :, part],
                (((1,), (1,)), ((), ())),
                preferred_element_type=jnp.float32,
            )
            row_max = jnp.max(scores, axis=-1, keepdims=True)
            raised = jnp.exp2((scores - row_max) * exponent_scale).astype(jnp.bfloat16)
            value_ones = jnp.concatenate([kv_in[1, :, part], ones_column], axis=1)
            mixed = jnp.dot(raised, value_ones, preferred_element_type=jnp.float32)
            mixed = (mixed[:, :HEAD_DIM] / mixed[:, HEAD_DIM : HEAD_DIM + 1]).astype(jnp.bfloat16)
            att_out[both, :, part] = mixed.reshape(2, tok_rows, HEAD_DIM)
            residual = qs_in[both, 1, :, part].reshape(two, HEAD_DIM).astype(
                jnp.float32
            ) + gate_row[:, part] * mixed.astype(jnp.float32)
            modulated[:, part] = (residual * scale_row[:, part]).astype(jnp.bfloat16)
            square = square + jnp.sum(residual * residual, axis=1, keepdims=True)
        product = jnp.dot(modulated[...], basis_ref[...], preferred_element_type=jnp.float32)
        partial[...] = with_tail(product, square, tail_lane).reshape(partial.shape)
        own_part[step] = partial[c]
        core_send[step] = partial[other_c].astype(jnp.bfloat16)
        remote(
            core_send.at[step], core_recv.at[step], sent.at[9], core_sem.at[step], {"seq": pair}
        ).start()
        return carry

    def after_chip(step, carry):
        one_chip(step, carry)

        @pl.when(step == 0)
        def _last_batch():
            ring_step(gate_ring, half)

        @pl.when(step == 2)
        def _ring_one():
            ring_step(down_ring, 1)

        return carry

    lax.fori_loop(0, y_count, after_chip, 0)
    send_part(y_count - 1)

    def send_attended(index, carry):
        s_to = lax.rem(s + index, s_count)

        @pl.when(s_to == s)
        def _keep():
            pltpu.make_async_copy(att_out.at[s_to], attended.at[:, my_cols], att_sem).start()

        @pl.when(s_to != s)
        def _send():
            remote(
                att_out.at[s_to], attended.at[:, my_cols], sent.at[11], att_sem, {"seq": s_to}
            ).start()

        return carry

    values, square = add_core_part(0)
    wait_bytes(part_recv, part_sem)
    for step in range(y_count - 1):
        arrived = part_recv[step].astype(jnp.float32)
        values = values + arrived[:, :rank]
        square = square + arrived[:, rank : rank + 1] + arrived[:, rank + 1 : rank + 2]
    low_rank = (values / jnp.sqrt(square / model_width + epsilon)).astype(jnp.bfloat16)

    def pick_rows(y_to):
        row = lax.broadcasted_iota(jnp.int32, (z_count * slots, tok_rows), 0)
        slot_here = (((row // slots) * y_count + y_to) * slots + row % slots).astype(jnp.float32)
        pick = (slot_here == info_own[0:1, :]) | (slot_here == info_own[1:2, :])
        pick = jnp.where(pick, 1.0, 0.0).astype(jnp.bfloat16)
        return jnp.dot(pick, low_rank, preferred_element_type=jnp.float32).astype(jnp.bfloat16)

    chip_slots = 2 * slots

    def forward_rows(y_from):
        def to_x(x_step, inner):
            x_to = lax.rem(x + near_order(x_step), x_count)
            rows = pl.ds(pl.multiple_of(x_to * chip_slots, chip_slots), chip_slots)
            remote(
                near_rows.at[y_from, rows, :],
                slot_rows.at[x, y_from],
                sent.at[5],
                slot_sem,
                {"dp": x_to},
            ).start()
            return inner

        lax.fori_loop(1, x_count, to_x, 0)
        own = pl.ds(pl.multiple_of(x * chip_slots, chip_slots), chip_slots)
        pltpu.make_async_copy(near_rows.at[y_from, own, :], slot_rows.at[x, y_from], slot_sem).start()

    for step in range(1, y_count):
        y_to = lax.rem(y + near_order(step), y_count)
        out_rows[step - 1] = pick_rows(y_to)
        remote(
            out_rows.at[step - 1],
            near_rows.at[y],
            sent.at[12],
            near_sem.at[y],
            {"seq": 2 * y_to + c},
        ).start()


    near_rows[y] = pick_rows(y)
    forward_rows(y)
    ring_step(down_ring, 2)

    def forward_near(step, carry):
        y_from = lax.rem(y + y_count - near_order(step), y_count)
        lax.fori_loop(4 * step - 4, 4 * step, make_pick, 0)
        wait_bytes(near_rows.at[y_from], near_sem.at[y_from])
        forward_rows(y_from)
        return lax.fori_loop(2 * step, 2 * step + 2, send_attended, carry)

    lax.fori_loop(0, 2, send_attended, 0)
    named_all = info_x[...].reshape(group, info_x.shape[2], tok_rows)
    place = lax.broadcasted_iota(jnp.int32, (group, slots, tok_rows), 1)
    for which in range(2):
        slot_here = (place + ((2 * x + which) * y_count + y) * slots).astype(jnp.float32)
        routed = jnp.where(
            slot_here == named_all[:, 0:1, :], named_all[:, 2:3, :], 0.0
        ) + jnp.where(slot_here == named_all[:, 1:2, :], named_all[:, 3:4, :], 0.0)
        slot_weight[which] = jnp.sum(routed, axis=2, keepdims=True).reshape(chip_rows, 1)

    lax.fori_loop(1, y_count, forward_near, 0)

    wait_bytes(gate_up.at[other_c], pair_g_sem)
    wait_bytes(slot_rows, slot_sem)
    expert = lax.broadcasted_iota(jnp.int32, (chip_rows, 1), 0) % slots // CAP

    for twin_here in range(2):
        rows = slot_rows[:, :, pl.ds(twin_here * slots, slots), :].reshape(chip_rows, rank)
        both_halves = jnp.zeros((chip_rows, gate_up.shape[5]), jnp.float32)
        for which in range(4):
            product = jnp.dot(
                rows,
                gate_up[which // 2, :, twin_here, which % 2].reshape(rank, gate_up.shape[5]),
                preferred_element_type=jnp.float32,
            )
            both_halves = jnp.where(expert == which, product, both_halves)
        gate, up = both_halves[:, :LANES], both_halves[:, LANES:]
        hidden = gate / (1.0 + jnp.exp(-gate)) * up * slot_weight[twin_here]
        hidden_all[x, y, twin_here] = hidden.astype(jnp.bfloat16)
        held = hidden_all.at[x, y, twin_here]

        def hidden_near(step, carry):
            if twin_here == 0:
                device = {"dp": lax.rem(x + near_order(step), x_count)}
            else:
                device = {"seq": 2 * lax.rem(y + near_order(step), y_count) + c}
            remote(held, held, sent.at[15], hid_sem.at[twin_here], device).start()
            return carry

        lax.fori_loop(1, x_count, hidden_near, 0)

    ring_step(down_ring, 3)
    lax.fori_loop(4 * (y_count - 1), group, make_pick, 0)
    wait_bytes(hidden_all.at[pl.ds(0, x_count - 1), y, 0], hid_sem.at[0])

    def hidden_to_y(step, carry):
        held = hidden_all.at[:, y, 0]
        y_to = lax.rem(y + near_order(step), y_count)
        remote(held, held, sent.at[16], hid_y_sem.at[y], {"seq": 2 * y_to + c}).start()
        return carry

    lax.fori_loop(1, y_count, hidden_to_y, 0)
    wait_bytes(hidden_all.at[x, pl.ds(0, y_count - 1), 1], hid_sem.at[1])

    def hidden_to_x(step, carry):
        held = hidden_all.at[x, :, 1]
        x_to = lax.rem(x + near_order(step), x_count)
        remote(held, held, sent.at[18], hid_x_sem.at[x], {"dp": x_to}).start()
        return carry

    lax.fori_loop(1, x_count, hidden_to_x, 0)
    ring_step(down_ring, half)
    wait_bytes(weights.at[other_c], pair_w_sem)

    chip_expert = lax.broadcasted_iota(jnp.int32, (chip_rows, LANES), 0) % slots // CAP

    masks = [
        jnp.where(chip_expert == which, 1.0, 0.0).astype(jnp.bfloat16) for which in range(4)
    ]

    def down_block(x_from, y_from, twin_here):
        held = hidden_all[x_from, y_from, twin_here]
        z_from = 2 * x_from + twin_here
        masked = [held * mask for mask in masks]
        product = jnp.dot(
            jnp.concatenate(masked[:2], axis=1),
            weights[0, z_from, y_from],
            preferred_element_type=jnp.float32,
        ) + jnp.dot(
            jnp.concatenate(masked[2:], axis=1),
            weights[1, z_from, y_from],
            preferred_element_type=jnp.float32,
        )
        to = pl.ds(pl.multiple_of((z_from * y_count + y_from) * slots, slots), slots)
        slot_out[:, to, :] = product.astype(jnp.bfloat16).reshape(group, slots, cols)

    def down_step(step, carry):
        y_from = lax.rem(y + y_count - near_order(step), y_count)
        x_from = lax.rem(x + x_count - near_order(step), x_count)

        @pl.when(step > 0)
        def _arrive_y():
            wait_bytes(hidden_all.at[:, y_from, 0], hid_y_sem.at[y_from])

        def down_first(other, inner):
            down_block(other, y_from, 0)
            return inner

        lax.fori_loop(0, x_count, down_first, 0)

        @pl.when(step > 0)
        def _arrive_x():
            wait_bytes(hidden_all.at[x_from, :, 1], hid_x_sem.at[x_from])

        def down_second(other, inner):
            down_block(x_from, other, 1)
            return inner

        lax.fori_loop(0, y_count, down_second, 0)
        return carry

    lax.fori_loop(0, y_count, down_step, 0)

    mine = x * y_count + y

    def mix_one(step, carry):
        x_to = lax.rem(x + (step + 1) // y_count, x_count)
        y_to = lax.rem(y + step + 1, y_count)
        to = x_to * y_count + y_to
        mixed = jnp.dot(picks[to], slot_out[to], preferred_element_type=jnp.float32)
        mix_out[to] = mixed.astype(jnp.bfloat16)

        def give(first, last):
            source = mix_out.at[to, :, first:last]
            target = mix_in.at[mine, :, first:last]

            @pl.when(to == mine)
            def _keep():
                pltpu.make_async_copy(source, target, mix_sem.at[mine]).start()

            @pl.when(to != mine)
            def _send():
                remote(
                    source,
                    target,
                    sent.at[17],
                    mix_sem.at[mine],
                    {"dp": x_to, "seq": 2 * y_to + c},
                ).start()

        @pl.when(y % 2 == c)
        def _whole():
            give(0, cols)

        @pl.when((y % 2 == 0) & (c == 1))
        def _low():
            give(0, cols - LANES)

        @pl.when((y % 2 == 1) & (c == 0))
        def _high():
            give(LANES, cols)

        return carry

    lax.fori_loop(0, group, mix_one, 0)

    wait_bytes(stream_own, own_sem)
    wait_bytes(attended, att_sem)

    def finish(core):
        for block in range(s_count):
            part = slice(block * head_cols, (block + 1) * head_cols)
            even, odd = 2 * block, 2 * block + 1
            if core == 0:
                wait_bytes(mix_in.at[even], mix_sem.at[even])
                wait_bytes(mix_in.at[odd, :, LANES:cols], mix_sem.at[odd])
                mixed = [mix_in[even], mix_in[odd, :, LANES:]]
            else:
                wait_bytes(mix_in.at[even, :, 0 : cols - LANES], mix_sem.at[even])
                wait_bytes(mix_in.at[odd], mix_sem.at[odd])
                mixed = [mix_in[even, :, : cols - LANES], mix_in[odd]]
            mixed = jnp.concatenate(mixed, axis=1)
            residual = stream_own[:, part].astype(jnp.float32) + attn_gate_ref[:, part].astype(
                jnp.float32
            ) * attended[:, part].astype(jnp.float32)
            output_ref[:, part] = (
                residual + ffn_gate_ref[:, part].astype(jnp.float32) * mixed.astype(jnp.float32)
            ).astype(jnp.bfloat16)

    for core in range(2):

        @pl.when(c == core)
        def _finish():
            finish(core)

    wait_bytes(info_y.at[pl.ds(0, y_count - 1)], sent.at[0])
    wait_bytes(weights.at[0, 0, pl.ds(0, y_count - 1)], sent.at[1])
    batch_left(1, 0)
    batch_left(1, 1)

    @pl.when(z // 2 == x)
    def _spread_done():
        wait_bytes(gate_up.at[0, pl.ds(0, z_count - 1), 0], sent.at[4])

    wait_bytes(slot_rows.at[pl.ds(0, x_count - 1)], sent.at[5])
    wait_bytes(info_x.at[pl.ds(0, x_count - 1)], sent.at[6])
    wait_bytes(weights.at[0, pl.ds(0, z_count - 1)], sent.at[7])
    wait_bytes(weights.at[0], sent.at[8])
    wait_bytes(core_send, sent.at[9])
    wait_bytes(part_send, sent.at[10])
    wait_bytes(att_out.at[pl.ds(0, s_count - 1)], sent.at[11])
    wait_bytes(out_rows, sent.at[12])
    wait_bytes(gate_up.at[0, pl.ds(0, z_count - 1)], sent.at[13])
    wait_bytes(gate_up.at[0], sent.at[14])
    wait_bytes(hidden_all.at[pl.ds(0, 2), pl.ds(0, y_count - 1), 0], sent.at[15])
    wait_bytes(hidden_all.at[:, pl.ds(0, y_count - 1), 0], sent.at[16])
    wait_bytes(hidden_all.at[pl.ds(0, x_count - 1), :, 1], sent.at[18])

    @pl.when(y % 2 == c)
    def _whole_done():
        wait_bytes(mix_out.at[pl.ds(0, group - 1)], sent.at[17])

    @pl.when(y % 2 != c)
    def _part_done():
        wait_bytes(mix_out.at[pl.ds(0, group - 1), :, 0 : cols - LANES], sent.at[17])


def on_device(
    query_rows,
    key_rows,
    value_rows,
    stream,
    shared_basis,
    expert_gate_up,
    expert_down,
    attn_gate,
    ffn_scale,
    ffn_gate,
    expert_ids,
    route_weights,
):
    x_count, z_count, s_count = (lax.axis_size(name) for name in ("dp", "exp", "seq"))
    y_count = s_count // 2
    tok_rows, model_width = stream.shape
    experts_here, hidden_cols, _ = expert_down.shape
    expert_total = z_count * s_count * experts_here
    rank = shared_basis.shape[1]
    head_cols = model_width // s_count
    cols = 384
    slots = 4 * CAP
    length = s_count * tok_rows
    group = x_count * y_count

    vmem = pl.BlockSpec(memory_space=pltpu.VMEM)
    anywhere = pl.BlockSpec(memory_space=pl.ANY)
    bf16, f32 = jnp.bfloat16, jnp.float32
    wide = rank + LANES
    dma = pltpu.SemaphoreType.DMA
    return pl.pallas_call(
        block_kernel,
        out_shape=jax.ShapeDtypeStruct((tok_rows, model_width), bf16),
        in_specs=[anywhere] * 6 + [vmem] * 6,
        out_specs=vmem,
        scratch_shapes=[
            pltpu.VMEM((2, length, head_cols), bf16),
            pltpu.VMEM((s_count, 2, tok_rows, head_cols), bf16),
            pltpu.VMEM((tok_rows, model_width), bf16),
            pltpu.VMEM((s_count, tok_rows, head_cols), bf16),
            pltpu.VMEM((tok_rows, model_width), bf16),
            pltpu.VMEM((2 * tok_rows, head_cols), bf16),
            pltpu.VMEM((2, tok_rows, wide), f32),
            pltpu.VMEM((y_count, tok_rows, wide), f32),
            pltpu.VMEM((y_count, tok_rows, wide), bf16),
            pltpu.VMEM((y_count, tok_rows, wide), bf16),
            pltpu.VMEM((y_count - 1, tok_rows, wide), bf16),
            pltpu.VMEM((y_count - 1, tok_rows, wide), bf16),
            pltpu.VMEM((y_count - 1, z_count * slots, rank), bf16),
            pltpu.VMEM((y_count, z_count * slots, rank), bf16),
            pltpu.VMEM((x_count, y_count, 2 * slots, rank), bf16),
            pltpu.VMEM(
                (2, z_count, 2, experts_here, rank // z_count, 2 * hidden_cols), bf16
            ),
            pltpu.VMEM((x_count, y_count, 2, group * slots, hidden_cols), bf16),
            pltpu.VMEM((2, z_count, y_count, experts_here * hidden_cols, cols), bf16),
            pltpu.VMEM((group, z_count * y_count * slots, cols), bf16),
            pltpu.VMEM((group, tok_rows, cols), bf16),
            pltpu.VMEM((group, tok_rows, cols), bf16),
            pltpu.VMEM((8, tok_rows), f32),
            pltpu.VMEM((y_count, 8, tok_rows), f32),
            pltpu.VMEM((x_count, y_count, 8, tok_rows), f32),
            pltpu.VMEM((2, group * slots, 1), f32),
            pltpu.VMEM((group, tok_rows, group * 2 * slots), bf16),
            dma,
            dma((s_count,)),
            dma((2, 2)),
            dma,
            dma((2,)),
            dma,
            dma((z_count,)),
            dma,
            dma,
            dma((z_count,)),
            dma,
            dma((y_count,)),
            dma,
            dma,
            dma((y_count,)),
            dma,
            dma((2,)),
            dma((y_count,)),
            dma((x_count,)),
            dma((group,)),
            dma((19,)),
        ],
        compiler_params=pltpu.CompilerParams(
            collective_id=0, has_side_effects=True, vmem_limit_bytes=62 * 1024 * 1024
        ),
        name="block",
    )(
        query_rows,
        key_rows,
        value_rows,
        stream,
        expert_down,
        expert_gate_up,
        shared_basis,
        attn_gate,
        ffn_scale,
        ffn_gate,
        expert_ids.T,
        route_weights.T,
    )


def solution(mesh):
    in_specs = (
        P(("dp", "exp", "seq"), None),
        P(("dp", "exp", "seq"), None),
        P(("dp", "exp", "seq"), None),
        P(("dp", "exp", "seq"), None),
        P("seq", None),
        P(("exp", "seq"), None, None),
        P(("exp", "seq"), None, None),
        P(("dp", "exp"), None),
        P(("dp", "exp"), None),
        P(("dp", "exp"), None),
        P(("dp", "exp", "seq"), None),
        P(("dp", "exp", "seq"), None),
    )
    out_specs = P(("dp", "exp", "seq"), None)
    return jax.shard_map(
        on_device, mesh=mesh, in_specs=in_specs, out_specs=out_specs, check_vma=False
    )
```

```python
import functools
import math

import jax
import jax.numpy as jnp
from jax import lax
from jax.experimental import pallas as pl
from jax.experimental.pallas import tpu as pltpu
from jax.sharding import PartitionSpec as P

HEAD_DIM = 128
LANES = 128
MESH = pl.DeviceIdType.MESH
epsilon = 1e-06
CAP = 4


def block_kernel(
    query_ref,
    key_ref,
    value_ref,
    stream_ref,
    down_ref,
    gate_up_ref,
    basis_ref,
    attn_gate_ref,
    ffn_scale_ref,
    ffn_gate_ref,
    ids_ref,
    route_ref,
    output_ref,
    kv_in,
    qs_in,
    stream_own,
    att_out,
    attended,
    modulated,
    partial,
    own_part,
    core_send,
    core_recv,
    part_send,
    part_recv,
    out_rows,
    near_rows,
    slot_rows,
    gate_up,
    hidden_all,
    weights,
    slot_out,
    mix_out,
    mix_in,
    info_own,
    info_y,
    info_x,
    slot_weight,
    picks,
    kv_sem,
    qs_sem,
    batch_sem,
    own_sem,
    info_sem,
    near_w_sem,
    ring_sem,
    pair_w_sem,
    near_g_sem,
    ring_g_sem,
    pair_g_sem,
    core_sem,
    part_sem,
    att_sem,
    near_sem,
    slot_sem,
    hid_sem,
    hid_y_sem,
    hid_x_sem,
    mix_sem,
    sent,
):
    x_count, z_count, s_count = (lax.axis_size(name) for name in ("dp", "exp", "seq"))
    y_count = s_count // 2
    x, z, s = (lax.axis_index(name) for name in ("dp", "exp", "seq"))
    y, c = s // 2, s % 2
    other_c = 1 - c
    pair = 2 * y + other_c
    tok_rows, model_width = attended.shape
    head_cols = kv_in.shape[2]
    heads_here = head_cols // HEAD_DIM
    cols = weights.shape[4]
    rank = near_rows.shape[3]
    slots = 4 * CAP
    quarter = model_width // x_count

    def remote(src, dst, send_sem, recv_sem, device):
        return pltpu.make_async_remote_copy(
            src_ref=src,
            dst_ref=dst,
            send_sem=send_sem,
            recv_sem=recv_sem,
            device_id=device,
            device_id_type=MESH,
        )

    def wait_bytes(ref, sem):
        pltpu.make_async_copy(ref, ref, sem).wait()

    def first_column(y_to):
        return pl.multiple_of(x * quarter + (y_to // 2) * head_cols + (y_to % 2) * 256, LANES)

    def near_order(step):
        return step + step // 2 - 2 * (step // 3)

    barrier = pltpu.get_barrier_semaphore()

    def greet(device):
        pl.semaphore_signal(barrier, inc=1, device_id=device, device_id_type=MESH)

    def greet_seq(step, carry):
        greet({"seq": lax.rem(s + step, s_count)})
        return carry

    def greet_z(step, carry):
        greet({"exp": lax.rem(z + step, z_count)})
        return carry

    def greet_x(step, carry):
        greet({"dp": lax.rem(x + step, x_count)})

        def greet_xy(y_step, inner):
            greet(
                {
                    "dp": lax.rem(x + step, x_count),
                    "seq": 2 * lax.rem(y + y_step, y_count) + c,
                }
            )
            return inner

        return lax.fori_loop(1, y_count, greet_xy, carry)

    lax.fori_loop(1, s_count, greet_seq, 0)
    lax.fori_loop(1, z_count, greet_z, 0)
    lax.fori_loop(1, x_count, greet_x, 0)

    my_rows = pl.ds(pl.multiple_of(s * tok_rows, tok_rows), tok_rows)
    my_cols = pl.ds(pl.multiple_of(s * head_cols, head_cols), head_cols)
    kv_refs = (key_ref, value_ref)
    qs_refs = (query_ref, stream_ref)
    for which in range(2):
        pltpu.make_async_copy(
            kv_refs[which].at[:, my_cols], kv_in.at[which, my_rows, :], kv_sem
        ).start()
        pltpu.make_async_copy(
            qs_refs[which].at[:, my_cols], qs_in.at[s, which], qs_sem.at[s]
        ).start()
        pltpu.make_async_copy(
            down_ref.at[which, :, pl.ds(first_column(y), cols)],
            weights.at[c, z, y, pl.ds(which * LANES, LANES), :],
            near_w_sem,
        ).start()
    pltpu.make_async_copy(stream_ref, stream_own, own_sem).start()

    rank_part = rank // z_count
    twin = z - 2 * x

    @pl.when(z // 2 == x)
    def _own_gate_up():
        part = pl.ds(pl.multiple_of(z * rank_part, rank_part), rank_part)
        pltpu.make_async_copy(
            gate_up_ref.at[:, part, :], gate_up.at[c, z, twin], near_g_sem
        ).start()

    entries = 2 * tok_rows
    experts = 4 * z_count * y_count
    ids_row = jnp.concatenate([ids_ref[0:1, :], ids_ref[1:2, :]], axis=1)
    named = lax.broadcasted_iota(jnp.int32, (experts, entries), 0) == ids_row
    entry = [lax.broadcasted_iota(jnp.int32, (entries, entries), axis) for axis in (0, 1)]
    entry = [2 * (one % tok_rows) + one // tok_rows for one in entry]
    before = jnp.where(entry[0] < entry[1], 1.0, 0.0).astype(jnp.bfloat16)
    counts = jnp.dot(
        jnp.where(named, 1.0, 0.0).astype(jnp.bfloat16), before, preferred_element_type=jnp.float32
    )
    slot_ids = (
        jnp.sum(jnp.where(named, counts, 0.0), axis=0, keepdims=True)
        + ids_row.astype(jnp.float32) * CAP
    )
    info_row = lax.broadcasted_iota(jnp.int32, info_own.shape, 0)
    info = jnp.where(info_row == 2, route_ref[0:1, :], 0.0)
    info = jnp.where(info_row == 3, route_ref[1:2, :], info)
    info = jnp.where(info_row == 0, slot_ids[:, :tok_rows], info)
    info_own[...] = jnp.where(info_row == 1, slot_ids[:, tok_rows:], info)
    pltpu.make_async_copy(info_own, info_y.at[y], info_sem.at[0]).start()

    pl.semaphore_wait(barrier, s_count - 1 + z_count - 1 + (x_count - 1) * y_count)

    def info_to_y(step, carry):
        y_to = lax.rem(y + step, y_count)
        remote(
            info_own, info_y.at[y], sent.at[0], info_sem.at[0], {"seq": 2 * y_to + c}
        ).start()
        return carry

    lax.fori_loop(1, y_count, info_to_y, 0)

    def near_first(step, carry):
        y_to = lax.rem(y + near_order(step), y_count)
        device = {"seq": 2 * y_to + c}
        for which in range(2):
            remote(
                down_ref.at[which, :, pl.ds(first_column(y_to), cols)],
                weights.at[c, z, y, pl.ds(which * LANES, LANES), :],
                sent.at[1],
                near_w_sem,
                device,
            ).start()
        return carry

    lax.fori_loop(1, y_count, near_first, 0)

    @pl.when(z // 2 == x)
    def _spread_gate_up():
        def to_z(step, carry):
            z_to = lax.rem(z + step, z_count)
            part = pl.ds(pl.multiple_of(z_to * rank_part, rank_part), rank_part)
            remote(
                gate_up_ref.at[:, part, :],
                gate_up.at[c, z_to, twin],
                sent.at[4],
                near_g_sem,
                {"exp": z_to},
            ).start()
            return carry

        lax.fori_loop(1, z_count, to_z, 0)


    def send_batch(refs, slot_of, sem, send_sem, distances):
        def one_copy(index, carry):
            s_to = 2 * lax.rem(y + distances[0] + 2 * (index % len(distances)), y_count) + (
                index // len(distances)
            )
            columns = pl.ds(pl.multiple_of(s_to * head_cols, head_cols), head_cols)
            for which in range(2):
                remote(
                    refs[which].at[:, columns], slot_of(which), send_sem, sem, {"seq": s_to}
                ).start()
            return carry

        if len(distances) == 2:
            columns = pl.ds(pl.multiple_of(pair * head_cols, head_cols), head_cols)
            for which in range(2):
                remote(
                    refs[which].at[:, columns], slot_of(which), send_sem, sem, {"seq": pair}
                ).start()
        lax.fori_loop(0, 2 * len(distances), one_copy, 0)

    batches = ((1, 3), (2,))

    def send_kv(batch):
        send_batch(
            kv_refs,
            lambda which: kv_in.at[which, my_rows, :],
            kv_sem,
            batch_sem.at[0, batch],
            batches[batch],
        )

    def send_qs(batch):
        send_batch(
            qs_refs,
            lambda which: qs_in.at[s, which],
            qs_sem.at[s],
            batch_sem.at[1, batch],
            batches[batch],
        )

    def batch_left(kind, batch):
        peers = 5 if batch == 0 else 2
        wait_bytes(qs_in.at[pl.ds(0, peers)], batch_sem.at[kind, batch])

    send_kv(0)

    always = z >= 0
    half = z_count // 2

    def pass_on(buffer, sems, left_sem, pair_left, pair_sem, block, up, down):
        held = buffer.at[c, block]

        def pass_to(z_to):
            remote(held, held, left_sem, sems.at[block], {"exp": lax.rem(z_to, z_count)}).start()

        if up is not None:

            @pl.when(up)
            def _up():
                pass_to(z + 1)

        if down is not None:

            @pl.when(down)
            def _down():
                pass_to(z + z_count - 1)

        remote(held, held, pair_left, pair_sem, {"seq": pair}).start()

    def ring_step(ring, step):
        buffer, sems = ring[0], ring[1]
        below = lax.rem(z + z_count - step, z_count)
        above = lax.rem(z + step, z_count)
        wait_bytes(buffer.at[c, below], sems.at[below])
        if step == half:
            pass_on(*ring, below, None, None)
            return
        pass_on(*ring, below, always if step < half - 1 else c == 0, None)
        wait_bytes(buffer.at[c, above], sems.at[above])
        pass_on(*ring, above, None, always if step < half - 1 else c == 1)

    gate_ring = (gate_up, ring_g_sem, sent.at[13], sent.at[14], pair_g_sem)
    down_ring = (weights, ring_sem, sent.at[7], sent.at[8], pair_w_sem)

    wait_bytes(gate_up.at[c, z], near_g_sem)
    wait_bytes(info_y, info_sem.at[0])
    pltpu.make_async_copy(info_y, info_x.at[x], info_sem.at[1]).start()

    def info_to_x(step, carry):
        remote(
            info_y,
            info_x.at[x],
            sent.at[6],
            info_sem.at[1],
            {"dp": lax.rem(x + step, x_count)},
        ).start()
        return carry

    lax.fori_loop(1, x_count, info_to_x, 0)
    pass_on(*gate_ring, z, always, always)
    send_kv(1)
    ring_step(gate_ring, 1)
    wait_bytes(weights.at[c, z], near_w_sem)
    pass_on(*down_ring, z, always, always)
    batch_left(0, 0)
    send_qs(0)
    ring_step(gate_ring, 2)
    ring_step(gate_ring, 3)
    batch_left(0, 1)
    send_qs(1)

    wait_bytes(info_x, info_sem.at[1])
    group = x_count * y_count
    chip_rows = group * slots
    def make_pick(source, carry):
        slot_iota = lax.broadcasted_iota(jnp.int32, (picks.shape[2], tok_rows), 0).astype(
            jnp.float32
        )
        named_here = info_x[source // y_count, source % y_count]
        pick = (slot_iota == named_here[0:1, :]) | (slot_iota == named_here[1:2, :])
        picks[source] = jnp.where(pick, 1.0, 0.0).astype(jnp.bfloat16).T
        return carry

    wait_bytes(kv_in, kv_sem)

    length = s_count * tok_rows
    lane = lax.broadcasted_iota(jnp.int32, (length, HEAD_DIM), 1)
    ones_column = jnp.where(lane == 0, 1.0, 0.0).astype(jnp.bfloat16)
    exponent_scale = 1.0 / (math.sqrt(HEAD_DIM) * math.log(2.0))
    gate_row = attn_gate_ref[:, my_cols].astype(jnp.float32)
    scale_row = ffn_scale_ref[:, my_cols].astype(jnp.float32)
    two = 2 * tok_rows
    tail_lane = lax.broadcasted_iota(jnp.int32, (two, LANES), 1)

    def with_tail(values, square, tail):
        high = square.astype(jnp.bfloat16).astype(jnp.float32)
        extra = jnp.where(tail == 0, high, jnp.where(tail == 1, square - high, 0.0))
        return jnp.concatenate([values, extra], axis=1)

    def add_core_part(step):
        wait_bytes(core_recv.at[step], core_sem.at[step])
        total = own_part[step] + core_recv[step].astype(jnp.float32)
        square = total[:, rank : rank + 1] + total[:, rank + 1 : rank + 2]
        return total[:, :rank], square

    def send_part(step):
        values, square = add_core_part(step)
        part_send[step - 1] = with_tail(values, square, tail_lane[:tok_rows]).astype(jnp.bfloat16)
        distance = near_order(step)
        y_to = lax.rem(y + y_count - distance, y_count)
        remote(
            part_send.at[step - 1],
            part_recv.at[step - 1],
            sent.at[10],
            part_sem,
            {"seq": 2 * y_to + c},
        ).start()

    def send_attended(step):
        y_to = lax.rem(y + y_count - near_order(step), y_count)

        def one_core(core, carry):
            s_to = 2 * y_to + core

            @pl.when(s_to == s)
            def _keep():
                pltpu.make_async_copy(att_out.at[s_to], attended.at[:, my_cols], att_sem).start()

            @pl.when(s_to != s)
            def _send():
                remote(
                    att_out.at[s_to], attended.at[:, my_cols], sent.at[11], att_sem, {"seq": s_to}
                ).start()

            return carry

        lax.fori_loop(0, 2, one_core, 0)

    def one_chip(step, carry):
        y_from = lax.rem(y + y_count - near_order(step), y_count)

        @pl.when(step > 1)
        def _previous():
            send_part(step - 1)

        for core in range(2):
            wait_bytes(qs_in.at[2 * y_from + core], qs_sem.at[2 * y_from + core])

        @pl.when(step == y_count - 1)
        def _earlier():
            for earlier in range(y_count - 1):
                send_attended(earlier)

        both = pl.ds(2 * y_from, 2)
        square = jnp.zeros((two, 1), jnp.float32)
        for head in range(heads_here):
            part = slice(head * HEAD_DIM, (head + 1) * HEAD_DIM)
            scores = lax.dot_general(
                qs_in[both, 0, :, part].reshape(two, HEAD_DIM),
                kv_in[0, :, part],
                (((1,), (1,)), ((), ())),
                preferred_element_type=jnp.float32,
            )
            row_max = jnp.max(scores, axis=-1, keepdims=True)
            raised = jnp.exp2((scores - row_max) * exponent_scale).astype(jnp.bfloat16)
            value_ones = jnp.concatenate([kv_in[1, :, part], ones_column], axis=1)
            mixed = jnp.dot(raised, value_ones, preferred_element_type=jnp.float32)
            mixed = (mixed[:, :HEAD_DIM] / mixed[:, HEAD_DIM : HEAD_DIM + 1]).astype(jnp.bfloat16)
            att_out[both, :, part] = mixed.reshape(2, tok_rows, HEAD_DIM)
            residual = qs_in[both, 1, :, part].reshape(two, HEAD_DIM).astype(
                jnp.float32
            ) + gate_row[:, part] * mixed.astype(jnp.float32)
            modulated[:, part] = (residual * scale_row[:, part]).astype(jnp.bfloat16)
            square = square + jnp.sum(residual * residual, axis=1, keepdims=True)
        product = jnp.dot(modulated[...], basis_ref[...], preferred_element_type=jnp.float32)
        partial[...] = with_tail(product, square, tail_lane).reshape(partial.shape)
        own_part[step] = partial[c]
        core_send[step] = partial[other_c].astype(jnp.bfloat16)
        remote(
            core_send.at[step], core_recv.at[step], sent.at[9], core_sem.at[step], {"seq": pair}
        ).start()
        return carry

    def after_chip(step, carry):
        one_chip(step, carry)

        @pl.when(step == 0)
        def _last_batch():
            ring_step(gate_ring, half)

        @pl.when(step == 2)
        def _ring_one():
            ring_step(down_ring, 1)

        return carry

    lax.fori_loop(0, y_count, after_chip, 0)
    send_part(y_count - 1)

    values, square = add_core_part(0)
    wait_bytes(part_recv, part_sem)
    for step in range(y_count - 1):
        arrived = part_recv[step].astype(jnp.float32)
        values = values + arrived[:, :rank]
        square = square + arrived[:, rank : rank + 1] + arrived[:, rank + 1 : rank + 2]
    low_rank = (values / jnp.sqrt(square / model_width + epsilon)).astype(jnp.bfloat16)

    def pick_rows(y_to, twin_here):
        row = lax.broadcasted_iota(jnp.int32, (x_count * slots, tok_rows), 0)
        chip = (2 * (row // slots) + twin_here) * y_count + y_to
        slot_here = (chip * slots + row % slots).astype(jnp.float32)
        pick = (slot_here == info_own[0:1, :]) | (slot_here == info_own[1:2, :])
        pick = jnp.where(pick, 1.0, 0.0).astype(jnp.bfloat16)
        return jnp.dot(pick, low_rank, preferred_element_type=jnp.float32).astype(jnp.bfloat16)

    def forward_rows(y_from, twin_here):
        def to_x(x_step, inner):
            x_to = lax.rem(x + near_order(x_step), x_count)
            rows = pl.ds(pl.multiple_of(x_to * slots, slots), slots)
            remote(
                near_rows.at[twin_here, y_from, rows, :],
                slot_rows.at[twin_here, x, y_from],
                sent.at[5],
                slot_sem.at[twin_here],
                {"dp": x_to},
            ).start()
            return inner

        lax.fori_loop(1, x_count, to_x, 0)
        own = pl.ds(pl.multiple_of(x * slots, slots), slots)
        pltpu.make_async_copy(
            near_rows.at[twin_here, y_from, own, :],
            slot_rows.at[twin_here, x, y_from],
            slot_sem.at[twin_here],
        ).start()

    for twin_here in range(2):
        for step in range(1, y_count):
            y_to = lax.rem(y + near_order(step), y_count)
            out_rows[step - 1, twin_here] = pick_rows(y_to, twin_here)
            remote(
                out_rows.at[step - 1, twin_here],
                near_rows.at[twin_here, y],
                sent.at[12],
                near_sem.at[twin_here, y],
                {"seq": 2 * y_to + c},
            ).start()
        near_rows[twin_here, y] = pick_rows(y, twin_here)
        forward_rows(y, twin_here)

    ring_step(down_ring, 2)
    send_attended(y_count - 1)

    named_all = info_x[...].reshape(group, info_x.shape[2], tok_rows)
    place = lax.broadcasted_iota(jnp.int32, (group, slots, tok_rows), 1)
    for which in range(2):
        slot_here = (place + ((2 * x + which) * y_count + y) * slots).astype(jnp.float32)
        routed = jnp.where(
            slot_here == named_all[:, 0:1, :], named_all[:, 2:3, :], 0.0
        ) + jnp.where(slot_here == named_all[:, 1:2, :], named_all[:, 3:4, :], 0.0)
        slot_weight[which] = jnp.sum(routed, axis=2, keepdims=True).reshape(chip_rows, 1)

    expert = lax.broadcasted_iota(jnp.int32, (chip_rows, 1), 0) % slots // CAP
    half_rows = chip_rows // 2
    halves = (pl.ds(0, half_rows), pl.ds(half_rows, half_rows))

    def forward_half(twin_here):
        def forward_near(step, carry):
            y_from = lax.rem(y + y_count - near_order(step), y_count)
            if twin_here == 0:
                lax.fori_loop(4 * step - 4, 4 * step, make_pick, 0)
            wait_bytes(near_rows.at[twin_here, y_from], near_sem.at[twin_here, y_from])
            forward_rows(y_from, twin_here)
            return carry

        lax.fori_loop(1, y_count, forward_near, 0)

    def hidden_half(twin_here):
        wait_bytes(slot_rows.at[twin_here], slot_sem.at[twin_here])
        rows = slot_rows[twin_here].reshape(chip_rows, rank)
        both_halves = jnp.zeros((chip_rows, gate_up.shape[5]), jnp.float32)
        for which in range(4):
            product = jnp.dot(
                rows,
                gate_up[which // 2, :, twin_here, which % 2].reshape(rank, gate_up.shape[5]),
                preferred_element_type=jnp.float32,
            )
            both_halves = jnp.where(expert == which, product, both_halves)
        gate, up = both_halves[:, :LANES], both_halves[:, LANES:]
        hidden = gate / (1.0 + jnp.exp(-gate)) * up * slot_weight[twin_here]
        hidden_all[x, y, twin_here] = hidden.astype(jnp.bfloat16)

        def hidden_near(step, carry):
            devices = (
                {"dp": lax.rem(x + near_order(step), x_count)},
                {"seq": 2 * lax.rem(y + near_order(step), y_count) + c},
            )
            for which in range(2):
                held = hidden_all.at[x, y, twin_here, halves[which], :]
                remote(held, held, sent.at[15], hid_sem.at[twin_here, which], devices[which]).start()
            return carry

        lax.fori_loop(1, x_count, hidden_near, 0)

    def hidden_far(twin_here):
        for which in range(2):
            near = hidden_all.at[pl.ds(0, x_count - 1), 0, twin_here, halves[which], :]
            wait_bytes(near, hid_sem.at[twin_here, which])

            def push(step, carry):
                if which == 0:
                    held = hidden_all.at[:, y, twin_here, halves[0], :]
                    device = {"seq": 2 * lax.rem(y + near_order(step), y_count) + c}
                    remote(held, held, sent.at[16], hid_y_sem.at[twin_here, y], device).start()
                else:
                    held = hidden_all.at[x, :, twin_here, halves[1], :]
                    device = {"dp": lax.rem(x + near_order(step), x_count)}
                    remote(held, held, sent.at[18], hid_x_sem.at[twin_here, x], device).start()
                return carry

            lax.fori_loop(1, x_count, push, 0)

    def hidden_wait(twin_here):
        def arrive(step, carry):
            y_from = lax.rem(y + y_count - near_order(step), y_count)
            x_from = lax.rem(x + x_count - near_order(step), x_count)
            wait_bytes(
                hidden_all.at[:, y_from, twin_here, halves[0], :], hid_y_sem.at[twin_here, y_from]
            )
            wait_bytes(
                hidden_all.at[x_from, :, twin_here, halves[1], :], hid_x_sem.at[twin_here, x_from]
            )
            return carry

        lax.fori_loop(1, y_count, arrive, 0)

    forward_half(0)
    wait_bytes(gate_up.at[other_c], pair_g_sem)
    hidden_half(0)
    forward_half(1)
    hidden_far(0)
    hidden_half(1)
    ring_step(down_ring, 3)
    lax.fori_loop(4 * (y_count - 1), group, make_pick, 0)
    hidden_far(1)
    ring_step(down_ring, half)
    wait_bytes(weights.at[other_c], pair_w_sem)

    chip_expert = lax.broadcasted_iota(jnp.int32, (chip_rows, LANES), 0) % slots // CAP

    masks = [
        jnp.where(chip_expert == which, 1.0, 0.0).astype(jnp.bfloat16) for which in range(4)
    ]

    def down_block(x_from, y_from, twin_here):
        held = hidden_all[x_from, y_from, twin_here]
        z_from = 2 * x_from + twin_here
        masked = [held * mask for mask in masks]
        product = jnp.dot(
            jnp.concatenate(masked[:2], axis=1),
            weights[0, z_from, y_from],
            preferred_element_type=jnp.float32,
        ) + jnp.dot(
            jnp.concatenate(masked[2:], axis=1),
            weights[1, z_from, y_from],
            preferred_element_type=jnp.float32,
        )
        to = pl.ds(pl.multiple_of((z_from * y_count + y_from) * slots, slots), slots)
        slot_out[:, to, :] = product.astype(jnp.bfloat16).reshape(group, slots, cols)

    for twin_here in range(2):
        hidden_wait(twin_here)

        def down_one(chip, carry):
            down_block(chip // y_count, chip % y_count, twin_here)
            return carry

        lax.fori_loop(0, group, down_one, 0)

    mine = x * y_count + y

    def mix_one(step, carry):
        x_to = lax.rem(x + (step + 1) // y_count, x_count)
        y_to = lax.rem(y + step + 1, y_count)
        to = x_to * y_count + y_to
        mixed = jnp.dot(picks[to], slot_out[to], preferred_element_type=jnp.float32)
        mix_out[to] = mixed.astype(jnp.bfloat16)

        def give(first, last):
            source = mix_out.at[to, :, first:last]
            target = mix_in.at[mine, :, first:last]

            @pl.when(to == mine)
            def _keep():
                pltpu.make_async_copy(source, target, mix_sem.at[mine]).start()

            @pl.when(to != mine)
            def _send():
                remote(
                    source,
                    target,
                    sent.at[17],
                    mix_sem.at[mine],
                    {"dp": x_to, "seq": 2 * y_to + c},
                ).start()

        @pl.when(y % 2 == c)
        def _whole():
            give(0, cols)

        @pl.when((y % 2 == 0) & (c == 1))
        def _low():
            give(0, cols - LANES)

        @pl.when((y % 2 == 1) & (c == 0))
        def _high():
            give(LANES, cols)

        return carry

    lax.fori_loop(0, group, mix_one, 0)

    wait_bytes(stream_own, own_sem)
    wait_bytes(attended, att_sem)

    def finish(core):
        for block in range(s_count):
            part = slice(block * head_cols, (block + 1) * head_cols)
            even, odd = 2 * block, 2 * block + 1
            if core == 0:
                wait_bytes(mix_in.at[even], mix_sem.at[even])
                wait_bytes(mix_in.at[odd, :, LANES:cols], mix_sem.at[odd])
                mixed = [mix_in[even], mix_in[odd, :, LANES:]]
            else:
                wait_bytes(mix_in.at[even, :, 0 : cols - LANES], mix_sem.at[even])
                wait_bytes(mix_in.at[odd], mix_sem.at[odd])
                mixed = [mix_in[even, :, : cols - LANES], mix_in[odd]]
            mixed = jnp.concatenate(mixed, axis=1)
            residual = stream_own[:, part].astype(jnp.float32) + attn_gate_ref[:, part].astype(
                jnp.float32
            ) * attended[:, part].astype(jnp.float32)
            output_ref[:, part] = (
                residual + ffn_gate_ref[:, part].astype(jnp.float32) * mixed.astype(jnp.float32)
            ).astype(jnp.bfloat16)

    for core in range(2):

        @pl.when(c == core)
        def _finish():
            finish(core)

    wait_bytes(info_y.at[pl.ds(0, y_count - 1)], sent.at[0])
    wait_bytes(weights.at[0, 0, pl.ds(0, y_count - 1)], sent.at[1])
    batch_left(1, 0)
    batch_left(1, 1)

    @pl.when(z // 2 == x)
    def _spread_done():
        wait_bytes(gate_up.at[0, pl.ds(0, z_count - 1), 0], sent.at[4])

    wait_bytes(slot_rows.at[:, pl.ds(0, x_count - 1)], sent.at[5])
    wait_bytes(info_x.at[pl.ds(0, x_count - 1)], sent.at[6])
    wait_bytes(weights.at[0, pl.ds(0, z_count - 1)], sent.at[7])
    wait_bytes(weights.at[0], sent.at[8])
    wait_bytes(core_send, sent.at[9])
    wait_bytes(part_send, sent.at[10])
    wait_bytes(att_out.at[pl.ds(0, s_count - 1)], sent.at[11])
    wait_bytes(out_rows, sent.at[12])
    wait_bytes(gate_up.at[0, pl.ds(0, z_count - 1)], sent.at[13])
    wait_bytes(gate_up.at[0], sent.at[14])
    wait_bytes(hidden_all.at[pl.ds(0, x_count - 1), :, 0, halves[0], :], sent.at[15])
    wait_bytes(hidden_all.at[pl.ds(0, x_count - 1), :, :, halves[0], :], sent.at[16])
    wait_bytes(hidden_all.at[pl.ds(0, x_count - 1), :, :, halves[0], :], sent.at[18])

    @pl.when(y % 2 == c)
    def _whole_done():
        wait_bytes(mix_out.at[pl.ds(0, group - 1)], sent.at[17])

    @pl.when(y % 2 != c)
    def _part_done():
        wait_bytes(mix_out.at[pl.ds(0, group - 1), :, 0 : cols - LANES], sent.at[17])


def on_device(
    query_rows,
    key_rows,
    value_rows,
    stream,
    shared_basis,
    expert_gate_up,
    expert_down,
    attn_gate,
    ffn_scale,
    ffn_gate,
    expert_ids,
    route_weights,
):
    x_count, z_count, s_count = (lax.axis_size(name) for name in ("dp", "exp", "seq"))
    y_count = s_count // 2
    tok_rows, model_width = stream.shape
    experts_here, hidden_cols, _ = expert_down.shape
    expert_total = z_count * s_count * experts_here
    rank = shared_basis.shape[1]
    head_cols = model_width // s_count
    cols = 384
    slots = 4 * CAP
    length = s_count * tok_rows
    group = x_count * y_count

    vmem = pl.BlockSpec(memory_space=pltpu.VMEM)
    anywhere = pl.BlockSpec(memory_space=pl.ANY)
    bf16, f32 = jnp.bfloat16, jnp.float32
    wide = rank + LANES
    dma = pltpu.SemaphoreType.DMA
    return pl.pallas_call(
        block_kernel,
        out_shape=jax.ShapeDtypeStruct((tok_rows, model_width), bf16),
        in_specs=[anywhere] * 6 + [vmem] * 6,
        out_specs=vmem,
        scratch_shapes=[
            pltpu.VMEM((2, length, head_cols), bf16),
            pltpu.VMEM((s_count, 2, tok_rows, head_cols), bf16),
            pltpu.VMEM((tok_rows, model_width), bf16),
            pltpu.VMEM((s_count, tok_rows, head_cols), bf16),
            pltpu.VMEM((tok_rows, model_width), bf16),
            pltpu.VMEM((2 * tok_rows, head_cols), bf16),
            pltpu.VMEM((2, tok_rows, wide), f32),
            pltpu.VMEM((y_count, tok_rows, wide), f32),
            pltpu.VMEM((y_count, tok_rows, wide), bf16),
            pltpu.VMEM((y_count, tok_rows, wide), bf16),
            pltpu.VMEM((y_count - 1, tok_rows, wide), bf16),
            pltpu.VMEM((y_count - 1, tok_rows, wide), bf16),
            pltpu.VMEM((y_count - 1, 2, x_count * slots, rank), bf16),
            pltpu.VMEM((2, y_count, x_count * slots, rank), bf16),
            pltpu.VMEM((2, x_count, y_count, slots, rank), bf16),
            pltpu.VMEM(
                (2, z_count, 2, experts_here, rank // z_count, 2 * hidden_cols), bf16
            ),
            pltpu.VMEM((x_count, y_count, 2, group * slots, hidden_cols), bf16),
            pltpu.VMEM((2, z_count, y_count, experts_here * hidden_cols, cols), bf16),
            pltpu.VMEM((group, z_count * y_count * slots, cols), bf16),
            pltpu.VMEM((group, tok_rows, cols), bf16),
            pltpu.VMEM((group, tok_rows, cols), bf16),
            pltpu.VMEM((8, tok_rows), f32),
            pltpu.VMEM((y_count, 8, tok_rows), f32),
            pltpu.VMEM((x_count, y_count, 8, tok_rows), f32),
            pltpu.VMEM((2, group * slots, 1), f32),
            pltpu.VMEM((group, tok_rows, group * 2 * slots), bf16),
            dma,
            dma((s_count,)),
            dma((2, 2)),
            dma,
            dma((2,)),
            dma,
            dma((z_count,)),
            dma,
            dma,
            dma((z_count,)),
            dma,
            dma((y_count,)),
            dma,
            dma,
            dma((2, y_count)),
            dma((2,)),
            dma((2, 2)),
            dma((2, y_count)),
            dma((2, x_count)),
            dma((group,)),
            dma((19,)),
        ],
        compiler_params=pltpu.CompilerParams(
            collective_id=0, has_side_effects=True, vmem_limit_bytes=62 * 1024 * 1024
        ),
        name="block",
    )(
        query_rows,
        key_rows,
        value_rows,
        stream,
        expert_down,
        expert_gate_up,
        shared_basis,
        attn_gate,
        ffn_scale,
        ffn_gate,
        expert_ids.T,
        route_weights.T,
    )


def solution(mesh):
    in_specs = (
        P(("dp", "exp", "seq"), None),
        P(("dp", "exp", "seq"), None),
        P(("dp", "exp", "seq"), None),
        P(("dp", "exp", "seq"), None),
        P("seq", None),
        P(("exp", "seq"), None, None),
        P(("exp", "seq"), None, None),
        P(("dp", "exp"), None),
        P(("dp", "exp"), None),
        P(("dp", "exp"), None),
        P(("dp", "exp", "seq"), None),
        P(("dp", "exp", "seq"), None),
    )
    out_specs = P(("dp", "exp", "seq"), None)
    return jax.shard_map(
        on_device, mesh=mesh, in_specs=in_specs, out_specs=out_specs, check_vma=False
    )
```

```python
import functools
import math

import jax
import jax.numpy as jnp
from jax import lax
from jax.experimental import pallas as pl
from jax.experimental.pallas import tpu as pltpu
from jax.sharding import PartitionSpec as P

HEAD_DIM = 128
LANES = 128
MESH = pl.DeviceIdType.MESH
epsilon = 1e-06
CAP = 4


def block_kernel(
    query_ref,
    key_ref,
    value_ref,
    stream_ref,
    down_ref,
    gate_up_ref,
    basis_ref,
    attn_gate_ref,
    ffn_scale_ref,
    ffn_gate_ref,
    ids_ref,
    route_ref,
    output_ref,
    kv_in,
    qs_in,
    stream_own,
    att_out,
    attended,
    modulated,
    partial,
    own_part,
    core_send,
    core_recv,
    part_send,
    part_recv,
    out_rows,
    near_rows,
    slot_rows,
    gate_up,
    hidden_all,
    weights,
    slot_out,
    mix_out,
    mix_in,
    info_own,
    info_y,
    info_x,
    slot_weight,
    picks,
    kv_sem,
    qs_sem,
    batch_sem,
    own_sem,
    info_sem,
    near_w_sem,
    ring_sem,
    pair_w_sem,
    near_g_sem,
    ring_g_sem,
    pair_g_sem,
    core_sem,
    part_sem,
    att_sem,
    near_sem,
    slot_sem,
    hid_sem,
    hid_y_sem,
    hid_x_sem,
    mix_sem,
    sent,
):
    x_count, z_count, s_count = (lax.axis_size(name) for name in ("dp", "exp", "seq"))
    y_count = s_count // 2
    x, z, s = (lax.axis_index(name) for name in ("dp", "exp", "seq"))
    y, c = s // 2, s % 2
    other_c = 1 - c
    pair = 2 * y + other_c
    tok_rows, model_width = attended.shape
    head_cols = kv_in.shape[2]
    heads_here = head_cols // HEAD_DIM
    cols = weights.shape[4]
    rank = near_rows.shape[2]
    slots = 4 * CAP
    quarter = model_width // x_count

    def remote(src, dst, send_sem, recv_sem, device):
        return pltpu.make_async_remote_copy(
            src_ref=src,
            dst_ref=dst,
            send_sem=send_sem,
            recv_sem=recv_sem,
            device_id=device,
            device_id_type=MESH,
        )

    def wait_bytes(ref, sem):
        pltpu.make_async_copy(ref, ref, sem).wait()

    def first_column(y_to):
        return pl.multiple_of(x * quarter + (y_to // 2) * head_cols + (y_to % 2) * 256, LANES)

    def near_order(step):
        return step + step // 2 - 2 * (step // 3)

    barrier = pltpu.get_barrier_semaphore()

    def greet(device):
        pl.semaphore_signal(barrier, inc=1, device_id=device, device_id_type=MESH)

    def greet_seq(step, carry):
        greet({"seq": lax.rem(s + step, s_count)})
        return carry

    def greet_z(step, carry):
        greet({"exp": lax.rem(z + step, z_count)})
        return carry

    def greet_x(step, carry):
        greet({"dp": lax.rem(x + step, x_count)})

        def greet_xy(y_step, inner):
            greet(
                {
                    "dp": lax.rem(x + step, x_count),
                    "seq": 2 * lax.rem(y + y_step, y_count) + c,
                }
            )
            return inner

        return lax.fori_loop(1, y_count, greet_xy, carry)

    lax.fori_loop(1, s_count, greet_seq, 0)
    lax.fori_loop(1, z_count, greet_z, 0)
    lax.fori_loop(1, x_count, greet_x, 0)

    my_rows = pl.ds(pl.multiple_of(s * tok_rows, tok_rows), tok_rows)
    my_cols = pl.ds(pl.multiple_of(s * head_cols, head_cols), head_cols)
    kv_refs = (key_ref, value_ref)
    qs_refs = (query_ref, stream_ref)
    for which in range(2):
        pltpu.make_async_copy(
            kv_refs[which].at[:, my_cols], kv_in.at[which, my_rows, :], kv_sem
        ).start()
        pltpu.make_async_copy(
            qs_refs[which].at[:, my_cols], qs_in.at[s, which], qs_sem.at[which, s]
        ).start()
        pltpu.make_async_copy(
            down_ref.at[which, :, pl.ds(first_column(y), cols)],
            weights.at[c, z, y, pl.ds(which * LANES, LANES), :],
            near_w_sem,
        ).start()
    pltpu.make_async_copy(stream_ref, stream_own, own_sem).start()

    rank_part = rank // z_count
    twin = z - 2 * x

    @pl.when(z // 2 == x)
    def _own_gate_up():
        part = pl.ds(pl.multiple_of(z * rank_part, rank_part), rank_part)
        pltpu.make_async_copy(
            gate_up_ref.at[:, part, :], gate_up.at[c, z, twin], near_g_sem
        ).start()

    entries = 2 * tok_rows
    experts = 4 * z_count * y_count
    ids_row = jnp.concatenate([ids_ref[0:1, :], ids_ref[1:2, :]], axis=1)
    named = lax.broadcasted_iota(jnp.int32, (experts, entries), 0) == ids_row
    entry = [lax.broadcasted_iota(jnp.int32, (entries, entries), axis) for axis in (0, 1)]
    entry = [2 * (one % tok_rows) + one // tok_rows for one in entry]
    before = jnp.where(entry[0] < entry[1], 1.0, 0.0).astype(jnp.bfloat16)
    counts = jnp.dot(
        jnp.where(named, 1.0, 0.0).astype(jnp.bfloat16), before, preferred_element_type=jnp.float32
    )
    slot_ids = (
        jnp.sum(jnp.where(named, counts, 0.0), axis=0, keepdims=True)
        + ids_row.astype(jnp.float32) * CAP
    )
    info_row = lax.broadcasted_iota(jnp.int32, info_own.shape, 0)
    info = jnp.where(info_row == 2, route_ref[0:1, :], 0.0)
    info = jnp.where(info_row == 3, route_ref[1:2, :], info)
    info = jnp.where(info_row == 0, slot_ids[:, :tok_rows], info)
    info_own[...] = jnp.where(info_row == 1, slot_ids[:, tok_rows:], info)
    pltpu.make_async_copy(info_own, info_y.at[y], info_sem.at[0]).start()

    pl.semaphore_wait(barrier, s_count - 1 + z_count - 1 + (x_count - 1) * y_count)

    def info_to_y(step, carry):
        y_to = lax.rem(y + step, y_count)
        remote(
            info_own, info_y.at[y], sent.at[0], info_sem.at[0], {"seq": 2 * y_to + c}
        ).start()
        return carry

    lax.fori_loop(1, y_count, info_to_y, 0)

    def near_first(step, carry):
        y_to = lax.rem(y + near_order(step), y_count)
        device = {"seq": 2 * y_to + c}
        for which in range(2):
            remote(
                down_ref.at[which, :, pl.ds(first_column(y_to), cols)],
                weights.at[c, z, y, pl.ds(which * LANES, LANES), :],
                sent.at[1],
                near_w_sem,
                device,
            ).start()
        return carry

    lax.fori_loop(1, y_count, near_first, 0)

    @pl.when(z // 2 == x)
    def _spread_gate_up():
        def to_z(step, carry):
            z_to = lax.rem(z + step, z_count)
            part = pl.ds(pl.multiple_of(z_to * rank_part, rank_part), rank_part)
            remote(
                gate_up_ref.at[:, part, :],
                gate_up.at[c, z_to, twin],
                sent.at[4],
                near_g_sem,
                {"exp": z_to},
            ).start()
            return carry

        lax.fori_loop(1, z_count, to_z, 0)


    def send_batch(refs, slot_of, sem, send_sem, distances):
        for which in range(2):

            def one_copy(index, carry):
                s_to = 2 * lax.rem(y + distances[0] + 2 * (index % len(distances)), y_count) + (
                    index // len(distances)
                )
                columns = pl.ds(pl.multiple_of(s_to * head_cols, head_cols), head_cols)
                remote(
                    refs[which].at[:, columns], slot_of(which), send_sem, sem(which), {"seq": s_to}
                ).start()
                return carry

            if len(distances) == 2:
                columns = pl.ds(pl.multiple_of(pair * head_cols, head_cols), head_cols)
                remote(
                    refs[which].at[:, columns], slot_of(which), send_sem, sem(which), {"seq": pair}
                ).start()
            lax.fori_loop(0, 2 * len(distances), one_copy, 0)

    batches = ((1, 3), (2,))

    def send_kv(batch):
        send_batch(
            kv_refs,
            lambda which: kv_in.at[which, my_rows, :],
            lambda which: kv_sem,
            batch_sem.at[0, batch],
            batches[batch],
        )

    def send_qs(batch):
        send_batch(
            qs_refs,
            lambda which: qs_in.at[s, which],
            lambda which: qs_sem.at[which, s],
            batch_sem.at[1, batch],
            batches[batch],
        )

    def batch_left(kind, batch):
        peers = 5 if batch == 0 else 2
        wait_bytes(qs_in.at[pl.ds(0, peers)], batch_sem.at[kind, batch])

    send_kv(0)

    always = z >= 0
    half = z_count // 2

    def pass_on(buffer, sems, left_sem, pair_left, pair_sem, block, up, down):
        held = buffer.at[c, block]

        def pass_to(z_to):
            remote(held, held, left_sem, sems.at[block], {"exp": lax.rem(z_to, z_count)}).start()

        if up is not None:

            @pl.when(up)
            def _up():
                pass_to(z + 1)

        if down is not None:

            @pl.when(down)
            def _down():
                pass_to(z + z_count - 1)

        remote(held, held, pair_left, pair_sem, {"seq": pair}).start()

    def ring_step(ring, step):
        buffer, sems = ring[0], ring[1]
        below = lax.rem(z + z_count - step, z_count)
        above = lax.rem(z + step, z_count)
        wait_bytes(buffer.at[c, below], sems.at[below])
        if step == half:
            pass_on(*ring, below, None, None)
            return
        pass_on(*ring, below, always if step < half - 1 else c == 0, None)
        wait_bytes(buffer.at[c, above], sems.at[above])
        pass_on(*ring, above, None, always if step < half - 1 else c == 1)

    gate_ring = (gate_up, ring_g_sem, sent.at[13], sent.at[14], pair_g_sem)
    down_ring = (weights, ring_sem, sent.at[7], sent.at[8], pair_w_sem)

    wait_bytes(gate_up.at[c, z], near_g_sem)
    wait_bytes(info_y, info_sem.at[0])
    pltpu.make_async_copy(info_y, info_x.at[x], info_sem.at[1]).start()

    def info_to_x(step, carry):
        remote(
            info_y,
            info_x.at[x],
            sent.at[6],
            info_sem.at[1],
            {"dp": lax.rem(x + step, x_count)},
        ).start()
        return carry

    lax.fori_loop(1, x_count, info_to_x, 0)
    pass_on(*gate_ring, z, always, always)
    send_kv(1)
    ring_step(gate_ring, 1)
    wait_bytes(weights.at[c, z], near_w_sem)
    pass_on(*down_ring, z, always, always)
    batch_left(0, 0)
    send_qs(0)
    ring_step(gate_ring, 2)
    ring_step(gate_ring, 3)
    batch_left(0, 1)
    send_qs(1)

    wait_bytes(info_x, info_sem.at[1])
    group = x_count * y_count
    chip_rows = group * slots
    def make_pick(source, carry):
        slot_iota = lax.broadcasted_iota(jnp.int32, (picks.shape[2], tok_rows), 0).astype(
            jnp.float32
        )
        named_here = info_x[source // y_count, source % y_count]
        pick = (slot_iota == named_here[0:1, :]) | (slot_iota == named_here[1:2, :])
        picks[source] = jnp.where(pick, 1.0, 0.0).astype(jnp.bfloat16).T
        return carry

    wait_bytes(kv_in, kv_sem)

    length = s_count * tok_rows
    lane = lax.broadcasted_iota(jnp.int32, (length, HEAD_DIM), 1)
    ones_column = jnp.where(lane == 0, 1.0, 0.0).astype(jnp.bfloat16)
    exponent_scale = 1.0 / (math.sqrt(HEAD_DIM) * math.log(2.0))
    gate_row = attn_gate_ref[:, my_cols].astype(jnp.float32)
    scale_row = ffn_scale_ref[:, my_cols].astype(jnp.float32)
    two = 2 * tok_rows
    tail_lane = lax.broadcasted_iota(jnp.int32, (two, LANES), 1)

    def with_tail(values, square, tail):
        high = square.astype(jnp.bfloat16).astype(jnp.float32)
        extra = jnp.where(tail == 0, high, jnp.where(tail == 1, square - high, 0.0))
        return jnp.concatenate([values, extra], axis=1)

    def add_core_part(step):
        wait_bytes(core_recv.at[step], core_sem.at[step])
        total = own_part[step] + core_recv[step].astype(jnp.float32)
        square = total[:, rank : rank + 1] + total[:, rank + 1 : rank + 2]
        return total[:, :rank], square

    def send_part(step):
        values, square = add_core_part(step)
        part_send[step - 1] = with_tail(values, square, tail_lane[:tok_rows]).astype(jnp.bfloat16)
        distance = near_order(step)
        y_to = lax.rem(y + y_count - distance, y_count)
        remote(
            part_send.at[step - 1],
            part_recv.at[step - 1],
            sent.at[10],
            part_sem,
            {"seq": 2 * y_to + c},
        ).start()

    def one_chip(step, carry):
        y_from = lax.rem(y + y_count - near_order(step), y_count)

        @pl.when(step > 1)
        def _previous():
            send_part(step - 1)

        def wait_rows(which):
            for core in range(2):
                s_from = 2 * y_from + core
                wait_bytes(qs_in.at[s_from, which], qs_sem.at[which, s_from])

        wait_rows(0)
        both = pl.ds(2 * y_from, 2)
        square = jnp.zeros((two, 1), jnp.float32)
        for head in range(heads_here):
            part = slice(head * HEAD_DIM, (head + 1) * HEAD_DIM)
            scores = lax.dot_general(
                qs_in[both, 0, :, part].reshape(two, HEAD_DIM),
                kv_in[0, :, part],
                (((1,), (1,)), ((), ())),
                preferred_element_type=jnp.float32,
            )
            row_max = jnp.max(scores, axis=-1, keepdims=True)
            raised = jnp.exp2((scores - row_max) * exponent_scale).astype(jnp.bfloat16)
            value_ones = jnp.concatenate([kv_in[1, :, part], ones_column], axis=1)
            mixed = jnp.dot(raised, value_ones, preferred_element_type=jnp.float32)
            mixed = (mixed[:, :HEAD_DIM] / mixed[:, HEAD_DIM : HEAD_DIM + 1]).astype(jnp.bfloat16)
            att_out[both, :, part] = mixed.reshape(2, tok_rows, HEAD_DIM)

        wait_rows(1)
        for head in range(heads_here):
            part = slice(head * HEAD_DIM, (head + 1) * HEAD_DIM)
            mixed = att_out[both, :, part].reshape(two, HEAD_DIM)
            residual = qs_in[both, 1, :, part].reshape(two, HEAD_DIM).astype(
                jnp.float32
            ) + gate_row[:, part] * mixed.astype(jnp.float32)
            modulated[:, part] = (residual * scale_row[:, part]).astype(jnp.bfloat16)
            square = square + jnp.sum(residual * residual, axis=1, keepdims=True)
        product = jnp.dot(modulated[...], basis_ref[...], preferred_element_type=jnp.float32)
        partial[...] = with_tail(product, square, tail_lane).reshape(partial.shape)
        own_part[step] = partial[c]
        core_send[step] = partial[other_c].astype(jnp.bfloat16)
        remote(
            core_send.at[step], core_recv.at[step], sent.at[9], core_sem.at[step], {"seq": pair}
        ).start()
        return carry

    def after_chip(step, carry):
        one_chip(step, carry)

        @pl.when(step == 0)
        def _last_batch():
            ring_step(gate_ring, half)

        @pl.when(step == 2)
        def _ring_one():
            ring_step(down_ring, 1)

        return carry

    lax.fori_loop(0, y_count, after_chip, 0)
    send_part(y_count - 1)
    ring_step(down_ring, 2)

    def send_attended(index, carry):
        s_to = lax.rem(s + index, s_count)

        @pl.when(s_to == s)
        def _keep():
            pltpu.make_async_copy(att_out.at[s_to], attended.at[:, my_cols], att_sem).start()

        @pl.when(s_to != s)
        def _send():
            remote(
                att_out.at[s_to], attended.at[:, my_cols], sent.at[11], att_sem, {"seq": s_to}
            ).start()

        return carry

    values, square = add_core_part(0)
    wait_bytes(part_recv, part_sem)
    for step in range(y_count - 1):
        arrived = part_recv[step].astype(jnp.float32)
        values = values + arrived[:, :rank]
        square = square + arrived[:, rank : rank + 1] + arrived[:, rank + 1 : rank + 2]
    low_rank = (values / jnp.sqrt(square / model_width + epsilon)).astype(jnp.bfloat16)

    def pick_rows(y_to):
        row = lax.broadcasted_iota(jnp.int32, (z_count * slots, tok_rows), 0)
        slot_here = (((row // slots) * y_count + y_to) * slots + row % slots).astype(jnp.float32)
        pick = (slot_here == info_own[0:1, :]) | (slot_here == info_own[1:2, :])
        pick = jnp.where(pick, 1.0, 0.0).astype(jnp.bfloat16)
        return jnp.dot(pick, low_rank, preferred_element_type=jnp.float32).astype(jnp.bfloat16)

    chip_slots = 2 * slots

    def forward_rows(y_from):
        def to_x(x_step, inner):
            x_to = lax.rem(x + near_order(x_step), x_count)
            rows = pl.ds(pl.multiple_of(x_to * chip_slots, chip_slots), chip_slots)
            remote(
                near_rows.at[y_from, rows, :],
                slot_rows.at[x, y_from],
                sent.at[5],
                slot_sem,
                {"dp": x_to},
            ).start()
            return inner

        lax.fori_loop(1, x_count, to_x, 0)
        own = pl.ds(pl.multiple_of(x * chip_slots, chip_slots), chip_slots)
        pltpu.make_async_copy(near_rows.at[y_from, own, :], slot_rows.at[x, y_from], slot_sem).start()

    for step in range(1, y_count):
        y_to = lax.rem(y + near_order(step), y_count)
        out_rows[step - 1] = pick_rows(y_to)
        remote(
            out_rows.at[step - 1],
            near_rows.at[y],
            sent.at[12],
            near_sem.at[y],
            {"seq": 2 * y_to + c},
        ).start()


    near_rows[y] = pick_rows(y)
    forward_rows(y)

    def forward_near(step, carry):
        y_from = lax.rem(y + y_count - near_order(step), y_count)
        lax.fori_loop(4 * step - 4, 4 * step, make_pick, 0)
        wait_bytes(near_rows.at[y_from], near_sem.at[y_from])
        forward_rows(y_from)
        return lax.fori_loop(2 * step, 2 * step + 2, send_attended, carry)

    lax.fori_loop(0, 2, send_attended, 0)
    named_all = info_x[...].reshape(group, info_x.shape[2], tok_rows)
    place = lax.broadcasted_iota(jnp.int32, (group, slots, tok_rows), 1)
    for which in range(2):
        slot_here = (place + ((2 * x + which) * y_count + y) * slots).astype(jnp.float32)
        routed = jnp.where(
            slot_here == named_all[:, 0:1, :], named_all[:, 2:3, :], 0.0
        ) + jnp.where(slot_here == named_all[:, 1:2, :], named_all[:, 3:4, :], 0.0)
        slot_weight[which] = jnp.sum(routed, axis=2, keepdims=True).reshape(chip_rows, 1)

    lax.fori_loop(1, y_count, forward_near, 0)

    ring_step(down_ring, 3)
    wait_bytes(gate_up.at[other_c], pair_g_sem)
    wait_bytes(slot_rows, slot_sem)
    expert = lax.broadcasted_iota(jnp.int32, (chip_rows, 1), 0) % slots // CAP

    for twin_here in range(2):
        rows = slot_rows[:, :, pl.ds(twin_here * slots, slots), :].reshape(chip_rows, rank)
        both_halves = jnp.zeros((chip_rows, gate_up.shape[5]), jnp.float32)
        for which in range(4):
            product = jnp.dot(
                rows,
                gate_up[which // 2, :, twin_here, which % 2].reshape(rank, gate_up.shape[5]),
                preferred_element_type=jnp.float32,
            )
            both_halves = jnp.where(expert == which, product, both_halves)
        gate, up = both_halves[:, :LANES], both_halves[:, LANES:]
        hidden = gate / (1.0 + jnp.exp(-gate)) * up * slot_weight[twin_here]
        hidden_all[x, y, twin_here] = hidden.astype(jnp.bfloat16)
        held = hidden_all.at[x, y, twin_here]

        def hidden_near(step, carry):
            if twin_here == 0:
                device = {"dp": lax.rem(x + near_order(step), x_count)}
            else:
                device = {"seq": 2 * lax.rem(y + near_order(step), y_count) + c}
            remote(held, held, sent.at[15], hid_sem.at[twin_here], device).start()
            return carry

        lax.fori_loop(1, x_count, hidden_near, 0)

    lax.fori_loop(4 * (y_count - 1), group, make_pick, 0)
    wait_bytes(hidden_all.at[pl.ds(0, x_count - 1), y, 0], hid_sem.at[0])

    def hidden_to_y(step, carry):
        held = hidden_all.at[:, y, 0]
        y_to = lax.rem(y + near_order(step), y_count)
        remote(held, held, sent.at[16], hid_y_sem.at[y], {"seq": 2 * y_to + c}).start()
        return carry

    lax.fori_loop(1, y_count, hidden_to_y, 0)
    wait_bytes(hidden_all.at[x, pl.ds(0, y_count - 1), 1], hid_sem.at[1])

    def hidden_to_x(step, carry):
        held = hidden_all.at[x, :, 1]
        x_to = lax.rem(x + near_order(step), x_count)
        remote(held, held, sent.at[18], hid_x_sem.at[x], {"dp": x_to}).start()
        return carry

    lax.fori_loop(1, x_count, hidden_to_x, 0)
    ring_step(down_ring, half)
    wait_bytes(weights.at[other_c], pair_w_sem)

    chip_expert = lax.broadcasted_iota(jnp.int32, (chip_rows, LANES), 0) % slots // CAP

    masks = [
        jnp.where(chip_expert == which, 1.0, 0.0).astype(jnp.bfloat16) for which in range(4)
    ]

    def down_block(x_from, y_from, twin_here):
        held = hidden_all[x_from, y_from, twin_here]
        z_from = 2 * x_from + twin_here
        masked = [held * mask for mask in masks]
        product = jnp.dot(
            jnp.concatenate(masked[:2], axis=1),
            weights[0, z_from, y_from],
            preferred_element_type=jnp.float32,
        ) + jnp.dot(
            jnp.concatenate(masked[2:], axis=1),
            weights[1, z_from, y_from],
            preferred_element_type=jnp.float32,
        )
        to = pl.ds(pl.multiple_of((z_from * y_count + y_from) * slots, slots), slots)
        slot_out[:, to, :] = product.astype(jnp.bfloat16).reshape(group, slots, cols)

    def down_step(step, carry):
        y_from = lax.rem(y + y_count - near_order(step), y_count)
        x_from = lax.rem(x + x_count - near_order(step), x_count)

        @pl.when(step > 0)
        def _arrive_y():
            wait_bytes(hidden_all.at[:, y_from, 0], hid_y_sem.at[y_from])

        def down_first(other, inner):
            down_block(other, y_from, 0)
            return inner

        lax.fori_loop(0, x_count, down_first, 0)

        @pl.when(step > 0)
        def _arrive_x():
            wait_bytes(hidden_all.at[x_from, :, 1], hid_x_sem.at[x_from])

        def down_second(other, inner):
            down_block(x_from, other, 1)
            return inner

        lax.fori_loop(0, y_count, down_second, 0)
        return carry

    lax.fori_loop(0, y_count, down_step, 0)

    mine = x * y_count + y

    def mix_one(step, carry):
        x_to = lax.rem(x + (step + 1) // y_count, x_count)
        y_to = lax.rem(y + step + 1, y_count)
        to = x_to * y_count + y_to
        mixed = jnp.dot(picks[to], slot_out[to], preferred_element_type=jnp.float32)
        mix_out[to] = mixed.astype(jnp.bfloat16)

        def give(first, last):
            source = mix_out.at[to, :, first:last]
            target = mix_in.at[mine, :, first:last]

            @pl.when(to == mine)
            def _keep():
                pltpu.make_async_copy(source, target, mix_sem.at[mine]).start()

            @pl.when(to != mine)
            def _send():
                remote(
                    source,
                    target,
                    sent.at[17],
                    mix_sem.at[mine],
                    {"dp": x_to, "seq": 2 * y_to + c},
                ).start()

        @pl.when(y % 2 == c)
        def _whole():
            give(0, cols)

        @pl.when((y % 2 == 0) & (c == 1))
        def _low():
            give(0, cols - LANES)

        @pl.when((y % 2 == 1) & (c == 0))
        def _high():
            give(LANES, cols)

        return carry

    lax.fori_loop(0, group, mix_one, 0)

    wait_bytes(stream_own, own_sem)
    wait_bytes(attended, att_sem)

    def finish(core):
        for block in range(s_count):
            part = slice(block * head_cols, (block + 1) * head_cols)
            even, odd = 2 * block, 2 * block + 1
            if core == 0:
                wait_bytes(mix_in.at[even], mix_sem.at[even])
                wait_bytes(mix_in.at[odd, :, LANES:cols], mix_sem.at[odd])
                mixed = [mix_in[even], mix_in[odd, :, LANES:]]
            else:
                wait_bytes(mix_in.at[even, :, 0 : cols - LANES], mix_sem.at[even])
                wait_bytes(mix_in.at[odd], mix_sem.at[odd])
                mixed = [mix_in[even, :, : cols - LANES], mix_in[odd]]
            mixed = jnp.concatenate(mixed, axis=1)
            residual = stream_own[:, part].astype(jnp.float32) + attn_gate_ref[:, part].astype(
                jnp.float32
            ) * attended[:, part].astype(jnp.float32)
            output_ref[:, part] = (
                residual + ffn_gate_ref[:, part].astype(jnp.float32) * mixed.astype(jnp.float32)
            ).astype(jnp.bfloat16)

    for core in range(2):

        @pl.when(c == core)
        def _finish():
            finish(core)

    wait_bytes(info_y.at[pl.ds(0, y_count - 1)], sent.at[0])
    wait_bytes(weights.at[0, 0, pl.ds(0, y_count - 1)], sent.at[1])
    batch_left(1, 0)
    batch_left(1, 1)

    @pl.when(z // 2 == x)
    def _spread_done():
        wait_bytes(gate_up.at[0, pl.ds(0, z_count - 1), 0], sent.at[4])

    wait_bytes(slot_rows.at[pl.ds(0, x_count - 1)], sent.at[5])
    wait_bytes(info_x.at[pl.ds(0, x_count - 1)], sent.at[6])
    wait_bytes(weights.at[0, pl.ds(0, z_count - 1)], sent.at[7])
    wait_bytes(weights.at[0], sent.at[8])
    wait_bytes(core_send, sent.at[9])
    wait_bytes(part_send, sent.at[10])
    wait_bytes(att_out.at[pl.ds(0, s_count - 1)], sent.at[11])
    wait_bytes(out_rows, sent.at[12])
    wait_bytes(gate_up.at[0, pl.ds(0, z_count - 1)], sent.at[13])
    wait_bytes(gate_up.at[0], sent.at[14])
    wait_bytes(hidden_all.at[pl.ds(0, 2), pl.ds(0, y_count - 1), 0], sent.at[15])
    wait_bytes(hidden_all.at[:, pl.ds(0, y_count - 1), 0], sent.at[16])
    wait_bytes(hidden_all.at[pl.ds(0, x_count - 1), :, 1], sent.at[18])

    @pl.when(y % 2 == c)
    def _whole_done():
        wait_bytes(mix_out.at[pl.ds(0, group - 1)], sent.at[17])

    @pl.when(y % 2 != c)
    def _part_done():
        wait_bytes(mix_out.at[pl.ds(0, group - 1), :, 0 : cols - LANES], sent.at[17])


def on_device(
    query_rows,
    key_rows,
    value_rows,
    stream,
    shared_basis,
    expert_gate_up,
    expert_down,
    attn_gate,
    ffn_scale,
    ffn_gate,
    expert_ids,
    route_weights,
):
    x_count, z_count, s_count = (lax.axis_size(name) for name in ("dp", "exp", "seq"))
    y_count = s_count // 2
    tok_rows, model_width = stream.shape
    experts_here, hidden_cols, _ = expert_down.shape
    expert_total = z_count * s_count * experts_here
    rank = shared_basis.shape[1]
    head_cols = model_width // s_count
    cols = 384
    slots = 4 * CAP
    length = s_count * tok_rows
    group = x_count * y_count

    vmem = pl.BlockSpec(memory_space=pltpu.VMEM)
    anywhere = pl.BlockSpec(memory_space=pl.ANY)
    bf16, f32 = jnp.bfloat16, jnp.float32
    wide = rank + LANES
    dma = pltpu.SemaphoreType.DMA
    return pl.pallas_call(
        block_kernel,
        out_shape=jax.ShapeDtypeStruct((tok_rows, model_width), bf16),
        in_specs=[anywhere] * 6 + [vmem] * 6,
        out_specs=vmem,
        scratch_shapes=[
            pltpu.VMEM((2, length, head_cols), bf16),
            pltpu.VMEM((s_count, 2, tok_rows, head_cols), bf16),
            pltpu.VMEM((tok_rows, model_width), bf16),
            pltpu.VMEM((s_count, tok_rows, head_cols), bf16),
            pltpu.VMEM((tok_rows, model_width), bf16),
            pltpu.VMEM((2 * tok_rows, head_cols), bf16),
            pltpu.VMEM((2, tok_rows, wide), f32),
            pltpu.VMEM((y_count, tok_rows, wide), f32),
            pltpu.VMEM((y_count, tok_rows, wide), bf16),
            pltpu.VMEM((y_count, tok_rows, wide), bf16),
            pltpu.VMEM((y_count - 1, tok_rows, wide), bf16),
            pltpu.VMEM((y_count - 1, tok_rows, wide), bf16),
            pltpu.VMEM((y_count - 1, z_count * slots, rank), bf16),
            pltpu.VMEM((y_count, z_count * slots, rank), bf16),
            pltpu.VMEM((x_count, y_count, 2 * slots, rank), bf16),
            pltpu.VMEM(
                (2, z_count, 2, experts_here, rank // z_count, 2 * hidden_cols), bf16
            ),
            pltpu.VMEM((x_count, y_count, 2, group * slots, hidden_cols), bf16),
            pltpu.VMEM((2, z_count, y_count, experts_here * hidden_cols, cols), bf16),
            pltpu.VMEM((group, z_count * y_count * slots, cols), bf16),
            pltpu.VMEM((group, tok_rows, cols), bf16),
            pltpu.VMEM((group, tok_rows, cols), bf16),
            pltpu.VMEM((8, tok_rows), f32),
            pltpu.VMEM((y_count, 8, tok_rows), f32),
            pltpu.VMEM((x_count, y_count, 8, tok_rows), f32),
            pltpu.VMEM((2, group * slots, 1), f32),
            pltpu.VMEM((group, tok_rows, group * 2 * slots), bf16),
            dma,
            dma((2, s_count)),
            dma((2, 2)),
            dma,
            dma((2,)),
            dma,
            dma((z_count,)),
            dma,
            dma,
            dma((z_count,)),
            dma,
            dma((y_count,)),
            dma,
            dma,
            dma((y_count,)),
            dma,
            dma((2,)),
            dma((y_count,)),
            dma((x_count,)),
            dma((group,)),
            dma((19,)),
        ],
        compiler_params=pltpu.CompilerParams(
            collective_id=0, has_side_effects=True, vmem_limit_bytes=62 * 1024 * 1024
        ),
        name="block",
    )(
        query_rows,
        key_rows,
        value_rows,
        stream,
        expert_down,
        expert_gate_up,
        shared_basis,
        attn_gate,
        ffn_scale,
        ffn_gate,
        expert_ids.T,
        route_weights.T,
    )


def solution(mesh):
    in_specs = (
        P(("dp", "exp", "seq"), None),
        P(("dp", "exp", "seq"), None),
        P(("dp", "exp", "seq"), None),
        P(("dp", "exp", "seq"), None),
        P("seq", None),
        P(("exp", "seq"), None, None),
        P(("exp", "seq"), None, None),
        P(("dp", "exp"), None),
        P(("dp", "exp"), None),
        P(("dp", "exp"), None),
        P(("dp", "exp", "seq"), None),
        P(("dp", "exp", "seq"), None),
    )
    out_specs = P(("dp", "exp", "seq"), None)
    return jax.shard_map(
        on_device, mesh=mesh, in_specs=in_specs, out_specs=out_specs, check_vma=False
    )
```

```python
import functools
import math

import jax
import jax.numpy as jnp
from jax import lax
from jax.experimental import pallas as pl
from jax.experimental.pallas import tpu as pltpu
from jax.sharding import PartitionSpec as P

HEAD_DIM = 128
LANES = 128
MESH = pl.DeviceIdType.MESH
epsilon = 1e-06
CAP = 4


def block_kernel(
    query_ref,
    key_ref,
    value_ref,
    stream_ref,
    down_ref,
    gate_up_ref,
    basis_ref,
    attn_gate_ref,
    ffn_scale_ref,
    ffn_gate_ref,
    ids_ref,
    route_ref,
    output_ref,
    kv_in,
    qs_in,
    stream_own,
    att_out,
    attended,
    modulated,
    partial,
    own_part,
    core_send,
    core_recv,
    part_send,
    part_recv,
    out_rows,
    near_rows,
    slot_rows,
    gate_up,
    hidden_all,
    weights,
    slot_out,
    mix_out,
    mix_in,
    info_own,
    info_y,
    info_x,
    slot_weight,
    picks,
    kv_sem,
    qs_sem,
    batch_sem,
    own_sem,
    info_sem,
    near_w_sem,
    ring_sem,
    pair_w_sem,
    near_g_sem,
    ring_g_sem,
    pair_g_sem,
    core_sem,
    part_sem,
    att_sem,
    near_sem,
    slot_sem,
    hid_sem,
    hid_y_sem,
    hid_x_sem,
    mix_sem,
    sent,
):
    x_count, z_count, s_count = (lax.axis_size(name) for name in ("dp", "exp", "seq"))
    y_count = s_count // 2
    x, z, s = (lax.axis_index(name) for name in ("dp", "exp", "seq"))
    y, c = s // 2, s % 2
    other_c = 1 - c
    pair = 2 * y + other_c
    tok_rows, model_width = attended.shape
    head_cols = kv_in.shape[2]
    heads_here = head_cols // HEAD_DIM
    cols = weights.shape[4]
    rank = near_rows.shape[2]
    slots = 4 * CAP
    quarter = model_width // x_count

    def remote(src, dst, send_sem, recv_sem, device):
        return pltpu.make_async_remote_copy(
            src_ref=src,
            dst_ref=dst,
            send_sem=send_sem,
            recv_sem=recv_sem,
            device_id=device,
            device_id_type=MESH,
        )

    def wait_bytes(ref, sem):
        pltpu.make_async_copy(ref, ref, sem).wait()

    def first_column(y_to):
        return pl.multiple_of(x * quarter + (y_to // 2) * head_cols + (y_to % 2) * 256, LANES)

    def near_order(step):
        return step + step // 2 - 2 * (step // 3)

    barrier = pltpu.get_barrier_semaphore()

    def greet(device):
        pl.semaphore_signal(barrier, inc=1, device_id=device, device_id_type=MESH)

    def greet_seq(step, carry):
        greet({"seq": lax.rem(s + step, s_count)})
        return carry

    def greet_z(step, carry):
        greet({"exp": lax.rem(z + step, z_count)})
        return carry

    def greet_x(step, carry):
        greet({"dp": lax.rem(x + step, x_count)})

        def greet_xy(y_step, inner):
            greet(
                {
                    "dp": lax.rem(x + step, x_count),
                    "seq": 2 * lax.rem(y + y_step, y_count) + c,
                }
            )
            return inner

        return lax.fori_loop(1, y_count, greet_xy, carry)

    lax.fori_loop(1, s_count, greet_seq, 0)
    lax.fori_loop(1, z_count, greet_z, 0)
    lax.fori_loop(1, x_count, greet_x, 0)

    my_rows = pl.ds(pl.multiple_of(s * tok_rows, tok_rows), tok_rows)
    my_cols = pl.ds(pl.multiple_of(s * head_cols, head_cols), head_cols)
    kv_refs = (key_ref, value_ref)
    qs_refs = (query_ref, stream_ref)
    for which in range(2):
        pltpu.make_async_copy(
            kv_refs[which].at[:, my_cols], kv_in.at[which, my_rows, :], kv_sem
        ).start()
        pltpu.make_async_copy(
            qs_refs[which].at[:, my_cols], qs_in.at[s, which], qs_sem.at[which, s]
        ).start()
        pltpu.make_async_copy(
            down_ref.at[which, :, pl.ds(first_column(y), cols)],
            weights.at[c, z, y, pl.ds(which * LANES, LANES), :],
            near_w_sem,
        ).start()
    pltpu.make_async_copy(stream_ref, stream_own, own_sem).start()

    rank_part = rank // z_count
    twin = z - 2 * x

    @pl.when(z // 2 == x)
    def _own_gate_up():
        part = pl.ds(pl.multiple_of(z * rank_part, rank_part), rank_part)
        pltpu.make_async_copy(
            gate_up_ref.at[:, part, :], gate_up.at[c, z, twin], near_g_sem
        ).start()

    entries = 2 * tok_rows
    experts = 4 * z_count * y_count
    ids_row = jnp.concatenate([ids_ref[0:1, :], ids_ref[1:2, :]], axis=1)
    named = lax.broadcasted_iota(jnp.int32, (experts, entries), 0) == ids_row
    entry = [lax.broadcasted_iota(jnp.int32, (entries, entries), axis) for axis in (0, 1)]
    entry = [2 * (one % tok_rows) + one // tok_rows for one in entry]
    before = jnp.where(entry[0] < entry[1], 1.0, 0.0).astype(jnp.bfloat16)
    counts = jnp.dot(
        jnp.where(named, 1.0, 0.0).astype(jnp.bfloat16), before, preferred_element_type=jnp.float32
    )
    slot_ids = (
        jnp.sum(jnp.where(named, counts, 0.0), axis=0, keepdims=True)
        + ids_row.astype(jnp.float32) * CAP
    )
    info_row = lax.broadcasted_iota(jnp.int32, info_own.shape, 0)
    info = jnp.where(info_row == 2, route_ref[0:1, :], 0.0)
    info = jnp.where(info_row == 3, route_ref[1:2, :], info)
    info = jnp.where(info_row == 0, slot_ids[:, :tok_rows], info)
    info_own[...] = jnp.where(info_row == 1, slot_ids[:, tok_rows:], info)
    pltpu.make_async_copy(info_own, info_y.at[y], info_sem.at[0]).start()

    pl.semaphore_wait(barrier, s_count - 1 + z_count - 1 + (x_count - 1) * y_count)

    def info_to_y(step, carry):
        y_to = lax.rem(y + step, y_count)
        remote(
            info_own, info_y.at[y], sent.at[0], info_sem.at[0], {"seq": 2 * y_to + c}
        ).start()
        return carry

    lax.fori_loop(1, y_count, info_to_y, 0)

    def near_first(step, carry):
        y_to = lax.rem(y + near_order(step), y_count)
        device = {"seq": 2 * y_to + c}
        for which in range(2):
            remote(
                down_ref.at[which, :, pl.ds(first_column(y_to), cols)],
                weights.at[c, z, y, pl.ds(which * LANES, LANES), :],
                sent.at[1],
                near_w_sem,
                device,
            ).start()
        return carry

    lax.fori_loop(1, y_count, near_first, 0)

    @pl.when(z // 2 == x)
    def _spread_gate_up():
        def to_z(step, carry):
            z_to = lax.rem(z + step, z_count)
            part = pl.ds(pl.multiple_of(z_to * rank_part, rank_part), rank_part)
            remote(
                gate_up_ref.at[:, part, :],
                gate_up.at[c, z_to, twin],
                sent.at[4],
                near_g_sem,
                {"exp": z_to},
            ).start()
            return carry

        lax.fori_loop(1, z_count, to_z, 0)


    def send_batch(refs, slot_of, sem, send_sem, distances):
        for which in range(2):

            def one_copy(index, carry):
                s_to = 2 * lax.rem(y + distances[0] + 2 * (index % len(distances)), y_count) + (
                    index // len(distances)
                )
                columns = pl.ds(pl.multiple_of(s_to * head_cols, head_cols), head_cols)
                remote(
                    refs[which].at[:, columns], slot_of(which), send_sem, sem(which), {"seq": s_to}
                ).start()
                return carry

            if len(distances) == 2:
                columns = pl.ds(pl.multiple_of(pair * head_cols, head_cols), head_cols)
                remote(
                    refs[which].at[:, columns], slot_of(which), send_sem, sem(which), {"seq": pair}
                ).start()
            lax.fori_loop(0, 2 * len(distances), one_copy, 0)

    batches = ((1, 3), (2,))

    def send_kv(batch):
        send_batch(
            kv_refs,
            lambda which: kv_in.at[which, my_rows, :],
            lambda which: kv_sem,
            batch_sem.at[0, batch],
            batches[batch],
        )

    def send_qs(batch):
        send_batch(
            qs_refs,
            lambda which: qs_in.at[s, which],
            lambda which: qs_sem.at[which, s],
            batch_sem.at[1, batch],
            batches[batch],
        )

    def batch_left(kind, batch):
        peers = 5 if batch == 0 else 2
        wait_bytes(qs_in.at[pl.ds(0, peers)], batch_sem.at[kind, batch])

    send_kv(0)
    send_kv(1)

    always = z >= 0
    half = z_count // 2

    def pass_on(buffer, sems, left_sem, pair_left, pair_sem, block, up, down):
        held = buffer.at[c, block]

        def pass_to(z_to):
            remote(held, held, left_sem, sems.at[block], {"exp": lax.rem(z_to, z_count)}).start()

        if up is not None:

            @pl.when(up)
            def _up():
                pass_to(z + 1)

        if down is not None:

            @pl.when(down)
            def _down():
                pass_to(z + z_count - 1)

        remote(held, held, pair_left, pair_sem, {"seq": pair}).start()

    def ring_step(ring, step):
        buffer, sems = ring[0], ring[1]
        below = lax.rem(z + z_count - step, z_count)
        above = lax.rem(z + step, z_count)
        wait_bytes(buffer.at[c, below], sems.at[below])
        if step == half:
            pass_on(*ring, below, None, None)
            return
        pass_on(*ring, below, always if step < half - 1 else c == 0, None)
        wait_bytes(buffer.at[c, above], sems.at[above])
        pass_on(*ring, above, None, always if step < half - 1 else c == 1)

    gate_ring = (gate_up, ring_g_sem, sent.at[13], sent.at[14], pair_g_sem)
    down_ring = (weights, ring_sem, sent.at[7], sent.at[8], pair_w_sem)

    wait_bytes(gate_up.at[c, z], near_g_sem)
    wait_bytes(info_y, info_sem.at[0])
    pltpu.make_async_copy(info_y, info_x.at[x], info_sem.at[1]).start()

    def info_to_x(step, carry):
        remote(
            info_y,
            info_x.at[x],
            sent.at[6],
            info_sem.at[1],
            {"dp": lax.rem(x + step, x_count)},
        ).start()
        return carry

    lax.fori_loop(1, x_count, info_to_x, 0)
    pass_on(*gate_ring, z, always, always)
    wait_bytes(weights.at[c, z], near_w_sem)
    pass_on(*down_ring, z, always, always)
    batch_left(0, 0)
    send_qs(0)
    ring_step(gate_ring, 1)
    ring_step(gate_ring, 2)
    batch_left(0, 1)
    send_qs(1)
    ring_step(gate_ring, 3)

    wait_bytes(info_x, info_sem.at[1])
    group = x_count * y_count
    chip_rows = group * slots
    def make_pick(source, carry):
        slot_iota = lax.broadcasted_iota(jnp.int32, (picks.shape[2], tok_rows), 0).astype(
            jnp.float32
        )
        named_here = info_x[source // y_count, source % y_count]
        pick = (slot_iota == named_here[0:1, :]) | (slot_iota == named_here[1:2, :])
        picks[source] = jnp.where(pick, 1.0, 0.0).astype(jnp.bfloat16).T
        return carry

    wait_bytes(kv_in, kv_sem)

    length = s_count * tok_rows
    lane = lax.broadcasted_iota(jnp.int32, (length, HEAD_DIM), 1)
    ones_column = jnp.where(lane == 0, 1.0, 0.0).astype(jnp.bfloat16)
    exponent_scale = 1.0 / (math.sqrt(HEAD_DIM) * math.log(2.0))
    gate_row = attn_gate_ref[:, my_cols].astype(jnp.float32)
    scale_row = ffn_scale_ref[:, my_cols].astype(jnp.float32)
    two = 2 * tok_rows
    tail_lane = lax.broadcasted_iota(jnp.int32, (two, LANES), 1)

    def with_tail(values, square, tail):
        high = square.astype(jnp.bfloat16).astype(jnp.float32)
        extra = jnp.where(tail == 0, high, jnp.where(tail == 1, square - high, 0.0))
        return jnp.concatenate([values, extra], axis=1)

    def add_core_part(step):
        wait_bytes(core_recv.at[step], core_sem.at[step])
        total = own_part[step] + core_recv[step].astype(jnp.float32)
        square = total[:, rank : rank + 1] + total[:, rank + 1 : rank + 2]
        return total[:, :rank], square

    def send_part(step):
        values, square = add_core_part(step)
        part_send[step - 1] = with_tail(values, square, tail_lane[:tok_rows]).astype(jnp.bfloat16)
        distance = near_order(step)
        y_to = lax.rem(y + y_count - distance, y_count)
        remote(
            part_send.at[step - 1],
            part_recv.at[step - 1],
            sent.at[10],
            part_sem,
            {"seq": 2 * y_to + c},
        ).start()

    def one_chip(step, carry):
        y_from = lax.rem(y + y_count - near_order(step), y_count)

        @pl.when(step > 1)
        def _previous():
            send_part(step - 1)

        def wait_rows(which):
            for core in range(2):
                s_from = 2 * y_from + core
                wait_bytes(qs_in.at[s_from, which], qs_sem.at[which, s_from])

        wait_rows(0)
        both = pl.ds(2 * y_from, 2)
        square = jnp.zeros((two, 1), jnp.float32)
        for head in range(heads_here):
            part = slice(head * HEAD_DIM, (head + 1) * HEAD_DIM)
            scores = lax.dot_general(
                qs_in[both, 0, :, part].reshape(two, HEAD_DIM),
                kv_in[0, :, part],
                (((1,), (1,)), ((), ())),
                preferred_element_type=jnp.float32,
            )
            row_max = jnp.max(scores, axis=-1, keepdims=True)
            raised = jnp.exp2((scores - row_max) * exponent_scale).astype(jnp.bfloat16)
            value_ones = jnp.concatenate([kv_in[1, :, part], ones_column], axis=1)
            mixed = jnp.dot(raised, value_ones, preferred_element_type=jnp.float32)
            mixed = (mixed[:, :HEAD_DIM] / mixed[:, HEAD_DIM : HEAD_DIM + 1]).astype(jnp.bfloat16)
            att_out[both, :, part] = mixed.reshape(2, tok_rows, HEAD_DIM)

        wait_rows(1)
        for head in range(heads_here):
            part = slice(head * HEAD_DIM, (head + 1) * HEAD_DIM)
            mixed = att_out[both, :, part].reshape(two, HEAD_DIM)
            residual = qs_in[both, 1, :, part].reshape(two, HEAD_DIM).astype(
                jnp.float32
            ) + gate_row[:, part] * mixed.astype(jnp.float32)
            modulated[:, part] = (residual * scale_row[:, part]).astype(jnp.bfloat16)
            square = square + jnp.sum(residual * residual, axis=1, keepdims=True)
        product = jnp.dot(modulated[...], basis_ref[...], preferred_element_type=jnp.float32)
        partial[...] = with_tail(product, square, tail_lane).reshape(partial.shape)
        own_part[step] = partial[c]
        core_send[step] = partial[other_c].astype(jnp.bfloat16)
        remote(
            core_send.at[step], core_recv.at[step], sent.at[9], core_sem.at[step], {"seq": pair}
        ).start()
        return carry

    def after_chip(step, carry):
        one_chip(step, carry)

        @pl.when(step == 0)
        def _last_batch():
            ring_step(gate_ring, half)

        @pl.when(step == 2)
        def _ring_one():
            ring_step(down_ring, 1)

        return carry

    lax.fori_loop(0, y_count, after_chip, 0)
    send_part(y_count - 1)

    def send_attended(index, carry):
        s_to = lax.rem(s + index, s_count)

        @pl.when(s_to == s)
        def _keep():
            pltpu.make_async_copy(att_out.at[s_to], attended.at[:, my_cols], att_sem).start()

        @pl.when(s_to != s)
        def _send():
            remote(
                att_out.at[s_to], attended.at[:, my_cols], sent.at[11], att_sem, {"seq": s_to}
            ).start()

        return carry

    values, square = add_core_part(0)
    wait_bytes(part_recv, part_sem)
    for step in range(y_count - 1):
        arrived = part_recv[step].astype(jnp.float32)
        values = values + arrived[:, :rank]
        square = square + arrived[:, rank : rank + 1] + arrived[:, rank + 1 : rank + 2]
    low_rank = (values / jnp.sqrt(square / model_width + epsilon)).astype(jnp.bfloat16)

    def pick_rows(y_to):
        row = lax.broadcasted_iota(jnp.int32, (z_count * slots, tok_rows), 0)
        slot_here = (((row // slots) * y_count + y_to) * slots + row % slots).astype(jnp.float32)
        pick = (slot_here == info_own[0:1, :]) | (slot_here == info_own[1:2, :])
        pick = jnp.where(pick, 1.0, 0.0).astype(jnp.bfloat16)
        return jnp.dot(pick, low_rank, preferred_element_type=jnp.float32).astype(jnp.bfloat16)

    chip_slots = 2 * slots

    def forward_rows(y_from):
        def to_x(x_step, inner):
            x_to = lax.rem(x + near_order(x_step), x_count)
            rows = pl.ds(pl.multiple_of(x_to * chip_slots, chip_slots), chip_slots)
            remote(
                near_rows.at[y_from, rows, :],
                slot_rows.at[x, y_from],
                sent.at[5],
                slot_sem,
                {"dp": x_to},
            ).start()
            return inner

        lax.fori_loop(1, x_count, to_x, 0)
        own = pl.ds(pl.multiple_of(x * chip_slots, chip_slots), chip_slots)
        pltpu.make_async_copy(near_rows.at[y_from, own, :], slot_rows.at[x, y_from], slot_sem).start()

    for step in range(1, y_count):
        y_to = lax.rem(y + near_order(step), y_count)
        out_rows[step - 1] = pick_rows(y_to)
        remote(
            out_rows.at[step - 1],
            near_rows.at[y],
            sent.at[12],
            near_sem.at[y],
            {"seq": 2 * y_to + c},
        ).start()


    near_rows[y] = pick_rows(y)
    forward_rows(y)
    ring_step(down_ring, 2)

    def forward_near(step, carry):
        y_from = lax.rem(y + y_count - near_order(step), y_count)
        lax.fori_loop(4 * step - 4, 4 * step, make_pick, 0)
        wait_bytes(near_rows.at[y_from], near_sem.at[y_from])
        forward_rows(y_from)
        return lax.fori_loop(2 * step, 2 * step + 2, send_attended, carry)

    lax.fori_loop(0, 2, send_attended, 0)
    named_all = info_x[...].reshape(group, info_x.shape[2], tok_rows)
    place = lax.broadcasted_iota(jnp.int32, (group, slots, tok_rows), 1)
    for which in range(2):
        slot_here = (place + ((2 * x + which) * y_count + y) * slots).astype(jnp.float32)
        routed = jnp.where(
            slot_here == named_all[:, 0:1, :], named_all[:, 2:3, :], 0.0
        ) + jnp.where(slot_here == named_all[:, 1:2, :], named_all[:, 3:4, :], 0.0)
        slot_weight[which] = jnp.sum(routed, axis=2, keepdims=True).reshape(chip_rows, 1)

    lax.fori_loop(1, y_count, forward_near, 0)

    wait_bytes(gate_up.at[other_c], pair_g_sem)
    wait_bytes(slot_rows, slot_sem)
    expert = lax.broadcasted_iota(jnp.int32, (chip_rows, 1), 0) % slots // CAP

    for twin_here in range(2):
        rows = slot_rows[:, :, pl.ds(twin_here * slots, slots), :].reshape(chip_rows, rank)
        both_halves = jnp.zeros((chip_rows, gate_up.shape[5]), jnp.float32)
        for which in range(4):
            product = jnp.dot(
                rows,
                gate_up[which // 2, :, twin_here, which % 2].reshape(rank, gate_up.shape[5]),
                preferred_element_type=jnp.float32,
            )
            both_halves = jnp.where(expert == which, product, both_halves)
        gate, up = both_halves[:, :LANES], both_halves[:, LANES:]
        hidden = gate / (1.0 + jnp.exp(-gate)) * up * slot_weight[twin_here]
        hidden_all[x, y, twin_here] = hidden.astype(jnp.bfloat16)
        held = hidden_all.at[x, y, twin_here]

        def hidden_near(step, carry):
            if twin_here == 0:
                device = {"dp": lax.rem(x + near_order(step), x_count)}
            else:
                device = {"seq": 2 * lax.rem(y + near_order(step), y_count) + c}
            remote(held, held, sent.at[15], hid_sem.at[twin_here], device).start()
            return carry

        lax.fori_loop(1, x_count, hidden_near, 0)

    ring_step(down_ring, 3)
    lax.fori_loop(4 * (y_count - 1), group, make_pick, 0)
    wait_bytes(hidden_all.at[pl.ds(0, x_count - 1), y, 0], hid_sem.at[0])

    def hidden_to_y(step, carry):
        held = hidden_all.at[:, y, 0]
        y_to = lax.rem(y + near_order(step), y_count)
        remote(held, held, sent.at[16], hid_y_sem.at[y], {"seq": 2 * y_to + c}).start()
        return carry

    lax.fori_loop(1, y_count, hidden_to_y, 0)
    wait_bytes(hidden_all.at[x, pl.ds(0, y_count - 1), 1], hid_sem.at[1])

    def hidden_to_x(step, carry):
        held = hidden_all.at[x, :, 1]
        x_to = lax.rem(x + near_order(step), x_count)
        remote(held, held, sent.at[18], hid_x_sem.at[x], {"dp": x_to}).start()
        return carry

    lax.fori_loop(1, x_count, hidden_to_x, 0)
    ring_step(down_ring, half)
    wait_bytes(weights.at[other_c], pair_w_sem)

    chip_expert = lax.broadcasted_iota(jnp.int32, (chip_rows, LANES), 0) % slots // CAP

    masks = [
        jnp.where(chip_expert == which, 1.0, 0.0).astype(jnp.bfloat16) for which in range(4)
    ]

    def down_block(x_from, y_from, twin_here):
        held = hidden_all[x_from, y_from, twin_here]
        z_from = 2 * x_from + twin_here
        masked = [held * mask for mask in masks]
        product = jnp.dot(
            jnp.concatenate(masked[:2], axis=1),
            weights[0, z_from, y_from],
            preferred_element_type=jnp.float32,
        ) + jnp.dot(
            jnp.concatenate(masked[2:], axis=1),
            weights[1, z_from, y_from],
            preferred_element_type=jnp.float32,
        )
        to = pl.ds(pl.multiple_of((z_from * y_count + y_from) * slots, slots), slots)
        slot_out[:, to, :] = product.astype(jnp.bfloat16).reshape(group, slots, cols)

    def down_step(step, carry):
        y_from = lax.rem(y + y_count - near_order(step), y_count)
        x_from = lax.rem(x + x_count - near_order(step), x_count)

        @pl.when(step > 0)
        def _arrive_y():
            wait_bytes(hidden_all.at[:, y_from, 0], hid_y_sem.at[y_from])

        def down_first(other, inner):
            down_block(other, y_from, 0)
            return inner

        lax.fori_loop(0, x_count, down_first, 0)

        @pl.when(step > 0)
        def _arrive_x():
            wait_bytes(hidden_all.at[x_from, :, 1], hid_x_sem.at[x_from])

        def down_second(other, inner):
            down_block(x_from, other, 1)
            return inner

        lax.fori_loop(0, y_count, down_second, 0)
        return carry

    lax.fori_loop(0, y_count, down_step, 0)

    mine = x * y_count + y

    def mix_one(step, carry):
        x_to = lax.rem(x + (step + 1) // y_count, x_count)
        y_to = lax.rem(y + step + 1, y_count)
        to = x_to * y_count + y_to
        mixed = jnp.dot(picks[to], slot_out[to], preferred_element_type=jnp.float32)
        mix_out[to] = mixed.astype(jnp.bfloat16)

        def give(first, last):
            source = mix_out.at[to, :, first:last]
            target = mix_in.at[mine, :, first:last]

            @pl.when(to == mine)
            def _keep():
                pltpu.make_async_copy(source, target, mix_sem.at[mine]).start()

            @pl.when(to != mine)
            def _send():
                remote(
                    source,
                    target,
                    sent.at[17],
                    mix_sem.at[mine],
                    {"dp": x_to, "seq": 2 * y_to + c},
                ).start()

        @pl.when(y % 2 == c)
        def _whole():
            give(0, cols)

        @pl.when((y % 2 == 0) & (c == 1))
        def _low():
            give(0, cols - LANES)

        @pl.when((y % 2 == 1) & (c == 0))
        def _high():
            give(LANES, cols)

        return carry

    lax.fori_loop(0, group, mix_one, 0)

    wait_bytes(stream_own, own_sem)
    wait_bytes(attended, att_sem)

    def finish(core):
        for block in range(s_count):
            part = slice(block * head_cols, (block + 1) * head_cols)
            even, odd = 2 * block, 2 * block + 1
            if core == 0:
                wait_bytes(mix_in.at[even], mix_sem.at[even])
                wait_bytes(mix_in.at[odd, :, LANES:cols], mix_sem.at[odd])
                mixed = [mix_in[even], mix_in[odd, :, LANES:]]
            else:
                wait_bytes(mix_in.at[even, :, 0 : cols - LANES], mix_sem.at[even])
                wait_bytes(mix_in.at[odd], mix_sem.at[odd])
                mixed = [mix_in[even, :, : cols - LANES], mix_in[odd]]
            mixed = jnp.concatenate(mixed, axis=1)
            residual = stream_own[:, part].astype(jnp.float32) + attn_gate_ref[:, part].astype(
                jnp.float32
            ) * attended[:, part].astype(jnp.float32)
            output_ref[:, part] = (
                residual + ffn_gate_ref[:, part].astype(jnp.float32) * mixed.astype(jnp.float32)
            ).astype(jnp.bfloat16)

    for core in range(2):

        @pl.when(c == core)
        def _finish():
            finish(core)

    wait_bytes(info_y.at[pl.ds(0, y_count - 1)], sent.at[0])
    wait_bytes(weights.at[0, 0, pl.ds(0, y_count - 1)], sent.at[1])
    batch_left(1, 0)
    batch_left(1, 1)

    @pl.when(z // 2 == x)
    def _spread_done():
        wait_bytes(gate_up.at[0, pl.ds(0, z_count - 1), 0], sent.at[4])

    wait_bytes(slot_rows.at[pl.ds(0, x_count - 1)], sent.at[5])
    wait_bytes(info_x.at[pl.ds(0, x_count - 1)], sent.at[6])
    wait_bytes(weights.at[0, pl.ds(0, z_count - 1)], sent.at[7])
    wait_bytes(weights.at[0], sent.at[8])
    wait_bytes(core_send, sent.at[9])
    wait_bytes(part_send, sent.at[10])
    wait_bytes(att_out.at[pl.ds(0, s_count - 1)], sent.at[11])
    wait_bytes(out_rows, sent.at[12])
    wait_bytes(gate_up.at[0, pl.ds(0, z_count - 1)], sent.at[13])
    wait_bytes(gate_up.at[0], sent.at[14])
    wait_bytes(hidden_all.at[pl.ds(0, 2), pl.ds(0, y_count - 1), 0], sent.at[15])
    wait_bytes(hidden_all.at[:, pl.ds(0, y_count - 1), 0], sent.at[16])
    wait_bytes(hidden_all.at[pl.ds(0, x_count - 1), :, 1], sent.at[18])

    @pl.when(y % 2 == c)
    def _whole_done():
        wait_bytes(mix_out.at[pl.ds(0, group - 1)], sent.at[17])

    @pl.when(y % 2 != c)
    def _part_done():
        wait_bytes(mix_out.at[pl.ds(0, group - 1), :, 0 : cols - LANES], sent.at[17])


def on_device(
    query_rows,
    key_rows,
    value_rows,
    stream,
    shared_basis,
    expert_gate_up,
    expert_down,
    attn_gate,
    ffn_scale,
    ffn_gate,
    expert_ids,
    route_weights,
):
    x_count, z_count, s_count = (lax.axis_size(name) for name in ("dp", "exp", "seq"))
    y_count = s_count // 2
    tok_rows, model_width = stream.shape
    experts_here, hidden_cols, _ = expert_down.shape
    expert_total = z_count * s_count * experts_here
    rank = shared_basis.shape[1]
    head_cols = model_width // s_count
    cols = 384
    slots = 4 * CAP
    length = s_count * tok_rows
    group = x_count * y_count

    vmem = pl.BlockSpec(memory_space=pltpu.VMEM)
    anywhere = pl.BlockSpec(memory_space=pl.ANY)
    bf16, f32 = jnp.bfloat16, jnp.float32
    wide = rank + LANES
    dma = pltpu.SemaphoreType.DMA
    return pl.pallas_call(
        block_kernel,
        out_shape=jax.ShapeDtypeStruct((tok_rows, model_width), bf16),
        in_specs=[anywhere] * 6 + [vmem] * 6,
        out_specs=vmem,
        scratch_shapes=[
            pltpu.VMEM((2, length, head_cols), bf16),
            pltpu.VMEM((s_count, 2, tok_rows, head_cols), bf16),
            pltpu.VMEM((tok_rows, model_width), bf16),
            pltpu.VMEM((s_count, tok_rows, head_cols), bf16),
            pltpu.VMEM((tok_rows, model_width), bf16),
            pltpu.VMEM((2 * tok_rows, head_cols), bf16),
            pltpu.VMEM((2, tok_rows, wide), f32),
            pltpu.VMEM((y_count, tok_rows, wide), f32),
            pltpu.VMEM((y_count, tok_rows, wide), bf16),
            pltpu.VMEM((y_count, tok_rows, wide), bf16),
            pltpu.VMEM((y_count - 1, tok_rows, wide), bf16),
            pltpu.VMEM((y_count - 1, tok_rows, wide), bf16),
            pltpu.VMEM((y_count - 1, z_count * slots, rank), bf16),
            pltpu.VMEM((y_count, z_count * slots, rank), bf16),
            pltpu.VMEM((x_count, y_count, 2 * slots, rank), bf16),
            pltpu.VMEM(
                (2, z_count, 2, experts_here, rank // z_count, 2 * hidden_cols), bf16
            ),
            pltpu.VMEM((x_count, y_count, 2, group * slots, hidden_cols), bf16),
            pltpu.VMEM((2, z_count, y_count, experts_here * hidden_cols, cols), bf16),
            pltpu.VMEM((group, z_count * y_count * slots, cols), bf16),
            pltpu.VMEM((group, tok_rows, cols), bf16),
            pltpu.VMEM((group, tok_rows, cols), bf16),
            pltpu.VMEM((8, tok_rows), f32),
            pltpu.VMEM((y_count, 8, tok_rows), f32),
            pltpu.VMEM((x_count, y_count, 8, tok_rows), f32),
            pltpu.VMEM((2, group * slots, 1), f32),
            pltpu.VMEM((group, tok_rows, group * 2 * slots), bf16),
            dma,
            dma((2, s_count)),
            dma((2, 2)),
            dma,
            dma((2,)),
            dma,
            dma((z_count,)),
            dma,
            dma,
            dma((z_count,)),
            dma,
            dma((y_count,)),
            dma,
            dma,
            dma((y_count,)),
            dma,
            dma((2,)),
            dma((y_count,)),
            dma((x_count,)),
            dma((group,)),
            dma((19,)),
        ],
        compiler_params=pltpu.CompilerParams(
            collective_id=0, has_side_effects=True, vmem_limit_bytes=62 * 1024 * 1024
        ),
        name="block",
    )(
        query_rows,
        key_rows,
        value_rows,
        stream,
        expert_down,
        expert_gate_up,
        shared_basis,
        attn_gate,
        ffn_scale,
        ffn_gate,
        expert_ids.T,
        route_weights.T,
    )


def solution(mesh):
    in_specs = (
        P(("dp", "exp", "seq"), None),
        P(("dp", "exp", "seq"), None),
        P(("dp", "exp", "seq"), None),
        P(("dp", "exp", "seq"), None),
        P("seq", None),
        P(("exp", "seq"), None, None),
        P(("exp", "seq"), None, None),
        P(("dp", "exp"), None),
        P(("dp", "exp"), None),
        P(("dp", "exp"), None),
        P(("dp", "exp", "seq"), None),
        P(("dp", "exp", "seq"), None),
    )
    out_specs = P(("dp", "exp", "seq"), None)
    return jax.shard_map(
        on_device, mesh=mesh, in_specs=in_specs, out_specs=out_specs, check_vma=False
    )
```

```python
import functools
import math

import jax
import jax.numpy as jnp
from jax import lax
from jax.experimental import pallas as pl
from jax.experimental.pallas import tpu as pltpu
from jax.sharding import PartitionSpec as P

HEAD_DIM = 128
LANES = 128
MESH = pl.DeviceIdType.MESH
epsilon = 1e-06
CAP = 4


def block_kernel(
    query_ref,
    key_ref,
    value_ref,
    stream_ref,
    down_ref,
    gate_up_ref,
    basis_ref,
    attn_gate_ref,
    ffn_scale_ref,
    ffn_gate_ref,
    ids_ref,
    route_ref,
    output_ref,
    kv_in,
    qs_in,
    stream_own,
    att_out,
    attended,
    modulated,
    partial,
    own_part,
    core_send,
    core_recv,
    part_send,
    part_recv,
    out_rows,
    near_rows,
    slot_rows,
    gate_up,
    hidden_all,
    weights,
    slot_out,
    mix_out,
    mix_in,
    info_own,
    info_y,
    info_x,
    slot_weight,
    picks,
    kv_sem,
    qs_sem,
    batch_sem,
    own_sem,
    info_sem,
    near_w_sem,
    ring_sem,
    pair_w_sem,
    near_g_sem,
    ring_g_sem,
    pair_g_sem,
    core_sem,
    part_sem,
    att_sem,
    near_sem,
    slot_sem,
    hid_sem,
    hid_y_sem,
    hid_x_sem,
    mix_sem,
    sent,
):
    x_count, z_count, s_count = (lax.axis_size(name) for name in ("dp", "exp", "seq"))
    y_count = s_count // 2
    x, z, s = (lax.axis_index(name) for name in ("dp", "exp", "seq"))
    y, c = s // 2, s % 2
    other_c = 1 - c
    pair = 2 * y + other_c
    tok_rows, model_width = attended.shape
    head_cols = kv_in.shape[2]
    heads_here = head_cols // HEAD_DIM
    cols = weights.shape[4]
    rank = near_rows.shape[2]
    slots = 4 * CAP
    quarter = model_width // x_count

    def remote(src, dst, send_sem, recv_sem, device):
        return pltpu.make_async_remote_copy(
            src_ref=src,
            dst_ref=dst,
            send_sem=send_sem,
            recv_sem=recv_sem,
            device_id=device,
            device_id_type=MESH,
        )

    def wait_bytes(ref, sem):
        pltpu.make_async_copy(ref, ref, sem).wait()

    def first_column(y_to):
        return pl.multiple_of(x * quarter + (y_to // 2) * head_cols + (y_to % 2) * 256, LANES)

    def near_order(step):
        return step + step // 2 - 2 * (step // 3)

    barrier = pltpu.get_barrier_semaphore()

    def greet(device):
        pl.semaphore_signal(barrier, inc=1, device_id=device, device_id_type=MESH)

    def greet_seq(step, carry):
        greet({"seq": lax.rem(s + step, s_count)})
        return carry

    def greet_z(step, carry):
        greet({"exp": lax.rem(z + step, z_count)})
        return carry

    def greet_x(step, carry):
        greet({"dp": lax.rem(x + step, x_count)})

        def greet_xy(y_step, inner):
            greet(
                {
                    "dp": lax.rem(x + step, x_count),
                    "seq": 2 * lax.rem(y + y_step, y_count) + c,
                }
            )
            return inner

        return lax.fori_loop(1, y_count, greet_xy, carry)

    lax.fori_loop(1, s_count, greet_seq, 0)
    lax.fori_loop(1, z_count, greet_z, 0)
    lax.fori_loop(1, x_count, greet_x, 0)

    my_rows = pl.ds(pl.multiple_of(s * tok_rows, tok_rows), tok_rows)
    my_cols = pl.ds(pl.multiple_of(s * head_cols, head_cols), head_cols)
    kv_refs = (key_ref, value_ref)
    qs_refs = (query_ref, stream_ref)
    for which in range(2):
        pltpu.make_async_copy(
            kv_refs[which].at[:, my_cols], kv_in.at[which, my_rows, :], kv_sem
        ).start()
        pltpu.make_async_copy(
            qs_refs[which].at[:, my_cols], qs_in.at[s, which], qs_sem.at[which, s]
        ).start()
        pltpu.make_async_copy(
            down_ref.at[which, :, pl.ds(first_column(y), cols)],
            weights.at[c, z, y, pl.ds(which * LANES, LANES), :],
            near_w_sem,
        ).start()
    pltpu.make_async_copy(stream_ref, stream_own, own_sem).start()

    rank_part = rank // z_count
    twin = z - 2 * x

    @pl.when(z // 2 == x)
    def _own_gate_up():
        part = pl.ds(pl.multiple_of(z * rank_part, rank_part), rank_part)
        pltpu.make_async_copy(
            gate_up_ref.at[:, part, :], gate_up.at[c, z, twin], near_g_sem
        ).start()

    entries = 2 * tok_rows
    experts = 4 * z_count * y_count
    ids_row = jnp.concatenate([ids_ref[0:1, :], ids_ref[1:2, :]], axis=1)
    named = lax.broadcasted_iota(jnp.int32, (experts, entries), 0) == ids_row
    entry = [lax.broadcasted_iota(jnp.int32, (entries, entries), axis) for axis in (0, 1)]
    entry = [2 * (one % tok_rows) + one // tok_rows for one in entry]
    before = jnp.where(entry[0] < entry[1], 1.0, 0.0).astype(jnp.bfloat16)
    counts = jnp.dot(
        jnp.where(named, 1.0, 0.0).astype(jnp.bfloat16), before, preferred_element_type=jnp.float32
    )
    slot_ids = (
        jnp.sum(jnp.where(named, counts, 0.0), axis=0, keepdims=True)
        + ids_row.astype(jnp.float32) * CAP
    )
    info_row = lax.broadcasted_iota(jnp.int32, info_own.shape, 0)
    info = jnp.where(info_row == 2, route_ref[0:1, :], 0.0)
    info = jnp.where(info_row == 3, route_ref[1:2, :], info)
    info = jnp.where(info_row == 0, slot_ids[:, :tok_rows], info)
    info_own[...] = jnp.where(info_row == 1, slot_ids[:, tok_rows:], info)
    pltpu.make_async_copy(info_own, info_y.at[y], info_sem.at[0]).start()

    pl.semaphore_wait(barrier, s_count - 1 + z_count - 1 + (x_count - 1) * y_count)

    def info_to_y(step, carry):
        y_to = lax.rem(y + step, y_count)
        remote(
            info_own, info_y.at[y], sent.at[0], info_sem.at[0], {"seq": 2 * y_to + c}
        ).start()
        return carry

    lax.fori_loop(1, y_count, info_to_y, 0)

    def near_first(step, carry):
        y_to = lax.rem(y + near_order(step), y_count)
        device = {"seq": 2 * y_to + c}
        for which in range(2):
            remote(
                down_ref.at[which, :, pl.ds(first_column(y_to), cols)],
                weights.at[c, z, y, pl.ds(which * LANES, LANES), :],
                sent.at[1],
                near_w_sem,
                device,
            ).start()
        return carry

    lax.fori_loop(1, y_count, near_first, 0)

    @pl.when(z // 2 == x)
    def _spread_gate_up():
        def to_z(step, carry):
            z_to = lax.rem(z + step, z_count)
            part = pl.ds(pl.multiple_of(z_to * rank_part, rank_part), rank_part)
            remote(
                gate_up_ref.at[:, part, :],
                gate_up.at[c, z_to, twin],
                sent.at[4],
                near_g_sem,
                {"exp": z_to},
            ).start()
            return carry

        lax.fori_loop(1, z_count, to_z, 0)


    def send_batch(refs, slot_of, sem, send_sem, distances):
        for which in range(2):

            def one_copy(index, carry):
                s_to = 2 * lax.rem(y + distances[0] + 2 * (index % len(distances)), y_count) + (
                    index // len(distances)
                )
                columns = pl.ds(pl.multiple_of(s_to * head_cols, head_cols), head_cols)
                remote(
                    refs[which].at[:, columns], slot_of(which), send_sem, sem(which), {"seq": s_to}
                ).start()
                return carry

            if len(distances) == 2:
                columns = pl.ds(pl.multiple_of(pair * head_cols, head_cols), head_cols)
                remote(
                    refs[which].at[:, columns], slot_of(which), send_sem, sem(which), {"seq": pair}
                ).start()
            lax.fori_loop(0, 2 * len(distances), one_copy, 0)

    batches = ((1, 3), (2,))

    def send_kv(batch):
        send_batch(
            kv_refs,
            lambda which: kv_in.at[which, my_rows, :],
            lambda which: kv_sem,
            batch_sem.at[0, batch],
            batches[batch],
        )

    def send_qs(batch):
        send_batch(
            qs_refs,
            lambda which: qs_in.at[s, which],
            lambda which: qs_sem.at[which, s],
            batch_sem.at[1, batch],
            batches[batch],
        )

    def batch_left(kind, batch):
        peers = 5 if batch == 0 else 2
        wait_bytes(qs_in.at[pl.ds(0, peers)], batch_sem.at[kind, batch])

    send_kv(0)
    send_kv(1)

    always = z >= 0
    half = z_count // 2

    def pass_on(buffer, sems, left_sem, pair_left, pair_sem, block, up, down):
        held = buffer.at[c, block]

        def pass_to(z_to):
            remote(held, held, left_sem, sems.at[block], {"exp": lax.rem(z_to, z_count)}).start()

        if up is not None:

            @pl.when(up)
            def _up():
                pass_to(z + 1)

        if down is not None:

            @pl.when(down)
            def _down():
                pass_to(z + z_count - 1)

        remote(held, held, pair_left, pair_sem, {"seq": pair}).start()

    def ring_step(ring, step):
        buffer, sems = ring[0], ring[1]
        below = lax.rem(z + z_count - step, z_count)
        above = lax.rem(z + step, z_count)
        wait_bytes(buffer.at[c, below], sems.at[below])
        if step == half:
            pass_on(*ring, below, None, None)
            return
        pass_on(*ring, below, always if step < half - 1 else c == 0, None)
        wait_bytes(buffer.at[c, above], sems.at[above])
        pass_on(*ring, above, None, always if step < half - 1 else c == 1)

    gate_ring = (gate_up, ring_g_sem, sent.at[13], sent.at[14], pair_g_sem)
    down_ring = (weights, ring_sem, sent.at[7], sent.at[8], pair_w_sem)

    wait_bytes(weights.at[c, z], near_w_sem)
    pass_on(*down_ring, z, always, always)
    wait_bytes(gate_up.at[c, z], near_g_sem)
    wait_bytes(info_y, info_sem.at[0])
    pltpu.make_async_copy(info_y, info_x.at[x], info_sem.at[1]).start()

    def info_to_x(step, carry):
        remote(
            info_y,
            info_x.at[x],
            sent.at[6],
            info_sem.at[1],
            {"dp": lax.rem(x + step, x_count)},
        ).start()
        return carry

    lax.fori_loop(1, x_count, info_to_x, 0)
    pass_on(*gate_ring, z, always, always)
    batch_left(0, 0)
    send_qs(0)
    batch_left(0, 1)
    send_qs(1)

    wait_bytes(info_x, info_sem.at[1])
    group = x_count * y_count
    chip_rows = group * slots
    def make_pick(source, carry):
        slot_iota = lax.broadcasted_iota(jnp.int32, (picks.shape[2], tok_rows), 0).astype(
            jnp.float32
        )
        named_here = info_x[source // y_count, source % y_count]
        pick = (slot_iota == named_here[0:1, :]) | (slot_iota == named_here[1:2, :])
        picks[source] = jnp.where(pick, 1.0, 0.0).astype(jnp.bfloat16).T
        return carry

    wait_bytes(kv_in, kv_sem)

    length = s_count * tok_rows
    lane = lax.broadcasted_iota(jnp.int32, (length, HEAD_DIM), 1)
    ones_column = jnp.where(lane == 0, 1.0, 0.0).astype(jnp.bfloat16)
    exponent_scale = 1.0 / (math.sqrt(HEAD_DIM) * math.log(2.0))
    gate_row = attn_gate_ref[:, my_cols].astype(jnp.float32)
    scale_row = ffn_scale_ref[:, my_cols].astype(jnp.float32)
    two = 2 * tok_rows
    tail_lane = lax.broadcasted_iota(jnp.int32, (two, LANES), 1)

    def with_tail(values, square, tail):
        high = square.astype(jnp.bfloat16).astype(jnp.float32)
        extra = jnp.where(tail == 0, high, jnp.where(tail == 1, square - high, 0.0))
        return jnp.concatenate([values, extra], axis=1)

    def add_core_part(step):
        wait_bytes(core_recv.at[step], core_sem.at[step])
        total = own_part[step] + core_recv[step].astype(jnp.float32)
        square = total[:, rank : rank + 1] + total[:, rank + 1 : rank + 2]
        return total[:, :rank], square

    def send_part(step):
        values, square = add_core_part(step)
        part_send[step - 1] = with_tail(values, square, tail_lane[:tok_rows]).astype(jnp.bfloat16)
        distance = near_order(step)
        y_to = lax.rem(y + y_count - distance, y_count)
        remote(
            part_send.at[step - 1],
            part_recv.at[step - 1],
            sent.at[10],
            part_sem,
            {"seq": 2 * y_to + c},
        ).start()

    def one_chip(step, carry):
        y_from = lax.rem(y + y_count - near_order(step), y_count)

        @pl.when(step > 1)
        def _previous():
            send_part(step - 1)

        def wait_rows(which):
            for core in range(2):
                s_from = 2 * y_from + core
                wait_bytes(qs_in.at[s_from, which], qs_sem.at[which, s_from])

        wait_rows(0)
        both = pl.ds(2 * y_from, 2)
        square = jnp.zeros((two, 1), jnp.float32)
        for head in range(heads_here):
            part = slice(head * HEAD_DIM, (head + 1) * HEAD_DIM)
            scores = lax.dot_general(
                qs_in[both, 0, :, part].reshape(two, HEAD_DIM),
                kv_in[0, :, part],
                (((1,), (1,)), ((), ())),
                preferred_element_type=jnp.float32,
            )
            row_max = jnp.max(scores, axis=-1, keepdims=True)
            raised = jnp.exp2((scores - row_max) * exponent_scale).astype(jnp.bfloat16)
            value_ones = jnp.concatenate([kv_in[1, :, part], ones_column], axis=1)
            mixed = jnp.dot(raised, value_ones, preferred_element_type=jnp.float32)
            mixed = (mixed[:, :HEAD_DIM] / mixed[:, HEAD_DIM : HEAD_DIM + 1]).astype(jnp.bfloat16)
            att_out[both, :, part] = mixed.reshape(2, tok_rows, HEAD_DIM)

        wait_rows(1)
        for head in range(heads_here):
            part = slice(head * HEAD_DIM, (head + 1) * HEAD_DIM)
            mixed = att_out[both, :, part].reshape(two, HEAD_DIM)
            residual = qs_in[both, 1, :, part].reshape(two, HEAD_DIM).astype(
                jnp.float32
            ) + gate_row[:, part] * mixed.astype(jnp.float32)
            modulated[:, part] = (residual * scale_row[:, part]).astype(jnp.bfloat16)
            square = square + jnp.sum(residual * residual, axis=1, keepdims=True)
        product = jnp.dot(modulated[...], basis_ref[...], preferred_element_type=jnp.float32)
        partial[...] = with_tail(product, square, tail_lane).reshape(partial.shape)
        own_part[step] = partial[c]
        core_send[step] = partial[other_c].astype(jnp.bfloat16)
        remote(
            core_send.at[step], core_recv.at[step], sent.at[9], core_sem.at[step], {"seq": pair}
        ).start()
        return carry

    def after_chip(step, carry):
        one_chip(step, carry)

        @pl.when(step == 0)
        def _gate_one():
            ring_step(gate_ring, 1)

        @pl.when(step == 1)
        def _down_one():
            ring_step(down_ring, 1)

        @pl.when(step == 2)
        def _gate_two():
            ring_step(gate_ring, 2)

        return carry

    lax.fori_loop(0, y_count, after_chip, 0)
    send_part(y_count - 1)
    ring_step(gate_ring, 3)
    ring_step(down_ring, 2)

    def send_attended(index, carry):
        s_to = lax.rem(s + index, s_count)

        @pl.when(s_to == s)
        def _keep():
            pltpu.make_async_copy(att_out.at[s_to], attended.at[:, my_cols], att_sem).start()

        @pl.when(s_to != s)
        def _send():
            remote(
                att_out.at[s_to], attended.at[:, my_cols], sent.at[11], att_sem, {"seq": s_to}
            ).start()

        return carry

    values, square = add_core_part(0)
    wait_bytes(part_recv, part_sem)
    for step in range(y_count - 1):
        arrived = part_recv[step].astype(jnp.float32)
        values = values + arrived[:, :rank]
        square = square + arrived[:, rank : rank + 1] + arrived[:, rank + 1 : rank + 2]
    low_rank = (values / jnp.sqrt(square / model_width + epsilon)).astype(jnp.bfloat16)

    def pick_rows(y_to):
        row = lax.broadcasted_iota(jnp.int32, (z_count * slots, tok_rows), 0)
        slot_here = (((row // slots) * y_count + y_to) * slots + row % slots).astype(jnp.float32)
        pick = (slot_here == info_own[0:1, :]) | (slot_here == info_own[1:2, :])
        pick = jnp.where(pick, 1.0, 0.0).astype(jnp.bfloat16)
        return jnp.dot(pick, low_rank, preferred_element_type=jnp.float32).astype(jnp.bfloat16)

    chip_slots = 2 * slots

    def forward_rows(y_from):
        def to_x(x_step, inner):
            x_to = lax.rem(x + near_order(x_step), x_count)
            rows = pl.ds(pl.multiple_of(x_to * chip_slots, chip_slots), chip_slots)
            remote(
                near_rows.at[y_from, rows, :],
                slot_rows.at[x, y_from],
                sent.at[5],
                slot_sem,
                {"dp": x_to},
            ).start()
            return inner

        lax.fori_loop(1, x_count, to_x, 0)
        own = pl.ds(pl.multiple_of(x * chip_slots, chip_slots), chip_slots)
        pltpu.make_async_copy(near_rows.at[y_from, own, :], slot_rows.at[x, y_from], slot_sem).start()

    for step in range(1, y_count):
        y_to = lax.rem(y + near_order(step), y_count)
        out_rows[step - 1] = pick_rows(y_to)
        remote(
            out_rows.at[step - 1],
            near_rows.at[y],
            sent.at[12],
            near_sem.at[y],
            {"seq": 2 * y_to + c},
        ).start()


    near_rows[y] = pick_rows(y)
    forward_rows(y)
    ring_step(gate_ring, half)

    def forward_near(step, carry):
        y_from = lax.rem(y + y_count - near_order(step), y_count)
        lax.fori_loop(4 * step - 4, 4 * step, make_pick, 0)
        wait_bytes(near_rows.at[y_from], near_sem.at[y_from])
        forward_rows(y_from)
        return lax.fori_loop(2 * step, 2 * step + 2, send_attended, carry)

    lax.fori_loop(0, 2, send_attended, 0)
    named_all = info_x[...].reshape(group, info_x.shape[2], tok_rows)
    place = lax.broadcasted_iota(jnp.int32, (group, slots, tok_rows), 1)
    for which in range(2):
        slot_here = (place + ((2 * x + which) * y_count + y) * slots).astype(jnp.float32)
        routed = jnp.where(
            slot_here == named_all[:, 0:1, :], named_all[:, 2:3, :], 0.0
        ) + jnp.where(slot_here == named_all[:, 1:2, :], named_all[:, 3:4, :], 0.0)
        slot_weight[which] = jnp.sum(routed, axis=2, keepdims=True).reshape(chip_rows, 1)

    lax.fori_loop(1, y_count, forward_near, 0)

    ring_step(down_ring, 3)
    wait_bytes(gate_up.at[other_c], pair_g_sem)
    wait_bytes(slot_rows, slot_sem)
    expert = lax.broadcasted_iota(jnp.int32, (chip_rows, 1), 0) % slots // CAP

    for twin_here in range(2):
        rows = slot_rows[:, :, pl.ds(twin_here * slots, slots), :].reshape(chip_rows, rank)
        both_halves = jnp.zeros((chip_rows, gate_up.shape[5]), jnp.float32)
        for which in range(4):
            product = jnp.dot(
                rows,
                gate_up[which // 2, :, twin_here, which % 2].reshape(rank, gate_up.shape[5]),
                preferred_element_type=jnp.float32,
            )
            both_halves = jnp.where(expert == which, product, both_halves)
        gate, up = both_halves[:, :LANES], both_halves[:, LANES:]
        hidden = gate / (1.0 + jnp.exp(-gate)) * up * slot_weight[twin_here]
        hidden_all[x, y, twin_here] = hidden.astype(jnp.bfloat16)
        held = hidden_all.at[x, y, twin_here]

        def hidden_near(step, carry):
            if twin_here == 0:
                device = {"dp": lax.rem(x + near_order(step), x_count)}
            else:
                device = {"seq": 2 * lax.rem(y + near_order(step), y_count) + c}
            remote(held, held, sent.at[15], hid_sem.at[twin_here], device).start()
            return carry

        lax.fori_loop(1, x_count, hidden_near, 0)

    lax.fori_loop(4 * (y_count - 1), group, make_pick, 0)
    wait_bytes(hidden_all.at[pl.ds(0, x_count - 1), y, 0], hid_sem.at[0])

    def hidden_to_y(step, carry):
        held = hidden_all.at[:, y, 0]
        y_to = lax.rem(y + near_order(step), y_count)
        remote(held, held, sent.at[16], hid_y_sem.at[y], {"seq": 2 * y_to + c}).start()
        return carry

    lax.fori_loop(1, y_count, hidden_to_y, 0)
    wait_bytes(hidden_all.at[x, pl.ds(0, y_count - 1), 1], hid_sem.at[1])

    def hidden_to_x(step, carry):
        held = hidden_all.at[x, :, 1]
        x_to = lax.rem(x + near_order(step), x_count)
        remote(held, held, sent.at[18], hid_x_sem.at[x], {"dp": x_to}).start()
        return carry

    lax.fori_loop(1, x_count, hidden_to_x, 0)
    ring_step(down_ring, half)
    wait_bytes(weights.at[other_c], pair_w_sem)

    chip_expert = lax.broadcasted_iota(jnp.int32, (chip_rows, LANES), 0) % slots // CAP

    masks = [
        jnp.where(chip_expert == which, 1.0, 0.0).astype(jnp.bfloat16) for which in range(4)
    ]

    def down_block(x_from, y_from, twin_here):
        held = hidden_all[x_from, y_from, twin_here]
        z_from = 2 * x_from + twin_here
        masked = [held * mask for mask in masks]
        product = jnp.dot(
            jnp.concatenate(masked[:2], axis=1),
            weights[0, z_from, y_from],
            preferred_element_type=jnp.float32,
        ) + jnp.dot(
            jnp.concatenate(masked[2:], axis=1),
            weights[1, z_from, y_from],
            preferred_element_type=jnp.float32,
        )
        to = pl.ds(pl.multiple_of((z_from * y_count + y_from) * slots, slots), slots)
        slot_out[:, to, :] = product.astype(jnp.bfloat16).reshape(group, slots, cols)

    def down_step(step, carry):
        y_from = lax.rem(y + y_count - near_order(step), y_count)
        x_from = lax.rem(x + x_count - near_order(step), x_count)

        @pl.when(step > 0)
        def _arrive_y():
            wait_bytes(hidden_all.at[:, y_from, 0], hid_y_sem.at[y_from])

        def down_first(other, inner):
            down_block(other, y_from, 0)
            return inner

        lax.fori_loop(0, x_count, down_first, 0)

        @pl.when(step > 0)
        def _arrive_x():
            wait_bytes(hidden_all.at[x_from, :, 1], hid_x_sem.at[x_from])

        def down_second(other, inner):
            down_block(x_from, other, 1)
            return inner

        lax.fori_loop(0, y_count, down_second, 0)
        return carry

    lax.fori_loop(0, y_count, down_step, 0)

    mine = x * y_count + y

    def mix_one(step, carry):
        x_to = lax.rem(x + (step + 1) // y_count, x_count)
        y_to = lax.rem(y + step + 1, y_count)
        to = x_to * y_count + y_to
        mixed = jnp.dot(picks[to], slot_out[to], preferred_element_type=jnp.float32)
        mix_out[to] = mixed.astype(jnp.bfloat16)

        def give(first, last):
            source = mix_out.at[to, :, first:last]
            target = mix_in.at[mine, :, first:last]

            @pl.when(to == mine)
            def _keep():
                pltpu.make_async_copy(source, target, mix_sem.at[mine]).start()

            @pl.when(to != mine)
            def _send():
                remote(
                    source,
                    target,
                    sent.at[17],
                    mix_sem.at[mine],
                    {"dp": x_to, "seq": 2 * y_to + c},
                ).start()

        @pl.when(y % 2 == c)
        def _whole():
            give(0, cols)

        @pl.when((y % 2 == 0) & (c == 1))
        def _low():
            give(0, cols - LANES)

        @pl.when((y % 2 == 1) & (c == 0))
        def _high():
            give(LANES, cols)

        return carry

    lax.fori_loop(0, group, mix_one, 0)

    wait_bytes(stream_own, own_sem)
    wait_bytes(attended, att_sem)

    def finish(core):
        for block in range(s_count):
            part = slice(block * head_cols, (block + 1) * head_cols)
            even, odd = 2 * block, 2 * block + 1
            if core == 0:
                wait_bytes(mix_in.at[even], mix_sem.at[even])
                wait_bytes(mix_in.at[odd, :, LANES:cols], mix_sem.at[odd])
                mixed = [mix_in[even], mix_in[odd, :, LANES:]]
            else:
                wait_bytes(mix_in.at[even, :, 0 : cols - LANES], mix_sem.at[even])
                wait_bytes(mix_in.at[odd], mix_sem.at[odd])
                mixed = [mix_in[even, :, : cols - LANES], mix_in[odd]]
            mixed = jnp.concatenate(mixed, axis=1)
            residual = stream_own[:, part].astype(jnp.float32) + attn_gate_ref[:, part].astype(
                jnp.float32
            ) * attended[:, part].astype(jnp.float32)
            output_ref[:, part] = (
                residual + ffn_gate_ref[:, part].astype(jnp.float32) * mixed.astype(jnp.float32)
            ).astype(jnp.bfloat16)

    for core in range(2):

        @pl.when(c == core)
        def _finish():
            finish(core)

    wait_bytes(info_y.at[pl.ds(0, y_count - 1)], sent.at[0])
    wait_bytes(weights.at[0, 0, pl.ds(0, y_count - 1)], sent.at[1])
    batch_left(1, 0)
    batch_left(1, 1)

    @pl.when(z // 2 == x)
    def _spread_done():
        wait_bytes(gate_up.at[0, pl.ds(0, z_count - 1), 0], sent.at[4])

    wait_bytes(slot_rows.at[pl.ds(0, x_count - 1)], sent.at[5])
    wait_bytes(info_x.at[pl.ds(0, x_count - 1)], sent.at[6])
    wait_bytes(weights.at[0, pl.ds(0, z_count - 1)], sent.at[7])
    wait_bytes(weights.at[0], sent.at[8])
    wait_bytes(core_send, sent.at[9])
    wait_bytes(part_send, sent.at[10])
    wait_bytes(att_out.at[pl.ds(0, s_count - 1)], sent.at[11])
    wait_bytes(out_rows, sent.at[12])
    wait_bytes(gate_up.at[0, pl.ds(0, z_count - 1)], sent.at[13])
    wait_bytes(gate_up.at[0], sent.at[14])
    wait_bytes(hidden_all.at[pl.ds(0, 2), pl.ds(0, y_count - 1), 0], sent.at[15])
    wait_bytes(hidden_all.at[:, pl.ds(0, y_count - 1), 0], sent.at[16])
    wait_bytes(hidden_all.at[pl.ds(0, x_count - 1), :, 1], sent.at[18])

    @pl.when(y % 2 == c)
    def _whole_done():
        wait_bytes(mix_out.at[pl.ds(0, group - 1)], sent.at[17])

    @pl.when(y % 2 != c)
    def _part_done():
        wait_bytes(mix_out.at[pl.ds(0, group - 1), :, 0 : cols - LANES], sent.at[17])


def on_device(
    query_rows,
    key_rows,
    value_rows,
    stream,
    shared_basis,
    expert_gate_up,
    expert_down,
    attn_gate,
    ffn_scale,
    ffn_gate,
    expert_ids,
    route_weights,
):
    x_count, z_count, s_count = (lax.axis_size(name) for name in ("dp", "exp", "seq"))
    y_count = s_count // 2
    tok_rows, model_width = stream.shape
    experts_here, hidden_cols, _ = expert_down.shape
    expert_total = z_count * s_count * experts_here
    rank = shared_basis.shape[1]
    head_cols = model_width // s_count
    cols = 384
    slots = 4 * CAP
    length = s_count * tok_rows
    group = x_count * y_count

    vmem = pl.BlockSpec(memory_space=pltpu.VMEM)
    anywhere = pl.BlockSpec(memory_space=pl.ANY)
    bf16, f32 = jnp.bfloat16, jnp.float32
    wide = rank + LANES
    dma = pltpu.SemaphoreType.DMA
    return pl.pallas_call(
        block_kernel,
        out_shape=jax.ShapeDtypeStruct((tok_rows, model_width), bf16),
        in_specs=[anywhere] * 6 + [vmem] * 6,
        out_specs=vmem,
        scratch_shapes=[
            pltpu.VMEM((2, length, head_cols), bf16),
            pltpu.VMEM((s_count, 2, tok_rows, head_cols), bf16),
            pltpu.VMEM((tok_rows, model_width), bf16),
            pltpu.VMEM((s_count, tok_rows, head_cols), bf16),
            pltpu.VMEM((tok_rows, model_width), bf16),
            pltpu.VMEM((2 * tok_rows, head_cols), bf16),
            pltpu.VMEM((2, tok_rows, wide), f32),
            pltpu.VMEM((y_count, tok_rows, wide), f32),
            pltpu.VMEM((y_count, tok_rows, wide), bf16),
            pltpu.VMEM((y_count, tok_rows, wide), bf16),
            pltpu.VMEM((y_count - 1, tok_rows, wide), bf16),
            pltpu.VMEM((y_count - 1, tok_rows, wide), bf16),
            pltpu.VMEM((y_count - 1, z_count * slots, rank), bf16),
            pltpu.VMEM((y_count, z_count * slots, rank), bf16),
            pltpu.VMEM((x_count, y_count, 2 * slots, rank), bf16),
            pltpu.VMEM(
                (2, z_count, 2, experts_here, rank // z_count, 2 * hidden_cols), bf16
            ),
            pltpu.VMEM((x_count, y_count, 2, group * slots, hidden_cols), bf16),
            pltpu.VMEM((2, z_count, y_count, experts_here * hidden_cols, cols), bf16),
            pltpu.VMEM((group, z_count * y_count * slots, cols), bf16),
            pltpu.VMEM((group, tok_rows, cols), bf16),
            pltpu.VMEM((group, tok_rows, cols), bf16),
            pltpu.VMEM((8, tok_rows), f32),
            pltpu.VMEM((y_count, 8, tok_rows), f32),
            pltpu.VMEM((x_count, y_count, 8, tok_rows), f32),
            pltpu.VMEM((2, group * slots, 1), f32),
            pltpu.VMEM((group, tok_rows, group * 2 * slots), bf16),
            dma,
            dma((2, s_count)),
            dma((2, 2)),
            dma,
            dma((2,)),
            dma,
            dma((z_count,)),
            dma,
            dma,
            dma((z_count,)),
            dma,
            dma((y_count,)),
            dma,
            dma,
            dma((y_count,)),
            dma,
            dma((2,)),
            dma((y_count,)),
            dma((x_count,)),
            dma((group,)),
            dma((19,)),
        ],
        compiler_params=pltpu.CompilerParams(
            collective_id=0, has_side_effects=True, vmem_limit_bytes=62 * 1024 * 1024
        ),
        name="block",
    )(
        query_rows,
        key_rows,
        value_rows,
        stream,
        expert_down,
        expert_gate_up,
        shared_basis,
        attn_gate,
        ffn_scale,
        ffn_gate,
        expert_ids.T,
        route_weights.T,
    )


def solution(mesh):
    in_specs = (
        P(("dp", "exp", "seq"), None),
        P(("dp", "exp", "seq"), None),
        P(("dp", "exp", "seq"), None),
        P(("dp", "exp", "seq"), None),
        P("seq", None),
        P(("exp", "seq"), None, None),
        P(("exp", "seq"), None, None),
        P(("dp", "exp"), None),
        P(("dp", "exp"), None),
        P(("dp", "exp"), None),
        P(("dp", "exp", "seq"), None),
        P(("dp", "exp", "seq"), None),
    )
    out_specs = P(("dp", "exp", "seq"), None)
    return jax.shard_map(
        on_device, mesh=mesh, in_specs=in_specs, out_specs=out_specs, check_vma=False
    )
```

```python
import functools
import math

import jax
import jax.numpy as jnp
from jax import lax
from jax.experimental import pallas as pl
from jax.experimental.pallas import tpu as pltpu
from jax.sharding import PartitionSpec as P

HEAD_DIM = 128
LANES = 128
MESH = pl.DeviceIdType.MESH
epsilon = 1e-06
CAP = 4


def block_kernel(
    query_ref,
    key_ref,
    value_ref,
    stream_ref,
    down_ref,
    gate_up_ref,
    basis_ref,
    attn_gate_ref,
    ffn_scale_ref,
    ffn_gate_ref,
    ids_ref,
    route_ref,
    output_ref,
    kv_in,
    qs_in,
    stream_own,
    att_out,
    attended,
    modulated,
    partial,
    own_part,
    core_send,
    core_recv,
    part_send,
    part_recv,
    out_rows,
    near_rows,
    slot_rows,
    gate_up,
    hidden_all,
    weights,
    slot_out,
    mix_out,
    mix_in,
    info_own,
    info_y,
    info_x,
    slot_weight,
    picks,
    kv_sem,
    qs_sem,
    batch_sem,
    own_sem,
    info_sem,
    near_w_sem,
    ring_sem,
    pair_w_sem,
    near_g_sem,
    ring_g_sem,
    pair_g_sem,
    core_sem,
    part_sem,
    att_sem,
    near_sem,
    slot_sem,
    hid_sem,
    hid_y_sem,
    hid_x_sem,
    mix_sem,
    sent,
):
    x_count, z_count, s_count = (lax.axis_size(name) for name in ("dp", "exp", "seq"))
    y_count = s_count // 2
    x, z, s = (lax.axis_index(name) for name in ("dp", "exp", "seq"))
    y, c = s // 2, s % 2
    other_c = 1 - c
    pair = 2 * y + other_c
    tok_rows, model_width = attended.shape
    head_cols = kv_in.shape[2]
    heads_here = head_cols // HEAD_DIM
    cols = weights.shape[4]
    rank = near_rows.shape[2]
    slots = 4 * CAP
    quarter = model_width // x_count

    def remote(src, dst, send_sem, recv_sem, device):
        return pltpu.make_async_remote_copy(
            src_ref=src,
            dst_ref=dst,
            send_sem=send_sem,
            recv_sem=recv_sem,
            device_id=device,
            device_id_type=MESH,
        )

    def wait_bytes(ref, sem):
        pltpu.make_async_copy(ref, ref, sem).wait()

    def first_column(y_to):
        return pl.multiple_of(x * quarter + (y_to // 2) * head_cols + (y_to % 2) * 256, LANES)

    def near_order(step):
        return step + step // 2 - 2 * (step // 3)

    barrier = pltpu.get_barrier_semaphore()

    def greet(device):
        pl.semaphore_signal(barrier, inc=1, device_id=device, device_id_type=MESH)

    def greet_seq(step, carry):
        greet({"seq": lax.rem(s + step, s_count)})
        return carry

    def greet_z(step, carry):
        greet({"exp": lax.rem(z + step, z_count)})
        return carry

    def greet_x(step, carry):
        greet({"dp": lax.rem(x + step, x_count)})

        def greet_xy(y_step, inner):
            greet(
                {
                    "dp": lax.rem(x + step, x_count),
                    "seq": 2 * lax.rem(y + y_step, y_count) + c,
                }
            )
            return inner

        return lax.fori_loop(1, y_count, greet_xy, carry)

    lax.fori_loop(1, s_count, greet_seq, 0)
    lax.fori_loop(1, z_count, greet_z, 0)
    lax.fori_loop(1, x_count, greet_x, 0)

    my_rows = pl.ds(pl.multiple_of(s * tok_rows, tok_rows), tok_rows)
    my_cols = pl.ds(pl.multiple_of(s * head_cols, head_cols), head_cols)
    kv_refs = (key_ref, value_ref)
    qs_refs = (query_ref, stream_ref)
    for which in range(2):
        pltpu.make_async_copy(
            kv_refs[which].at[:, my_cols], kv_in.at[which, my_rows, :], kv_sem
        ).start()
        pltpu.make_async_copy(
            qs_refs[which].at[:, my_cols], qs_in.at[s, which], qs_sem.at[which, s]
        ).start()
        pltpu.make_async_copy(
            down_ref.at[which, :, pl.ds(first_column(y), cols)],
            weights.at[c, z, y, pl.ds(which * LANES, LANES), :],
            near_w_sem,
        ).start()
    pltpu.make_async_copy(stream_ref, stream_own, own_sem).start()

    rank_part = rank // z_count
    twin = z - 2 * x

    @pl.when(z // 2 == x)
    def _own_gate_up():
        part = pl.ds(pl.multiple_of(z * rank_part, rank_part), rank_part)
        pltpu.make_async_copy(
            gate_up_ref.at[:, part, :], gate_up.at[c, z, twin], near_g_sem
        ).start()

    entries = 2 * tok_rows
    experts = 4 * z_count * y_count
    ids_row = jnp.concatenate([ids_ref[0:1, :], ids_ref[1:2, :]], axis=1)
    named = lax.broadcasted_iota(jnp.int32, (experts, entries), 0) == ids_row
    entry = [lax.broadcasted_iota(jnp.int32, (entries, entries), axis) for axis in (0, 1)]
    entry = [2 * (one % tok_rows) + one // tok_rows for one in entry]
    before = jnp.where(entry[0] < entry[1], 1.0, 0.0).astype(jnp.bfloat16)
    counts = jnp.dot(
        jnp.where(named, 1.0, 0.0).astype(jnp.bfloat16), before, preferred_element_type=jnp.float32
    )
    slot_ids = (
        jnp.sum(jnp.where(named, counts, 0.0), axis=0, keepdims=True)
        + ids_row.astype(jnp.float32) * CAP
    )
    info_row = lax.broadcasted_iota(jnp.int32, info_own.shape, 0)
    info = jnp.where(info_row == 2, route_ref[0:1, :], 0.0)
    info = jnp.where(info_row == 3, route_ref[1:2, :], info)
    info = jnp.where(info_row == 0, slot_ids[:, :tok_rows], info)
    info_own[...] = jnp.where(info_row == 1, slot_ids[:, tok_rows:], info)
    pltpu.make_async_copy(info_own, info_y.at[y], info_sem.at[0]).start()

    pl.semaphore_wait(barrier, s_count - 1 + z_count - 1 + (x_count - 1) * y_count)

    def info_to_y(step, carry):
        y_to = lax.rem(y + step, y_count)
        remote(
            info_own, info_y.at[y], sent.at[0], info_sem.at[0], {"seq": 2 * y_to + c}
        ).start()
        return carry

    lax.fori_loop(1, y_count, info_to_y, 0)

    def near_first(step, carry):
        y_to = lax.rem(y + near_order(step), y_count)
        device = {"seq": 2 * y_to + c}
        for which in range(2):
            remote(
                down_ref.at[which, :, pl.ds(first_column(y_to), cols)],
                weights.at[c, z, y, pl.ds(which * LANES, LANES), :],
                sent.at[1],
                near_w_sem,
                device,
            ).start()
        return carry

    lax.fori_loop(1, y_count, near_first, 0)

    @pl.when(z // 2 == x)
    def _spread_gate_up():
        def to_z(step, carry):
            z_to = lax.rem(z + step, z_count)
            part = pl.ds(pl.multiple_of(z_to * rank_part, rank_part), rank_part)
            remote(
                gate_up_ref.at[:, part, :],
                gate_up.at[c, z_to, twin],
                sent.at[4],
                near_g_sem,
                {"exp": z_to},
            ).start()
            return carry

        lax.fori_loop(1, z_count, to_z, 0)


    def send_batch(refs, slot_of, sem, send_sem, distances):
        for which in range(2):

            def one_copy(index, carry):
                s_to = 2 * lax.rem(y + distances[0] + 2 * (index % len(distances)), y_count) + (
                    index // len(distances)
                )
                columns = pl.ds(pl.multiple_of(s_to * head_cols, head_cols), head_cols)
                remote(
                    refs[which].at[:, columns], slot_of(which), send_sem, sem(which), {"seq": s_to}
                ).start()
                return carry

            if len(distances) == 2:
                columns = pl.ds(pl.multiple_of(pair * head_cols, head_cols), head_cols)
                remote(
                    refs[which].at[:, columns], slot_of(which), send_sem, sem(which), {"seq": pair}
                ).start()
            lax.fori_loop(0, 2 * len(distances), one_copy, 0)

    batches = ((1, 3), (2,))

    def send_kv(batch):
        send_batch(
            kv_refs,
            lambda which: kv_in.at[which, my_rows, :],
            lambda which: kv_sem,
            batch_sem.at[0, batch],
            batches[batch],
        )

    def send_qs(batch):
        send_batch(
            qs_refs,
            lambda which: qs_in.at[s, which],
            lambda which: qs_sem.at[which, s],
            batch_sem.at[1, batch],
            batches[batch],
        )

    def batch_left(kind, batch):
        peers = 5 if batch == 0 else 2
        wait_bytes(qs_in.at[pl.ds(0, peers)], batch_sem.at[kind, batch])

    send_kv(0)
    send_kv(1)

    always = z >= 0
    half = z_count // 2

    def pass_on(buffer, sems, left_sem, pair_left, pair_sem, block, up, down):
        held = buffer.at[c, block]

        def pass_to(z_to):
            remote(held, held, left_sem, sems.at[block], {"exp": lax.rem(z_to, z_count)}).start()

        if up is not None:

            @pl.when(up)
            def _up():
                pass_to(z + 1)

        if down is not None:

            @pl.when(down)
            def _down():
                pass_to(z + z_count - 1)

        remote(held, held, pair_left, pair_sem, {"seq": pair}).start()

    def ring_step(ring, step):
        buffer, sems = ring[0], ring[1]
        below = lax.rem(z + z_count - step, z_count)
        above = lax.rem(z + step, z_count)
        wait_bytes(buffer.at[c, below], sems.at[below])
        if step == half:
            pass_on(*ring, below, None, None)
            return
        pass_on(*ring, below, always if step < half - 1 else c == 0, None)
        wait_bytes(buffer.at[c, above], sems.at[above])
        pass_on(*ring, above, None, always if step < half - 1 else c == 1)

    gate_ring = (gate_up, ring_g_sem, sent.at[13], sent.at[14], pair_g_sem)
    down_ring = (weights, ring_sem, sent.at[7], sent.at[8], pair_w_sem)

    wait_bytes(weights.at[c, z], near_w_sem)
    pass_on(*down_ring, z, always, always)
    batch_left(0, 0)
    send_qs(0)
    wait_bytes(gate_up.at[c, z], near_g_sem)
    wait_bytes(info_y, info_sem.at[0])
    pltpu.make_async_copy(info_y, info_x.at[x], info_sem.at[1]).start()

    def info_to_x(step, carry):
        remote(
            info_y,
            info_x.at[x],
            sent.at[6],
            info_sem.at[1],
            {"dp": lax.rem(x + step, x_count)},
        ).start()
        return carry

    lax.fori_loop(1, x_count, info_to_x, 0)
    pass_on(*gate_ring, z, always, always)
    batch_left(0, 1)
    send_qs(1)

    wait_bytes(info_x, info_sem.at[1])
    group = x_count * y_count
    chip_rows = group * slots
    def make_pick(source, carry):
        slot_iota = lax.broadcasted_iota(jnp.int32, (picks.shape[2], tok_rows), 0).astype(
            jnp.float32
        )
        named_here = info_x[source // y_count, source % y_count]
        pick = (slot_iota == named_here[0:1, :]) | (slot_iota == named_here[1:2, :])
        picks[source] = jnp.where(pick, 1.0, 0.0).astype(jnp.bfloat16).T
        return carry

    wait_bytes(kv_in, kv_sem)

    length = s_count * tok_rows
    lane = lax.broadcasted_iota(jnp.int32, (length, HEAD_DIM), 1)
    ones_column = jnp.where(lane == 0, 1.0, 0.0).astype(jnp.bfloat16)
    exponent_scale = 1.0 / (math.sqrt(HEAD_DIM) * math.log(2.0))
    gate_row = attn_gate_ref[:, my_cols].astype(jnp.float32)
    scale_row = ffn_scale_ref[:, my_cols].astype(jnp.float32)
    two = 2 * tok_rows
    tail_lane = lax.broadcasted_iota(jnp.int32, (two, LANES), 1)

    def with_tail(values, square, tail):
        high = square.astype(jnp.bfloat16).astype(jnp.float32)
        extra = jnp.where(tail == 0, high, jnp.where(tail == 1, square - high, 0.0))
        return jnp.concatenate([values, extra], axis=1)

    def add_core_part(step):
        wait_bytes(core_recv.at[step], core_sem.at[step])
        total = own_part[step] + core_recv[step].astype(jnp.float32)
        square = total[:, rank : rank + 1] + total[:, rank + 1 : rank + 2]
        return total[:, :rank], square

    def send_part(step):
        values, square = add_core_part(step)
        part_send[step - 1] = with_tail(values, square, tail_lane[:tok_rows]).astype(jnp.bfloat16)
        distance = near_order(step)
        y_to = lax.rem(y + y_count - distance, y_count)
        remote(
            part_send.at[step - 1],
            part_recv.at[step - 1],
            sent.at[10],
            part_sem,
            {"seq": 2 * y_to + c},
        ).start()

    def one_chip(step, carry):
        y_from = lax.rem(y + y_count - near_order(step), y_count)

        @pl.when(step > 1)
        def _previous():
            send_part(step - 1)

        def wait_rows(which):
            for core in range(2):
                s_from = 2 * y_from + core
                wait_bytes(qs_in.at[s_from, which], qs_sem.at[which, s_from])

        wait_rows(0)
        both = pl.ds(2 * y_from, 2)
        square = jnp.zeros((two, 1), jnp.float32)
        for head in range(heads_here):
            part = slice(head * HEAD_DIM, (head + 1) * HEAD_DIM)
            scores = lax.dot_general(
                qs_in[both, 0, :, part].reshape(two, HEAD_DIM),
                kv_in[0, :, part],
                (((1,), (1,)), ((), ())),
                preferred_element_type=jnp.float32,
            )
            row_max = jnp.max(scores, axis=-1, keepdims=True)
            raised = jnp.exp2((scores - row_max) * exponent_scale).astype(jnp.bfloat16)
            value_ones = jnp.concatenate([kv_in[1, :, part], ones_column], axis=1)
            mixed = jnp.dot(raised, value_ones, preferred_element_type=jnp.float32)
            mixed = (mixed[:, :HEAD_DIM] / mixed[:, HEAD_DIM : HEAD_DIM + 1]).astype(jnp.bfloat16)
            att_out[both, :, part] = mixed.reshape(2, tok_rows, HEAD_DIM)

        wait_rows(1)
        for head in range(heads_here):
            part = slice(head * HEAD_DIM, (head + 1) * HEAD_DIM)
            mixed = att_out[both, :, part].reshape(two, HEAD_DIM)
            residual = qs_in[both, 1, :, part].reshape(two, HEAD_DIM).astype(
                jnp.float32
            ) + gate_row[:, part] * mixed.astype(jnp.float32)
            modulated[:, part] = (residual * scale_row[:, part]).astype(jnp.bfloat16)
            square = square + jnp.sum(residual * residual, axis=1, keepdims=True)
        product = jnp.dot(modulated[...], basis_ref[...], preferred_element_type=jnp.float32)
        partial[...] = with_tail(product, square, tail_lane).reshape(partial.shape)
        own_part[step] = partial[c]
        core_send[step] = partial[other_c].astype(jnp.bfloat16)
        remote(
            core_send.at[step], core_recv.at[step], sent.at[9], core_sem.at[step], {"seq": pair}
        ).start()
        return carry

    def after_chip(step, carry):
        one_chip(step, carry)

        @pl.when(step == 0)
        def _down_one():
            ring_step(down_ring, 1)

        @pl.when(step == 1)
        def _gate_one():
            ring_step(gate_ring, 1)

        @pl.when(step == 2)
        def _down_two():
            ring_step(down_ring, 2)

        return carry

    lax.fori_loop(0, y_count, after_chip, 0)
    send_part(y_count - 1)
    ring_step(gate_ring, 2)
    ring_step(down_ring, 3)

    def send_attended(index, carry):
        s_to = lax.rem(s + index, s_count)

        @pl.when(s_to == s)
        def _keep():
            pltpu.make_async_copy(att_out.at[s_to], attended.at[:, my_cols], att_sem).start()

        @pl.when(s_to != s)
        def _send():
            remote(
                att_out.at[s_to], attended.at[:, my_cols], sent.at[11], att_sem, {"seq": s_to}
            ).start()

        return carry

    values, square = add_core_part(0)
    wait_bytes(part_recv, part_sem)
    for step in range(y_count - 1):
        arrived = part_recv[step].astype(jnp.float32)
        values = values + arrived[:, :rank]
        square = square + arrived[:, rank : rank + 1] + arrived[:, rank + 1 : rank + 2]
    low_rank = (values / jnp.sqrt(square / model_width + epsilon)).astype(jnp.bfloat16)

    def pick_rows(y_to):
        row = lax.broadcasted_iota(jnp.int32, (z_count * slots, tok_rows), 0)
        slot_here = (((row // slots) * y_count + y_to) * slots + row % slots).astype(jnp.float32)
        pick = (slot_here == info_own[0:1, :]) | (slot_here == info_own[1:2, :])
        pick = jnp.where(pick, 1.0, 0.0).astype(jnp.bfloat16)
        return jnp.dot(pick, low_rank, preferred_element_type=jnp.float32).astype(jnp.bfloat16)

    chip_slots = 2 * slots

    def forward_rows(y_from):
        def to_x(x_step, inner):
            x_to = lax.rem(x + near_order(x_step), x_count)
            rows = pl.ds(pl.multiple_of(x_to * chip_slots, chip_slots), chip_slots)
            remote(
                near_rows.at[y_from, rows, :],
                slot_rows.at[x, y_from],
                sent.at[5],
                slot_sem,
                {"dp": x_to},
            ).start()
            return inner

        lax.fori_loop(1, x_count, to_x, 0)
        own = pl.ds(pl.multiple_of(x * chip_slots, chip_slots), chip_slots)
        pltpu.make_async_copy(near_rows.at[y_from, own, :], slot_rows.at[x, y_from], slot_sem).start()

    for step in range(1, y_count):
        y_to = lax.rem(y + near_order(step), y_count)
        out_rows[step - 1] = pick_rows(y_to)
        remote(
            out_rows.at[step - 1],
            near_rows.at[y],
            sent.at[12],
            near_sem.at[y],
            {"seq": 2 * y_to + c},
        ).start()


    near_rows[y] = pick_rows(y)
    forward_rows(y)
    ring_step(gate_ring, 3)

    def forward_near(step, carry):
        y_from = lax.rem(y + y_count - near_order(step), y_count)
        lax.fori_loop(4 * step - 4, 4 * step, make_pick, 0)
        wait_bytes(near_rows.at[y_from], near_sem.at[y_from])
        forward_rows(y_from)
        return lax.fori_loop(2 * step, 2 * step + 2, send_attended, carry)

    lax.fori_loop(0, 2, send_attended, 0)
    named_all = info_x[...].reshape(group, info_x.shape[2], tok_rows)
    place = lax.broadcasted_iota(jnp.int32, (group, slots, tok_rows), 1)
    for which in range(2):
        slot_here = (place + ((2 * x + which) * y_count + y) * slots).astype(jnp.float32)
        routed = jnp.where(
            slot_here == named_all[:, 0:1, :], named_all[:, 2:3, :], 0.0
        ) + jnp.where(slot_here == named_all[:, 1:2, :], named_all[:, 3:4, :], 0.0)
        slot_weight[which] = jnp.sum(routed, axis=2, keepdims=True).reshape(chip_rows, 1)

    lax.fori_loop(1, y_count, forward_near, 0)

    ring_step(gate_ring, half)
    wait_bytes(gate_up.at[other_c], pair_g_sem)
    wait_bytes(slot_rows, slot_sem)
    expert = lax.broadcasted_iota(jnp.int32, (chip_rows, 1), 0) % slots // CAP

    for twin_here in range(2):
        rows = slot_rows[:, :, pl.ds(twin_here * slots, slots), :].reshape(chip_rows, rank)
        both_halves = jnp.zeros((chip_rows, gate_up.shape[5]), jnp.float32)
        for which in range(4):
            product = jnp.dot(
                rows,
                gate_up[which // 2, :, twin_here, which % 2].reshape(rank, gate_up.shape[5]),
                preferred_element_type=jnp.float32,
            )
            both_halves = jnp.where(expert == which, product, both_halves)
        gate, up = both_halves[:, :LANES], both_halves[:, LANES:]
        hidden = gate / (1.0 + jnp.exp(-gate)) * up * slot_weight[twin_here]
        hidden_all[x, y, twin_here] = hidden.astype(jnp.bfloat16)
        held = hidden_all.at[x, y, twin_here]

        def hidden_near(step, carry):
            if twin_here == 0:
                device = {"dp": lax.rem(x + near_order(step), x_count)}
            else:
                device = {"seq": 2 * lax.rem(y + near_order(step), y_count) + c}
            remote(held, held, sent.at[15], hid_sem.at[twin_here], device).start()
            return carry

        lax.fori_loop(1, x_count, hidden_near, 0)

    lax.fori_loop(4 * (y_count - 1), group, make_pick, 0)
    wait_bytes(hidden_all.at[pl.ds(0, x_count - 1), y, 0], hid_sem.at[0])

    def hidden_to_y(step, carry):
        held = hidden_all.at[:, y, 0]
        y_to = lax.rem(y + near_order(step), y_count)
        remote(held, held, sent.at[16], hid_y_sem.at[y], {"seq": 2 * y_to + c}).start()
        return carry

    lax.fori_loop(1, y_count, hidden_to_y, 0)
    wait_bytes(hidden_all.at[x, pl.ds(0, y_count - 1), 1], hid_sem.at[1])

    def hidden_to_x(step, carry):
        held = hidden_all.at[x, :, 1]
        x_to = lax.rem(x + near_order(step), x_count)
        remote(held, held, sent.at[18], hid_x_sem.at[x], {"dp": x_to}).start()
        return carry

    lax.fori_loop(1, x_count, hidden_to_x, 0)
    ring_step(down_ring, half)
    wait_bytes(weights.at[other_c], pair_w_sem)

    chip_expert = lax.broadcasted_iota(jnp.int32, (chip_rows, LANES), 0) % slots // CAP

    masks = [
        jnp.where(chip_expert == which, 1.0, 0.0).astype(jnp.bfloat16) for which in range(4)
    ]

    def down_block(x_from, y_from, twin_here):
        held = hidden_all[x_from, y_from, twin_here]
        z_from = 2 * x_from + twin_here
        masked = [held * mask for mask in masks]
        product = jnp.dot(
            jnp.concatenate(masked[:2], axis=1),
            weights[0, z_from, y_from],
            preferred_element_type=jnp.float32,
        ) + jnp.dot(
            jnp.concatenate(masked[2:], axis=1),
            weights[1, z_from, y_from],
            preferred_element_type=jnp.float32,
        )
        to = pl.ds(pl.multiple_of((z_from * y_count + y_from) * slots, slots), slots)
        slot_out[:, to, :] = product.astype(jnp.bfloat16).reshape(group, slots, cols)

    def down_step(step, carry):
        y_from = lax.rem(y + y_count - near_order(step), y_count)
        x_from = lax.rem(x + x_count - near_order(step), x_count)

        @pl.when(step > 0)
        def _arrive_y():
            wait_bytes(hidden_all.at[:, y_from, 0], hid_y_sem.at[y_from])

        def down_first(other, inner):
            down_block(other, y_from, 0)
            return inner

        lax.fori_loop(0, x_count, down_first, 0)

        @pl.when(step > 0)
        def _arrive_x():
            wait_bytes(hidden_all.at[x_from, :, 1], hid_x_sem.at[x_from])

        def down_second(other, inner):
            down_block(x_from, other, 1)
            return inner

        lax.fori_loop(0, y_count, down_second, 0)
        return carry

    lax.fori_loop(0, y_count, down_step, 0)

    mine = x * y_count + y

    def mix_one(step, carry):
        x_to = lax.rem(x + (step + 1) // y_count, x_count)
        y_to = lax.rem(y + step + 1, y_count)
        to = x_to * y_count + y_to
        mixed = jnp.dot(picks[to], slot_out[to], preferred_element_type=jnp.float32)
        mix_out[to] = mixed.astype(jnp.bfloat16)

        def give(first, last):
            source = mix_out.at[to, :, first:last]
            target = mix_in.at[mine, :, first:last]

            @pl.when(to == mine)
            def _keep():
                pltpu.make_async_copy(source, target, mix_sem.at[mine]).start()

            @pl.when(to != mine)
            def _send():
                remote(
                    source,
                    target,
                    sent.at[17],
                    mix_sem.at[mine],
                    {"dp": x_to, "seq": 2 * y_to + c},
                ).start()

        @pl.when(y % 2 == c)
        def _whole():
            give(0, cols)

        @pl.when((y % 2 == 0) & (c == 1))
        def _low():
            give(0, cols - LANES)

        @pl.when((y % 2 == 1) & (c == 0))
        def _high():
            give(LANES, cols)

        return carry

    lax.fori_loop(0, group, mix_one, 0)

    wait_bytes(stream_own, own_sem)
    wait_bytes(attended, att_sem)

    def finish(core):
        for block in range(s_count):
            part = slice(block * head_cols, (block + 1) * head_cols)
            even, odd = 2 * block, 2 * block + 1
            if core == 0:
                wait_bytes(mix_in.at[even], mix_sem.at[even])
                wait_bytes(mix_in.at[odd, :, LANES:cols], mix_sem.at[odd])
                mixed = [mix_in[even], mix_in[odd, :, LANES:]]
            else:
                wait_bytes(mix_in.at[even, :, 0 : cols - LANES], mix_sem.at[even])
                wait_bytes(mix_in.at[odd], mix_sem.at[odd])
                mixed = [mix_in[even, :, : cols - LANES], mix_in[odd]]
            mixed = jnp.concatenate(mixed, axis=1)
            residual = stream_own[:, part].astype(jnp.float32) + attn_gate_ref[:, part].astype(
                jnp.float32
            ) * attended[:, part].astype(jnp.float32)
            output_ref[:, part] = (
                residual + ffn_gate_ref[:, part].astype(jnp.float32) * mixed.astype(jnp.float32)
            ).astype(jnp.bfloat16)

    for core in range(2):

        @pl.when(c == core)
        def _finish():
            finish(core)

    wait_bytes(info_y.at[pl.ds(0, y_count - 1)], sent.at[0])
    wait_bytes(weights.at[0, 0, pl.ds(0, y_count - 1)], sent.at[1])
    batch_left(1, 0)
    batch_left(1, 1)

    @pl.when(z // 2 == x)
    def _spread_done():
        wait_bytes(gate_up.at[0, pl.ds(0, z_count - 1), 0], sent.at[4])

    wait_bytes(slot_rows.at[pl.ds(0, x_count - 1)], sent.at[5])
    wait_bytes(info_x.at[pl.ds(0, x_count - 1)], sent.at[6])
    wait_bytes(weights.at[0, pl.ds(0, z_count - 1)], sent.at[7])
    wait_bytes(weights.at[0], sent.at[8])
    wait_bytes(core_send, sent.at[9])
    wait_bytes(part_send, sent.at[10])
    wait_bytes(att_out.at[pl.ds(0, s_count - 1)], sent.at[11])
    wait_bytes(out_rows, sent.at[12])
    wait_bytes(gate_up.at[0, pl.ds(0, z_count - 1)], sent.at[13])
    wait_bytes(gate_up.at[0], sent.at[14])
    wait_bytes(hidden_all.at[pl.ds(0, 2), pl.ds(0, y_count - 1), 0], sent.at[15])
    wait_bytes(hidden_all.at[:, pl.ds(0, y_count - 1), 0], sent.at[16])
    wait_bytes(hidden_all.at[pl.ds(0, x_count - 1), :, 1], sent.at[18])

    @pl.when(y % 2 == c)
    def _whole_done():
        wait_bytes(mix_out.at[pl.ds(0, group - 1)], sent.at[17])

    @pl.when(y % 2 != c)
    def _part_done():
        wait_bytes(mix_out.at[pl.ds(0, group - 1), :, 0 : cols - LANES], sent.at[17])


def on_device(
    query_rows,
    key_rows,
    value_rows,
    stream,
    shared_basis,
    expert_gate_up,
    expert_down,
    attn_gate,
    ffn_scale,
    ffn_gate,
    expert_ids,
    route_weights,
):
    x_count, z_count, s_count = (lax.axis_size(name) for name in ("dp", "exp", "seq"))
    y_count = s_count // 2
    tok_rows, model_width = stream.shape
    experts_here, hidden_cols, _ = expert_down.shape
    expert_total = z_count * s_count * experts_here
    rank = shared_basis.shape[1]
    head_cols = model_width // s_count
    cols = 384
    slots = 4 * CAP
    length = s_count * tok_rows
    group = x_count * y_count

    vmem = pl.BlockSpec(memory_space=pltpu.VMEM)
    anywhere = pl.BlockSpec(memory_space=pl.ANY)
    bf16, f32 = jnp.bfloat16, jnp.float32
    wide = rank + LANES
    dma = pltpu.SemaphoreType.DMA
    return pl.pallas_call(
        block_kernel,
        out_shape=jax.ShapeDtypeStruct((tok_rows, model_width), bf16),
        in_specs=[anywhere] * 6 + [vmem] * 6,
        out_specs=vmem,
        scratch_shapes=[
            pltpu.VMEM((2, length, head_cols), bf16),
            pltpu.VMEM((s_count, 2, tok_rows, head_cols), bf16),
            pltpu.VMEM((tok_rows, model_width), bf16),
            pltpu.VMEM((s_count, tok_rows, head_cols), bf16),
            pltpu.VMEM((tok_rows, model_width), bf16),
            pltpu.VMEM((2 * tok_rows, head_cols), bf16),
            pltpu.VMEM((2, tok_rows, wide), f32),
            pltpu.VMEM((y_count, tok_rows, wide), f32),
            pltpu.VMEM((y_count, tok_rows, wide), bf16),
            pltpu.VMEM((y_count, tok_rows, wide), bf16),
            pltpu.VMEM((y_count - 1, tok_rows, wide), bf16),
            pltpu.VMEM((y_count - 1, tok_rows, wide), bf16),
            pltpu.VMEM((y_count - 1, z_count * slots, rank), bf16),
            pltpu.VMEM((y_count, z_count * slots, rank), bf16),
            pltpu.VMEM((x_count, y_count, 2 * slots, rank), bf16),
            pltpu.VMEM(
                (2, z_count, 2, experts_here, rank // z_count, 2 * hidden_cols), bf16
            ),
            pltpu.VMEM((x_count, y_count, 2, group * slots, hidden_cols), bf16),
            pltpu.VMEM((2, z_count, y_count, experts_here * hidden_cols, cols), bf16),
            pltpu.VMEM((group, z_count * y_count * slots, cols), bf16),
            pltpu.VMEM((group, tok_rows, cols), bf16),
            pltpu.VMEM((group, tok_rows, cols), bf16),
            pltpu.VMEM((8, tok_rows), f32),
            pltpu.VMEM((y_count, 8, tok_rows), f32),
            pltpu.VMEM((x_count, y_count, 8, tok_rows), f32),
            pltpu.VMEM((2, group * slots, 1), f32),
            pltpu.VMEM((group, tok_rows, group * 2 * slots), bf16),
            dma,
            dma((2, s_count)),
            dma((2, 2)),
            dma,
            dma((2,)),
            dma,
            dma((z_count,)),
            dma,
            dma,
            dma((z_count,)),
            dma,
            dma((y_count,)),
            dma,
            dma,
            dma((y_count,)),
            dma,
            dma((2,)),
            dma((y_count,)),
            dma((x_count,)),
            dma((group,)),
            dma((19,)),
        ],
        compiler_params=pltpu.CompilerParams(
            collective_id=0, has_side_effects=True, vmem_limit_bytes=62 * 1024 * 1024
        ),
        name="block",
    )(
        query_rows,
        key_rows,
        value_rows,
        stream,
        expert_down,
        expert_gate_up,
        shared_basis,
        attn_gate,
        ffn_scale,
        ffn_gate,
        expert_ids.T,
        route_weights.T,
    )


def solution(mesh):
    in_specs = (
        P(("dp", "exp", "seq"), None),
        P(("dp", "exp", "seq"), None),
        P(("dp", "exp", "seq"), None),
        P(("dp", "exp", "seq"), None),
        P("seq", None),
        P(("exp", "seq"), None, None),
        P(("exp", "seq"), None, None),
        P(("dp", "exp"), None),
        P(("dp", "exp"), None),
        P(("dp", "exp"), None),
        P(("dp", "exp", "seq"), None),
        P(("dp", "exp", "seq"), None),
    )
    out_specs = P(("dp", "exp", "seq"), None)
    return jax.shard_map(
        on_device, mesh=mesh, in_specs=in_specs, out_specs=out_specs, check_vma=False
    )
```

```python
import functools
import math

import jax
import jax.numpy as jnp
from jax import lax
from jax.experimental import pallas as pl
from jax.experimental.pallas import tpu as pltpu
from jax.sharding import PartitionSpec as P

HEAD_DIM = 128
LANES = 128
MESH = pl.DeviceIdType.MESH
epsilon = 1e-06
CAP = 4


def block_kernel(
    query_ref,
    key_ref,
    value_ref,
    stream_ref,
    down_ref,
    gate_up_ref,
    basis_ref,
    attn_gate_ref,
    ffn_scale_ref,
    ffn_gate_ref,
    ids_ref,
    route_ref,
    output_ref,
    kv_in,
    qs_in,
    stream_own,
    att_out,
    attended,
    modulated,
    partial,
    own_part,
    core_send,
    core_recv,
    part_send,
    part_recv,
    out_rows,
    near_rows,
    slot_rows,
    gate_up,
    hidden_all,
    weights,
    slot_out,
    mix_out,
    mix_in,
    info_own,
    info_y,
    info_x,
    slot_weight,
    picks,
    kv_sem,
    qs_sem,
    batch_sem,
    own_sem,
    info_sem,
    near_w_sem,
    ring_sem,
    pair_w_sem,
    near_g_sem,
    ring_g_sem,
    pair_g_sem,
    core_sem,
    part_sem,
    att_sem,
    near_sem,
    slot_sem,
    hid_sem,
    hid_y_sem,
    hid_x_sem,
    mix_sem,
    sent,
):
    x_count, z_count, s_count = (lax.axis_size(name) for name in ("dp", "exp", "seq"))
    y_count = s_count // 2
    x, z, s = (lax.axis_index(name) for name in ("dp", "exp", "seq"))
    y, c = s // 2, s % 2
    other_c = 1 - c
    pair = 2 * y + other_c
    tok_rows, model_width = attended.shape
    head_cols = kv_in.shape[2]
    heads_here = head_cols // HEAD_DIM
    cols = weights.shape[4]
    rank = near_rows.shape[2]
    slots = 4 * CAP
    quarter = model_width // x_count

    def remote(src, dst, send_sem, recv_sem, device):
        return pltpu.make_async_remote_copy(
            src_ref=src,
            dst_ref=dst,
            send_sem=send_sem,
            recv_sem=recv_sem,
            device_id=device,
            device_id_type=MESH,
        )

    def wait_bytes(ref, sem):
        pltpu.make_async_copy(ref, ref, sem).wait()

    def first_column(y_to):
        return pl.multiple_of(x * quarter + (y_to // 2) * head_cols + (y_to % 2) * 256, LANES)

    def near_order(step):
        return step + step // 2 - 2 * (step // 3)

    barrier = pltpu.get_barrier_semaphore()

    def greet(device):
        pl.semaphore_signal(barrier, inc=1, device_id=device, device_id_type=MESH)

    def greet_seq(step, carry):
        greet({"seq": lax.rem(s + step, s_count)})
        return carry

    def greet_z(step, carry):
        greet({"exp": lax.rem(z + step, z_count)})
        return carry

    def greet_x(step, carry):
        greet({"dp": lax.rem(x + step, x_count)})

        def greet_xy(y_step, inner):
            greet(
                {
                    "dp": lax.rem(x + step, x_count),
                    "seq": 2 * lax.rem(y + y_step, y_count) + c,
                }
            )
            return inner

        return lax.fori_loop(1, y_count, greet_xy, carry)

    lax.fori_loop(1, s_count, greet_seq, 0)
    lax.fori_loop(1, z_count, greet_z, 0)
    lax.fori_loop(1, x_count, greet_x, 0)

    my_rows = pl.ds(pl.multiple_of(s * tok_rows, tok_rows), tok_rows)
    my_cols = pl.ds(pl.multiple_of(s * head_cols, head_cols), head_cols)
    kv_refs = (key_ref, value_ref)
    qs_refs = (query_ref, stream_ref)
    for which in range(2):
        pltpu.make_async_copy(
            kv_refs[which].at[:, my_cols], kv_in.at[which, my_rows, :], kv_sem
        ).start()
        pltpu.make_async_copy(
            qs_refs[which].at[:, my_cols], qs_in.at[s, which], qs_sem.at[which, s]
        ).start()
        pltpu.make_async_copy(
            down_ref.at[which, :, pl.ds(first_column(y), cols)],
            weights.at[c, z, y, pl.ds(which * LANES, LANES), :],
            near_w_sem,
        ).start()
    pltpu.make_async_copy(stream_ref, stream_own, own_sem).start()

    rank_part = rank // z_count
    twin = z - 2 * x

    @pl.when(z // 2 == x)
    def _own_gate_up():
        part = pl.ds(pl.multiple_of(z * rank_part, rank_part), rank_part)
        pltpu.make_async_copy(
            gate_up_ref.at[:, part, :], gate_up.at[c, z, twin], near_g_sem
        ).start()

    entries = 2 * tok_rows
    experts = 4 * z_count * y_count
    ids_row = jnp.concatenate([ids_ref[0:1, :], ids_ref[1:2, :]], axis=1)
    named = lax.broadcasted_iota(jnp.int32, (experts, entries), 0) == ids_row
    entry = [lax.broadcasted_iota(jnp.int32, (entries, entries), axis) for axis in (0, 1)]
    entry = [2 * (one % tok_rows) + one // tok_rows for one in entry]
    before = jnp.where(entry[0] < entry[1], 1.0, 0.0).astype(jnp.bfloat16)
    counts = jnp.dot(
        jnp.where(named, 1.0, 0.0).astype(jnp.bfloat16), before, preferred_element_type=jnp.float32
    )
    slot_ids = (
        jnp.sum(jnp.where(named, counts, 0.0), axis=0, keepdims=True)
        + ids_row.astype(jnp.float32) * CAP
    )
    info_row = lax.broadcasted_iota(jnp.int32, info_own.shape, 0)
    info = jnp.where(info_row == 2, route_ref[0:1, :], 0.0)
    info = jnp.where(info_row == 3, route_ref[1:2, :], info)
    info = jnp.where(info_row == 0, slot_ids[:, :tok_rows], info)
    info_own[...] = jnp.where(info_row == 1, slot_ids[:, tok_rows:], info)
    pltpu.make_async_copy(info_own, info_y.at[y], info_sem.at[0]).start()

    pl.semaphore_wait(barrier, s_count - 1 + z_count - 1 + (x_count - 1) * y_count)

    def info_to_y(step, carry):
        y_to = lax.rem(y + step, y_count)
        remote(
            info_own, info_y.at[y], sent.at[0], info_sem.at[0], {"seq": 2 * y_to + c}
        ).start()
        return carry

    lax.fori_loop(1, y_count, info_to_y, 0)

    def near_first(step, carry):
        y_to = lax.rem(y + near_order(step), y_count)
        device = {"seq": 2 * y_to + c}
        for which in range(2):
            remote(
                down_ref.at[which, :, pl.ds(first_column(y_to), cols)],
                weights.at[c, z, y, pl.ds(which * LANES, LANES), :],
                sent.at[1],
                near_w_sem,
                device,
            ).start()
        return carry

    lax.fori_loop(1, y_count, near_first, 0)

    @pl.when(z // 2 == x)
    def _spread_gate_up():
        def to_z(step, carry):
            z_to = lax.rem(z + step, z_count)
            part = pl.ds(pl.multiple_of(z_to * rank_part, rank_part), rank_part)
            remote(
                gate_up_ref.at[:, part, :],
                gate_up.at[c, z_to, twin],
                sent.at[4],
                near_g_sem,
                {"exp": z_to},
            ).start()
            return carry

        lax.fori_loop(1, z_count, to_z, 0)


    def send_batch(refs, slot_of, sem, send_sem, distances):
        for which in range(2):

            def one_copy(index, carry):
                s_to = 2 * lax.rem(y + distances[0] + 2 * (index % len(distances)), y_count) + (
                    index // len(distances)
                )
                columns = pl.ds(pl.multiple_of(s_to * head_cols, head_cols), head_cols)
                remote(
                    refs[which].at[:, columns], slot_of(which), send_sem, sem(which), {"seq": s_to}
                ).start()
                return carry

            if len(distances) == 2:
                columns = pl.ds(pl.multiple_of(pair * head_cols, head_cols), head_cols)
                remote(
                    refs[which].at[:, columns], slot_of(which), send_sem, sem(which), {"seq": pair}
                ).start()
            lax.fori_loop(0, 2 * len(distances), one_copy, 0)

    batches = ((1, 3), (2,))

    def send_kv(batch):
        send_batch(
            kv_refs,
            lambda which: kv_in.at[which, my_rows, :],
            lambda which: kv_sem,
            batch_sem.at[0, batch],
            batches[batch],
        )

    def send_qs(batch):
        send_batch(
            qs_refs,
            lambda which: qs_in.at[s, which],
            lambda which: qs_sem.at[which, s],
            batch_sem.at[1, batch],
            batches[batch],
        )

    def batch_left(kind, batch):
        peers = 5 if batch == 0 else 2
        wait_bytes(qs_in.at[pl.ds(0, peers)], batch_sem.at[kind, batch])

    send_kv(0)
    send_kv(1)

    always = z >= 0
    half = z_count // 2

    def pass_on(buffer, sems, left_sem, pair_left, pair_sem, block, up, down):
        held = buffer.at[c, block]

        def pass_to(z_to):
            remote(held, held, left_sem, sems.at[block], {"exp": lax.rem(z_to, z_count)}).start()

        if up is not None:

            @pl.when(up)
            def _up():
                pass_to(z + 1)

        if down is not None:

            @pl.when(down)
            def _down():
                pass_to(z + z_count - 1)

        remote(held, held, pair_left, pair_sem, {"seq": pair}).start()

    def ring_step(ring, step):
        buffer, sems = ring[0], ring[1]
        below = lax.rem(z + z_count - step, z_count)
        above = lax.rem(z + step, z_count)
        wait_bytes(buffer.at[c, below], sems.at[below])
        if step == half:
            pass_on(*ring, below, None, None)
            return
        pass_on(*ring, below, always if step < half - 1 else c == 0, None)
        wait_bytes(buffer.at[c, above], sems.at[above])
        pass_on(*ring, above, None, always if step < half - 1 else c == 1)

    gate_ring = (gate_up, ring_g_sem, sent.at[13], sent.at[14], pair_g_sem)
    down_ring = (weights, ring_sem, sent.at[7], sent.at[8], pair_w_sem)

    wait_bytes(weights.at[c, z], near_w_sem)
    pass_on(*down_ring, z, always, always)
    wait_bytes(gate_up.at[c, z], near_g_sem)
    wait_bytes(info_y, info_sem.at[0])
    pltpu.make_async_copy(info_y, info_x.at[x], info_sem.at[1]).start()

    def info_to_x(step, carry):
        remote(
            info_y,
            info_x.at[x],
            sent.at[6],
            info_sem.at[1],
            {"dp": lax.rem(x + step, x_count)},
        ).start()
        return carry

    lax.fori_loop(1, x_count, info_to_x, 0)
    pass_on(*gate_ring, z, always, always)
    batch_left(0, 0)
    send_qs(0)
    batch_left(0, 1)
    send_qs(1)

    wait_bytes(info_x, info_sem.at[1])
    group = x_count * y_count
    chip_rows = group * slots
    def make_pick(source, carry):
        slot_iota = lax.broadcasted_iota(jnp.int32, (picks.shape[2], tok_rows), 0).astype(
            jnp.float32
        )
        named_here = info_x[source // y_count, source % y_count]
        pick = (slot_iota == named_here[0:1, :]) | (slot_iota == named_here[1:2, :])
        picks[source] = jnp.where(pick, 1.0, 0.0).astype(jnp.bfloat16).T
        return carry

    wait_bytes(kv_in, kv_sem)

    length = s_count * tok_rows
    lane = lax.broadcasted_iota(jnp.int32, (length, HEAD_DIM), 1)
    ones_column = jnp.where(lane == 0, 1.0, 0.0).astype(jnp.bfloat16)
    exponent_scale = 1.0 / (math.sqrt(HEAD_DIM) * math.log(2.0))
    gate_row = attn_gate_ref[:, my_cols].astype(jnp.float32)
    scale_row = ffn_scale_ref[:, my_cols].astype(jnp.float32)
    two = 2 * tok_rows
    tail_lane = lax.broadcasted_iota(jnp.int32, (two, LANES), 1)

    def with_tail(values, square, tail):
        high = square.astype(jnp.bfloat16).astype(jnp.float32)
        extra = jnp.where(tail == 0, high, jnp.where(tail == 1, square - high, 0.0))
        return jnp.concatenate([values, extra], axis=1)

    def add_core_part(step):
        wait_bytes(core_recv.at[step], core_sem.at[step])
        total = own_part[step] + core_recv[step].astype(jnp.float32)
        square = total[:, rank : rank + 1] + total[:, rank + 1 : rank + 2]
        return total[:, :rank], square

    def send_part(step):
        values, square = add_core_part(step)
        part_send[step - 1] = with_tail(values, square, tail_lane[:tok_rows]).astype(jnp.bfloat16)
        distance = near_order(step)
        y_to = lax.rem(y + y_count - distance, y_count)
        remote(
            part_send.at[step - 1],
            part_recv.at[step - 1],
            sent.at[10],
            part_sem,
            {"seq": 2 * y_to + c},
        ).start()

    def one_chip(step, carry):
        y_from = lax.rem(y + y_count - near_order(step), y_count)

        @pl.when(step > 1)
        def _previous():
            send_part(step - 1)

        def wait_rows(which):
            for core in range(2):
                s_from = 2 * y_from + core
                wait_bytes(qs_in.at[s_from, which], qs_sem.at[which, s_from])

        wait_rows(0)
        both = pl.ds(2 * y_from, 2)
        square = jnp.zeros((two, 1), jnp.float32)
        for head in range(heads_here):
            part = slice(head * HEAD_DIM, (head + 1) * HEAD_DIM)
            scores = lax.dot_general(
                qs_in[both, 0, :, part].reshape(two, HEAD_DIM),
                kv_in[0, :, part],
                (((1,), (1,)), ((), ())),
                preferred_element_type=jnp.float32,
            )
            row_max = jnp.max(scores, axis=-1, keepdims=True)
            raised = jnp.exp2((scores - row_max) * exponent_scale).astype(jnp.bfloat16)
            value_ones = jnp.concatenate([kv_in[1, :, part], ones_column], axis=1)
            mixed = jnp.dot(raised, value_ones, preferred_element_type=jnp.float32)
            mixed = (mixed[:, :HEAD_DIM] / mixed[:, HEAD_DIM : HEAD_DIM + 1]).astype(jnp.bfloat16)
            att_out[both, :, part] = mixed.reshape(2, tok_rows, HEAD_DIM)

        wait_rows(1)
        for head in range(heads_here):
            part = slice(head * HEAD_DIM, (head + 1) * HEAD_DIM)
            mixed = att_out[both, :, part].reshape(two, HEAD_DIM)
            residual = qs_in[both, 1, :, part].reshape(two, HEAD_DIM).astype(
                jnp.float32
            ) + gate_row[:, part] * mixed.astype(jnp.float32)
            modulated[:, part] = (residual * scale_row[:, part]).astype(jnp.bfloat16)
            square = square + jnp.sum(residual * residual, axis=1, keepdims=True)
        product = jnp.dot(modulated[...], basis_ref[...], preferred_element_type=jnp.float32)
        partial[...] = with_tail(product, square, tail_lane).reshape(partial.shape)
        own_part[step] = partial[c]
        core_send[step] = partial[other_c].astype(jnp.bfloat16)
        remote(
            core_send.at[step], core_recv.at[step], sent.at[9], core_sem.at[step], {"seq": pair}
        ).start()
        return carry

    def after_chip(step, carry):
        one_chip(step, carry)

        @pl.when(step == 0)
        def _gate_one():
            ring_step(gate_ring, 1)

        @pl.when(step == 1)
        def _down_one():
            ring_step(down_ring, 1)

        @pl.when(step == 2)
        def _gate_two():
            ring_step(gate_ring, 2)

        return carry

    lax.fori_loop(0, y_count, after_chip, 0)
    send_part(y_count - 1)
    ring_step(gate_ring, 3)

    def send_attended(index, carry):
        s_to = lax.rem(s + index, s_count)

        @pl.when(s_to == s)
        def _keep():
            pltpu.make_async_copy(att_out.at[s_to], attended.at[:, my_cols], att_sem).start()

        @pl.when(s_to != s)
        def _send():
            remote(
                att_out.at[s_to], attended.at[:, my_cols], sent.at[11], att_sem, {"seq": s_to}
            ).start()

        return carry

    values, square = add_core_part(0)
    wait_bytes(part_recv, part_sem)
    for step in range(y_count - 1):
        arrived = part_recv[step].astype(jnp.float32)
        values = values + arrived[:, :rank]
        square = square + arrived[:, rank : rank + 1] + arrived[:, rank + 1 : rank + 2]
    low_rank = (values / jnp.sqrt(square / model_width + epsilon)).astype(jnp.bfloat16)

    def pick_rows(y_to):
        row = lax.broadcasted_iota(jnp.int32, (z_count * slots, tok_rows), 0)
        slot_here = (((row // slots) * y_count + y_to) * slots + row % slots).astype(jnp.float32)
        pick = (slot_here == info_own[0:1, :]) | (slot_here == info_own[1:2, :])
        pick = jnp.where(pick, 1.0, 0.0).astype(jnp.bfloat16)
        return jnp.dot(pick, low_rank, preferred_element_type=jnp.float32).astype(jnp.bfloat16)

    chip_slots = 2 * slots

    def forward_rows(y_from):
        def to_x(x_step, inner):
            x_to = lax.rem(x + near_order(x_step), x_count)
            rows = pl.ds(pl.multiple_of(x_to * chip_slots, chip_slots), chip_slots)
            remote(
                near_rows.at[y_from, rows, :],
                slot_rows.at[x, y_from],
                sent.at[5],
                slot_sem,
                {"dp": x_to},
            ).start()
            return inner

        lax.fori_loop(1, x_count, to_x, 0)
        own = pl.ds(pl.multiple_of(x * chip_slots, chip_slots), chip_slots)
        pltpu.make_async_copy(near_rows.at[y_from, own, :], slot_rows.at[x, y_from], slot_sem).start()

    for step in range(1, y_count):
        y_to = lax.rem(y + near_order(step), y_count)
        out_rows[step - 1] = pick_rows(y_to)
        remote(
            out_rows.at[step - 1],
            near_rows.at[y],
            sent.at[12],
            near_sem.at[y],
            {"seq": 2 * y_to + c},
        ).start()


    near_rows[y] = pick_rows(y)
    forward_rows(y)
    ring_step(down_ring, 2)
    ring_step(gate_ring, half)

    def forward_near(step, carry):
        y_from = lax.rem(y + y_count - near_order(step), y_count)
        lax.fori_loop(4 * step - 4, 4 * step, make_pick, 0)
        wait_bytes(near_rows.at[y_from], near_sem.at[y_from])
        forward_rows(y_from)
        return lax.fori_loop(2 * step, 2 * step + 2, send_attended, carry)

    lax.fori_loop(0, 2, send_attended, 0)
    named_all = info_x[...].reshape(group, info_x.shape[2], tok_rows)
    place = lax.broadcasted_iota(jnp.int32, (group, slots, tok_rows), 1)
    for which in range(2):
        slot_here = (place + ((2 * x + which) * y_count + y) * slots).astype(jnp.float32)
        routed = jnp.where(
            slot_here == named_all[:, 0:1, :], named_all[:, 2:3, :], 0.0
        ) + jnp.where(slot_here == named_all[:, 1:2, :], named_all[:, 3:4, :], 0.0)
        slot_weight[which] = jnp.sum(routed, axis=2, keepdims=True).reshape(chip_rows, 1)

    lax.fori_loop(1, y_count, forward_near, 0)

    wait_bytes(gate_up.at[other_c], pair_g_sem)
    wait_bytes(slot_rows, slot_sem)
    expert = lax.broadcasted_iota(jnp.int32, (chip_rows, 1), 0) % slots // CAP

    for twin_here in range(2):
        rows = slot_rows[:, :, pl.ds(twin_here * slots, slots), :].reshape(chip_rows, rank)
        both_halves = jnp.zeros((chip_rows, gate_up.shape[5]), jnp.float32)
        for which in range(4):
            product = jnp.dot(
                rows,
                gate_up[which // 2, :, twin_here, which % 2].reshape(rank, gate_up.shape[5]),
                preferred_element_type=jnp.float32,
            )
            both_halves = jnp.where(expert == which, product, both_halves)
        gate, up = both_halves[:, :LANES], both_halves[:, LANES:]
        hidden = gate / (1.0 + jnp.exp(-gate)) * up * slot_weight[twin_here]
        hidden_all[x, y, twin_here] = hidden.astype(jnp.bfloat16)
        held = hidden_all.at[x, y, twin_here]

        def hidden_near(step, carry):
            if twin_here == 0:
                device = {"dp": lax.rem(x + near_order(step), x_count)}
            else:
                device = {"seq": 2 * lax.rem(y + near_order(step), y_count) + c}
            remote(held, held, sent.at[15], hid_sem.at[twin_here], device).start()
            return carry

        lax.fori_loop(1, x_count, hidden_near, 0)

    ring_step(down_ring, 3)
    lax.fori_loop(4 * (y_count - 1), group, make_pick, 0)
    wait_bytes(hidden_all.at[pl.ds(0, x_count - 1), y, 0], hid_sem.at[0])

    def hidden_to_y(step, carry):
        held = hidden_all.at[:, y, 0]
        y_to = lax.rem(y + near_order(step), y_count)
        remote(held, held, sent.at[16], hid_y_sem.at[y], {"seq": 2 * y_to + c}).start()
        return carry

    lax.fori_loop(1, y_count, hidden_to_y, 0)
    wait_bytes(hidden_all.at[x, pl.ds(0, y_count - 1), 1], hid_sem.at[1])

    def hidden_to_x(step, carry):
        held = hidden_all.at[x, :, 1]
        x_to = lax.rem(x + near_order(step), x_count)
        remote(held, held, sent.at[18], hid_x_sem.at[x], {"dp": x_to}).start()
        return carry

    lax.fori_loop(1, x_count, hidden_to_x, 0)
    ring_step(down_ring, half)
    wait_bytes(weights.at[other_c], pair_w_sem)

    chip_expert = lax.broadcasted_iota(jnp.int32, (chip_rows, LANES), 0) % slots // CAP

    masks = [
        jnp.where(chip_expert == which, 1.0, 0.0).astype(jnp.bfloat16) for which in range(4)
    ]

    def down_block(x_from, y_from, twin_here):
        held = hidden_all[x_from, y_from, twin_here]
        z_from = 2 * x_from + twin_here
        masked = [held * mask for mask in masks]
        product = jnp.dot(
            jnp.concatenate(masked[:2], axis=1),
            weights[0, z_from, y_from],
            preferred_element_type=jnp.float32,
        ) + jnp.dot(
            jnp.concatenate(masked[2:], axis=1),
            weights[1, z_from, y_from],
            preferred_element_type=jnp.float32,
        )
        to = pl.ds(pl.multiple_of((z_from * y_count + y_from) * slots, slots), slots)
        slot_out[:, to, :] = product.astype(jnp.bfloat16).reshape(group, slots, cols)

    def down_step(step, carry):
        y_from = lax.rem(y + y_count - near_order(step), y_count)
        x_from = lax.rem(x + x_count - near_order(step), x_count)

        @pl.when(step > 0)
        def _arrive_y():
            wait_bytes(hidden_all.at[:, y_from, 0], hid_y_sem.at[y_from])

        def down_first(other, inner):
            down_block(other, y_from, 0)
            return inner

        lax.fori_loop(0, x_count, down_first, 0)

        @pl.when(step > 0)
        def _arrive_x():
            wait_bytes(hidden_all.at[x_from, :, 1], hid_x_sem.at[x_from])

        def down_second(other, inner):
            down_block(x_from, other, 1)
            return inner

        lax.fori_loop(0, y_count, down_second, 0)
        return carry

    lax.fori_loop(0, y_count, down_step, 0)

    mine = x * y_count + y

    def mix_one(step, carry):
        x_to = lax.rem(x + (step + 1) // y_count, x_count)
        y_to = lax.rem(y + step + 1, y_count)
        to = x_to * y_count + y_to
        mixed = jnp.dot(picks[to], slot_out[to], preferred_element_type=jnp.float32)
        mix_out[to] = mixed.astype(jnp.bfloat16)

        def give(first, last):
            source = mix_out.at[to, :, first:last]
            target = mix_in.at[mine, :, first:last]

            @pl.when(to == mine)
            def _keep():
                pltpu.make_async_copy(source, target, mix_sem.at[mine]).start()

            @pl.when(to != mine)
            def _send():
                remote(
                    source,
                    target,
                    sent.at[17],
                    mix_sem.at[mine],
                    {"dp": x_to, "seq": 2 * y_to + c},
                ).start()

        @pl.when(y % 2 == c)
        def _whole():
            give(0, cols)

        @pl.when((y % 2 == 0) & (c == 1))
        def _low():
            give(0, cols - LANES)

        @pl.when((y % 2 == 1) & (c == 0))
        def _high():
            give(LANES, cols)

        return carry

    lax.fori_loop(0, group, mix_one, 0)

    wait_bytes(stream_own, own_sem)
    wait_bytes(attended, att_sem)

    def finish(core):
        for block in range(s_count):
            part = slice(block * head_cols, (block + 1) * head_cols)
            even, odd = 2 * block, 2 * block + 1
            if core == 0:
                wait_bytes(mix_in.at[even], mix_sem.at[even])
                wait_bytes(mix_in.at[odd, :, LANES:cols], mix_sem.at[odd])
                mixed = [mix_in[even], mix_in[odd, :, LANES:]]
            else:
                wait_bytes(mix_in.at[even, :, 0 : cols - LANES], mix_sem.at[even])
                wait_bytes(mix_in.at[odd], mix_sem.at[odd])
                mixed = [mix_in[even, :, : cols - LANES], mix_in[odd]]
            mixed = jnp.concatenate(mixed, axis=1)
            residual = stream_own[:, part].astype(jnp.float32) + attn_gate_ref[:, part].astype(
                jnp.float32
            ) * attended[:, part].astype(jnp.float32)
            output_ref[:, part] = (
                residual + ffn_gate_ref[:, part].astype(jnp.float32) * mixed.astype(jnp.float32)
            ).astype(jnp.bfloat16)

    for core in range(2):

        @pl.when(c == core)
        def _finish():
            finish(core)

    wait_bytes(info_y.at[pl.ds(0, y_count - 1)], sent.at[0])
    wait_bytes(weights.at[0, 0, pl.ds(0, y_count - 1)], sent.at[1])
    batch_left(1, 0)
    batch_left(1, 1)

    @pl.when(z // 2 == x)
    def _spread_done():
        wait_bytes(gate_up.at[0, pl.ds(0, z_count - 1), 0], sent.at[4])

    wait_bytes(slot_rows.at[pl.ds(0, x_count - 1)], sent.at[5])
    wait_bytes(info_x.at[pl.ds(0, x_count - 1)], sent.at[6])
    wait_bytes(weights.at[0, pl.ds(0, z_count - 1)], sent.at[7])
    wait_bytes(weights.at[0], sent.at[8])
    wait_bytes(core_send, sent.at[9])
    wait_bytes(part_send, sent.at[10])
    wait_bytes(att_out.at[pl.ds(0, s_count - 1)], sent.at[11])
    wait_bytes(out_rows, sent.at[12])
    wait_bytes(gate_up.at[0, pl.ds(0, z_count - 1)], sent.at[13])
    wait_bytes(gate_up.at[0], sent.at[14])
    wait_bytes(hidden_all.at[pl.ds(0, 2), pl.ds(0, y_count - 1), 0], sent.at[15])
    wait_bytes(hidden_all.at[:, pl.ds(0, y_count - 1), 0], sent.at[16])
    wait_bytes(hidden_all.at[pl.ds(0, x_count - 1), :, 1], sent.at[18])

    @pl.when(y % 2 == c)
    def _whole_done():
        wait_bytes(mix_out.at[pl.ds(0, group - 1)], sent.at[17])

    @pl.when(y % 2 != c)
    def _part_done():
        wait_bytes(mix_out.at[pl.ds(0, group - 1), :, 0 : cols - LANES], sent.at[17])


def on_device(
    query_rows,
    key_rows,
    value_rows,
    stream,
    shared_basis,
    expert_gate_up,
    expert_down,
    attn_gate,
    ffn_scale,
    ffn_gate,
    expert_ids,
    route_weights,
):
    x_count, z_count, s_count = (lax.axis_size(name) for name in ("dp", "exp", "seq"))
    y_count = s_count // 2
    tok_rows, model_width = stream.shape
    experts_here, hidden_cols, _ = expert_down.shape
    expert_total = z_count * s_count * experts_here
    rank = shared_basis.shape[1]
    head_cols = model_width // s_count
    cols = 384
    slots = 4 * CAP
    length = s_count * tok_rows
    group = x_count * y_count

    vmem = pl.BlockSpec(memory_space=pltpu.VMEM)
    anywhere = pl.BlockSpec(memory_space=pl.ANY)
    bf16, f32 = jnp.bfloat16, jnp.float32
    wide = rank + LANES
    dma = pltpu.SemaphoreType.DMA
    return pl.pallas_call(
        block_kernel,
        out_shape=jax.ShapeDtypeStruct((tok_rows, model_width), bf16),
        in_specs=[anywhere] * 6 + [vmem] * 6,
        out_specs=vmem,
        scratch_shapes=[
            pltpu.VMEM((2, length, head_cols), bf16),
            pltpu.VMEM((s_count, 2, tok_rows, head_cols), bf16),
            pltpu.VMEM((tok_rows, model_width), bf16),
            pltpu.VMEM((s_count, tok_rows, head_cols), bf16),
            pltpu.VMEM((tok_rows, model_width), bf16),
            pltpu.VMEM((2 * tok_rows, head_cols), bf16),
            pltpu.VMEM((2, tok_rows, wide), f32),
            pltpu.VMEM((y_count, tok_rows, wide), f32),
            pltpu.VMEM((y_count, tok_rows, wide), bf16),
            pltpu.VMEM((y_count, tok_rows, wide), bf16),
            pltpu.VMEM((y_count - 1, tok_rows, wide), bf16),
            pltpu.VMEM((y_count - 1, tok_rows, wide), bf16),
            pltpu.VMEM((y_count - 1, z_count * slots, rank), bf16),
            pltpu.VMEM((y_count, z_count * slots, rank), bf16),
            pltpu.VMEM((x_count, y_count, 2 * slots, rank), bf16),
            pltpu.VMEM(
                (2, z_count, 2, experts_here, rank // z_count, 2 * hidden_cols), bf16
            ),
            pltpu.VMEM((x_count, y_count, 2, group * slots, hidden_cols), bf16),
            pltpu.VMEM((2, z_count, y_count, experts_here * hidden_cols, cols), bf16),
            pltpu.VMEM((group, z_count * y_count * slots, cols), bf16),
            pltpu.VMEM((group, tok_rows, cols), bf16),
            pltpu.VMEM((group, tok_rows, cols), bf16),
            pltpu.VMEM((8, tok_rows), f32),
            pltpu.VMEM((y_count, 8, tok_rows), f32),
            pltpu.VMEM((x_count, y_count, 8, tok_rows), f32),
            pltpu.VMEM((2, group * slots, 1), f32),
            pltpu.VMEM((group, tok_rows, group * 2 * slots), bf16),
            dma,
            dma((2, s_count)),
            dma((2, 2)),
            dma,
            dma((2,)),
            dma,
            dma((z_count,)),
            dma,
            dma,
            dma((z_count,)),
            dma,
            dma((y_count,)),
            dma,
            dma,
            dma((y_count,)),
            dma,
            dma((2,)),
            dma((y_count,)),
            dma((x_count,)),
            dma((group,)),
            dma((19,)),
        ],
        compiler_params=pltpu.CompilerParams(
            collective_id=0, has_side_effects=True, vmem_limit_bytes=62 * 1024 * 1024
        ),
        name="block",
    )(
        query_rows,
        key_rows,
        value_rows,
        stream,
        expert_down,
        expert_gate_up,
        shared_basis,
        attn_gate,
        ffn_scale,
        ffn_gate,
        expert_ids.T,
        route_weights.T,
    )


def solution(mesh):
    in_specs = (
        P(("dp", "exp", "seq"), None),
        P(("dp", "exp", "seq"), None),
        P(("dp", "exp", "seq"), None),
        P(("dp", "exp", "seq"), None),
        P("seq", None),
        P(("exp", "seq"), None, None),
        P(("exp", "seq"), None, None),
        P(("dp", "exp"), None),
        P(("dp", "exp"), None),
        P(("dp", "exp"), None),
        P(("dp", "exp", "seq"), None),
        P(("dp", "exp", "seq"), None),
    )
    out_specs = P(("dp", "exp", "seq"), None)
    return jax.shard_map(
        on_device, mesh=mesh, in_specs=in_specs, out_specs=out_specs, check_vma=False
    )
```
